32 devices in a mesh: dp: 8 (over z, y), tensor: 4 (over x, core).
Axes of the slice: x: 2, y: 2, z: 4, core: 2. Of those that a mesh axis runs over, the one named last changes fastest.
Arguments:
- frames: bfloat16 [4, 8, 512, 1024], P(None, 'dp', 'tensor'), may hold values from -6 to 6
- skip_frames: bfloat16 [4, 8, 512, 1024], P(None, 'dp', 'tensor'), may hold values from -6 to 6
- time_embed: bfloat16 [4, 8, 1024], P(None, 'dp'), may hold values from -6 to 6
- lengths: int32 [4, 8], P(None, 'dp'), may hold values from 128 to 512, as said below
- out_grad: bfloat16 [4, 8, 512, 1024], P(None, 'dp', 'tensor'), may hold values from -6 to 6
- skip_weight: float32 [2048, 1024], P(('dp', 'tensor')), may hold values from -0.125 to 0.125
- adapt_weight: float32 [1024, 4096], P(None, ('dp', 'tensor')), may hold values from -0.1875 to 0.1875
- input_weight: float32 [1024, 3, 1024], P('dp', None, 'tensor'), may hold values from -0.1875 to 0.1875
- output_weight: float32 [1024, 1024], P('tensor', 'dp'), may hold values from -2 to 2
- up_weight: float32 [1024, 4096], P('dp', 'tensor'), may hold values from -0.1875 to 0.1875
- down_weight: float32 [4096, 1024], P('tensor', 'dp'), may hold values from -0.09375 to 0.09375
- skip_first: float32 [2048, 1024], P(('dp', 'tensor')), may hold values from -80 to 80
- adapt_first: float32 [1024, 4096], P(None, ('dp', 'tensor')), may hold values from -40 to 40
- input_first: float32 [1024, 3, 1024], P('dp', None, 'tensor'), may hold values from -80 to 80
- output_first: float32 [1024, 1024], P('tensor', 'dp'), may hold values from -8 to 8
- up_first: float32 [1024, 4096], P('dp', 'tensor'), may hold values from -32 to 32
- down_first: float32 [4096, 1024], P('tensor', 'dp'), may hold values from -64 to 64
- skip_second: float32 [2048, 1024], P(('dp', 'tensor')), may hold values from 16.384 to 65.536
- adapt_second: float32 [1024, 4096], P(None, ('dp', 'tensor')), may hold values from 4.096 to 16.384
- input_second: float32 [1024, 3, 1024], P('dp', None, 'tensor'), may hold values from 16.384 to 65.536
- output_second: float32 [1024, 1024], P('tensor', 'dp'), may hold values from 0.128 to 0.512
- up_second: float32 [1024, 4096], P('dp', 'tensor'), may hold values from 2.62144 to 10.48576
- down_second: float32 [4096, 1024], P('tensor', 'dp'), may hold values from 8.192 to 32.768
Outputs:
- block_out: bfloat16 [4, 8, 512, 1024], P(None, 'dp', 'tensor')
- frames_grad: float32 [4, 8, 512, 1024], P(None, 'dp', 'tensor')
- skips_grad: float32 [4, 8, 512, 1024], P(None, 'dp', 'tensor')
- time_grad: float32 [4, 8, 1024], P(None, 'dp')
- skip_mean: float32 [2048, 1024], P(('dp', 'tensor'))
- skip_square: float32 [2048, 1024], P(('dp', 'tensor'))
- skip_master: float32 [2048, 1024], P(('dp', 'tensor'))
- skip_copy: bfloat16 [2048, 1024], P(('dp', 'tensor'))
- adapt_mean: float32 [1024, 4096], P(None, ('dp', 'tensor'))
- adapt_square: float32 [1024, 4096], P(None, ('dp', 'tensor'))
- adapt_master: float32 [1024, 4096], P(None, ('dp', 'tensor'))
- adapt_copy: bfloat16 [1024, 4096], P(None, ('dp', 'tensor'))
- input_mean: float32 [1024, 3, 1024], P('dp', None, 'tensor')
- input_square: float32 [1024, 3, 1024], P('dp', None, 'tensor')
- input_master: float32 [1024, 3, 1024], P('dp', None, 'tensor')
- input_copy: bfloat16 [1024, 3, 1024], P('dp', None, 'tensor')
- output_mean: float32 [1024, 1024], P('tensor', 'dp')
- output_square: float32 [1024, 1024], P('tensor', 'dp')
- output_master: float32 [1024, 1024], P('tensor', 'dp')
- output_copy: bfloat16 [1024, 1024], P('tensor', 'dp')
- up_mean: float32 [1024, 4096], P('dp', 'tensor')
- up_square: float32 [1024, 4096], P('dp', 'tensor')
- up_master: float32 [1024, 4096], P('dp', 'tensor')
- up_copy: bfloat16 [1024, 4096], P('dp', 'tensor')
- down_mean: float32 [4096, 1024], P('tensor', 'dp')
- down_square: float32 [4096, 1024], P('tensor', 'dp')
- down_master: float32 [4096, 1024], P('tensor', 'dp')
- down_copy: bfloat16 [4096, 1024], P('tensor', 'dp')
The draws below stay inside these ranges and needn't reach their ends.
Inputs may be any that keep to these rules, and one draw needn't show every extreme that they name: `lengths`: in every column some micro-batch's utterance has exactly 512 frames; frames at positions from an utterance's length on are padding.
All inputs are finite; a program needn't handle non-finite values.
Results may differ from the reference program's by a relative error of at most 0.02.
The reference program's roundings to bfloat16 on the way count: a program that leaves them out, or rounds other values in their place, can miss the bound.
Values may be sent and summed in bfloat16 or wider, within the bound.
No kernel may reach another device: no remote copies, remote signals or barrier semaphores. Data moves between devices by JAX's collectives and lax.ppermute only.
A program may use at most 192 MiB of HBM per device.

```python
import jax
import jax.numpy as jnp
from jax import lax

D = 1024
HEADS = 16
HEAD_DIM = 64
FF = 4096
LEN = 512
MB = 4
STEP = 10
BATCH = 8
N_TENSOR = 4


def draw_lengths(key, part):
    key = jax.random.fold_in(key, 7)
    first_key, second_key = jax.random.split(key)
    base = jax.random.randint(first_key, (MB, BATCH), LEN // 4, LEN + 1)
    chosen = jax.random.randint(second_key, (BATCH,), 0, MB)
    full = jnp.arange(MB, dtype=jnp.int32)[:, None] == chosen[None, :]
    return jnp.where(full, LEN, base).astype(jnp.int32)


def shard_levels(stream_key, shape, cuts, low, top_value):
    loudness, own = 1.0, jax.random.fold_in(stream_key, 6)
    for axis_at, shards_of in cuts:
        steps = jnp.exp(jax.random.uniform(jax.random.fold_in(own, axis_at), (shards_of,), jnp.float32, low / len(cuts), top_value / len(cuts)))
        loudness = loudness * jnp.repeat(steps, shape[axis_at] // shards_of).reshape([-1 if axis == axis_at else 1 for axis in range(len(shape))])
    return loudness


def gaussian(key, extent, width, bound, pieces=(), held_as=jnp.bfloat16):
    values = width * jax.random.normal(key, extent, jnp.float32)
    if pieces:
        values = values * shard_levels(key, extent, pieces, -0.22, 0.18)
    return jnp.clip(values, -bound, bound).astype(held_as)


def setup_inputs(seed: int = 0) -> dict:
    seeds = jax.random.split(jax.random.key(seed), 24)
    return {
        "frames": gaussian(seeds[0], (MB, BATCH, LEN, D), 1.0, 6.0, ((1, 8), (2, 4))),
        "skip_frames": gaussian(seeds[1], (MB, BATCH, LEN, D), 1.0, 6.0, ((1, 8), (2, 4))),
        "time_embed": gaussian(seeds[2], (MB, BATCH, D), 1.0, 6.0, ((1, 8),)),
        "lengths": draw_lengths(jax.random.fold_in(seeds[23], 71), 0),
        "out_grad": gaussian(seeds[4], (MB, BATCH, LEN, D), 1.0, 6.0, ((1, 8), (2, 4))),
        "skip_weight": gaussian(seeds[5], (2 * D, D), (2 * D) ** -0.5, 0.125, ((0, 32),), jnp.float32),
        "adapt_weight": gaussian(seeds[6], (D, 4 * D), D ** -0.5, 0.1875, ((1, 32),), jnp.float32),
        "input_weight": gaussian(seeds[7], (D, 3, D), D ** -0.5, 0.1875, ((0, 8), (2, 4)), jnp.float32),
        "output_weight": gaussian(seeds[8], (D, D), (max(1, 4 * D // LEN)) ** -0.5, 2.0, ((0, 4), (1, 8)), jnp.float32),
        "up_weight": gaussian(seeds[9], (D, FF), D ** -0.5, 0.1875, ((0, 8), (1, 4)), jnp.float32),
        "down_weight": gaussian(seeds[10], (FF, D), FF ** -0.5, 0.09375, ((0, 4), (1, 8)), jnp.float32),
        "skip_first": gaussian(seeds[11], (2 * D, D), (0.11 * (MB * BATCH * LEN) ** 0.5), 80.0, ((0, 32),), jnp.float32),
        "adapt_first": gaussian(seeds[12], (D, 4 * D), (0.055 * (MB * BATCH * LEN) ** 0.5), 40.0, ((1, 32),), jnp.float32),
        "input_first": gaussian(seeds[13], (D, 3, D), (0.11 * (MB * BATCH * LEN) ** 0.5), 80.0, ((0, 8), (2, 4)), jnp.float32),
        "output_first": gaussian(seeds[14], (D, D), (0.22 * (MB * BATCH) ** 0.5), 8.0, ((0, 4), (1, 8)), jnp.float32),
        "up_first": gaussian(seeds[15], (D, FF), (0.044 * (MB * BATCH * LEN) ** 0.5), 32.0, ((0, 8), (1, 4)), jnp.float32),
        "down_first": gaussian(seeds[16], (FF, D), (0.077 * (MB * BATCH * LEN) ** 0.5), 64.0, ((0, 4), (1, 8)), jnp.float32),
        "skip_second": jnp.clip(16.384 + 49.152 * jax.random.uniform(seeds[17], (2 * D, D), jnp.float32) ** shard_levels(seeds[17], (2 * D, D), ((0, 32),), -0.2, 0.2), 16.384, 65.536),
        "adapt_second": jnp.clip(4.096 + 12.288 * jax.random.uniform(seeds[18], (D, 4 * D), jnp.float32) ** shard_levels(seeds[18], (D, 4 * D), ((1, 32),), -0.2, 0.2), 4.096, 16.384),
        "input_second": jnp.clip(16.384 + 49.152 * jax.random.uniform(seeds[19], (D, 3, D), jnp.float32) ** shard_levels(seeds[19], (D, 3, D), ((0, 8), (2, 4)), -0.2, 0.2), 16.384, 65.536),
        "output_second": jnp.clip(0.128 + 0.384 * jax.random.uniform(seeds[20], (D, D), jnp.float32) ** shard_levels(seeds[20], (D, D), ((0, 4), (1, 8)), -0.2, 0.2), 0.128, 0.512),
        "up_second": jnp.clip(2.62144 + 7.86432 * jax.random.uniform(seeds[21], (D, FF), jnp.float32) ** shard_levels(seeds[21], (D, FF), ((0, 8), (1, 4)), -0.2, 0.2), 2.62144, 10.48576),
        "down_second": jnp.clip(8.192 + 24.576 * jax.random.uniform(seeds[22], (FF, D), jnp.float32) ** shard_levels(seeds[22], (FF, D), ((0, 4), (1, 8)), -0.2, 0.2), 8.192, 32.768),
    }


@jax.custom_vjp
def low(v):
    return lax.optimization_barrier(v.astype(jnp.bfloat16)).astype(jnp.float32)

@jax.custom_vjp
def low_back(v):
    return v

def low_keep(v):
    return (low(v), None)

def low_pass(kept, grad):
    return (grad,)

def back_keep(v):
    return (v, None)

def back_low(kept, grad):
    return (low(grad),)
low.defvjp(low_keep, low_pass)
low_back.defvjp(back_keep, back_low)
norm_eps = 1e-06
neg_large = -1e+30
rates = (0.04, 0.06, 0.06, 0.6, 0.06, 0.03)
beta_first = 0.9
beta_second = 0.999
decay_rate = 0.01
adam_eps = 1e-08

def matmul(left, right):
    return jnp.dot(left, right, precision=lax.Precision.HIGHEST)

def layer_norm(values):
    center = values - lax.optimization_barrier(jnp.mean(values, axis=-1, keepdims=True))
    spread = lax.optimization_barrier(jnp.mean(center * center, axis=-1, keepdims=True))
    return center * lax.rsqrt(spread + norm_eps)

def modulate(values, shift, scale):
    return layer_norm(values) * (1.0 + scale) + shift

def rotate(values, positions):
    half = values.shape[-1] // 2
    frequency = 10000.0 ** (-jnp.arange(half).astype(jnp.float32) / half)
    angles = positions[:, None] * frequency[None, :]
    cosine = jnp.cos(angles)[:, None, :]
    sine = jnp.sin(angles)[:, None, :]
    first = values[..., :half]
    second = values[..., half:]
    return jnp.concatenate([first * cosine - second * sine, second * cosine + first * sine], axis=-1)

def activate(values):
    return jax.nn.gelu(values, approximate=True)

def attention(normed, input_matrix, output_matrix, key_ok, positions):
    heads = HEADS // N_TENSOR
    inner = heads * HEAD_DIM
    scale = HEAD_DIM ** (-0.5)
    total = jnp.zeros((normed.shape[0], D), jnp.float32)
    for group in range(N_TENSOR):
        part = low_back(normed)
        columns = input_matrix[:, :, group * inner:(group + 1) * inner]
        project = low_back(jnp.einsum('nd,dce->nce', part, columns, precision=lax.Precision.HIGHEST))
        queries = low(rotate(project[:, 0].reshape(-1, heads, HEAD_DIM), positions))
        keys = low(rotate(project[:, 1].reshape(-1, heads, HEAD_DIM), positions))
        values = low(project[:, 2].reshape(-1, heads, HEAD_DIM))
        scores = low_back(jnp.einsum('qhd,khd->hqk', queries, keys, precision=lax.Precision.HIGHEST) * scale)
        scores = jnp.where(key_ok[None, None, :], scores, neg_large)
        shares = low(jax.nn.softmax(scores, axis=-1))
        mixed = low_back(low(jnp.einsum('hqk,khd->qhd', shares, values, precision=lax.Precision.HIGHEST)))
        total = total + low(matmul(mixed.reshape(-1, inner), output_matrix[group * inner:(group + 1) * inner]))
    return low_back(total)

def feed(normed, up_matrix, down_matrix):
    inner = FF // N_TENSOR
    total = jnp.zeros((normed.shape[0], D), jnp.float32)
    for group in range(N_TENSOR):
        part = low_back(normed)
        lifted = low_back(matmul(part, up_matrix[:, group * inner:(group + 1) * inner]))
        gated = low(activate(lifted))
        total = total + low(matmul(gated, down_matrix[group * inner:(group + 1) * inner]))
    return low_back(total)

def block(weights, frame_rows, skip_rows, time_row, length):
    skip_matrix, adapt_matrix, input_matrix, output_matrix, up_matrix, down_matrix = weights
    index = jnp.arange(LEN, dtype=jnp.int32)
    positions = index.astype(jnp.float32)
    key_ok = index < length
    keep_row = key_ok.astype(jnp.float32)[:, None]
    joined = jnp.concatenate([frame_rows, skip_rows], axis=1)
    hidden = low_back(matmul(joined, skip_matrix))
    activity = low(jax.nn.silu(time_row))
    adaptation = matmul(activity[None, :], adapt_matrix)[0]
    shift_one, scale_one, shift_two, scale_two = jnp.split(adaptation, 4)
    normed_one = low(modulate(hidden, shift_one, scale_one))
    middle = hidden + attention(normed_one, input_matrix, output_matrix, key_ok, positions)
    normed_two = low(modulate(middle, shift_two, scale_two))
    return keep_row * (middle + feed(normed_two, up_matrix, down_matrix))

def adam_update(master, first, second, grad, rate):
    first_new = beta_first * first + (1.0 - beta_first) * grad
    second_new = beta_second * second + (1.0 - beta_second) * grad * grad
    first_hat = first_new / (1.0 - beta_first ** STEP)
    second_hat = second_new / (1.0 - beta_second ** STEP)
    master_new = master - rate * (first_hat / (jnp.sqrt(second_hat) + adam_eps) + decay_rate * master)
    return (first_new, second_new, master_new, master_new.astype(jnp.bfloat16))

def reference(frames, skip_frames, time_embed, lengths, out_grad, skip_weight, adapt_weight, input_weight, output_weight, up_weight, down_weight, skip_first, adapt_first, input_first, output_first, up_first, down_first, skip_second, adapt_second, input_second, output_second, up_second, down_second):
    masters = (skip_weight, adapt_weight, input_weight, output_weight, up_weight, down_weight)
    firsts = (skip_first, adapt_first, input_first, output_first, up_first, down_first)
    seconds = (skip_second, adapt_second, input_second, output_second, up_second, down_second)
    rounded = tuple((master.astype(jnp.bfloat16).astype(jnp.float32) for master in masters))
    count = MB * BATCH
    flat_frames = frames.reshape(count, LEN, D).astype(jnp.float32)
    flat_skips = skip_frames.reshape(count, LEN, D).astype(jnp.float32)
    flat_time = time_embed.reshape(count, D).astype(jnp.float32)
    flat_lengths = lengths.reshape(count).astype(jnp.int32)
    flat_grads = out_grad.reshape(count, LEN, D).astype(jnp.float32)

    def visit(totals, item):
        frame_rows, skip_rows, time_row, length, grad_rows = item

        def apply_block(weights, frame_in, skip_in, time_in):
            return block(weights, frame_in, skip_in, time_in, length)
        result, pullback = jax.vjp(apply_block, rounded, frame_rows, skip_rows, time_row)
        weight_grads, frame_grad, skip_grad, time_grad = pullback(grad_rows)
        totals = jax.tree.map(jnp.add, totals, weight_grads)
        return (totals, (result.astype(jnp.bfloat16), frame_grad, skip_grad, time_grad))
    zeros = tuple((jnp.zeros(master.shape, jnp.float32) for master in masters))
    totals, (outputs, frame_grads, skip_grads, time_grads) = lax.scan(visit, zeros, (flat_frames, flat_skips, flat_time, flat_lengths, flat_grads))
    updated = [adam_update(masters[number], firsts[number], seconds[number], totals[number], rates[number]) for number in range(6)]
    return (outputs.reshape(MB, BATCH, LEN, D), frame_grads.reshape(MB, BATCH, LEN, D), skip_grads.reshape(MB, BATCH, LEN, D), time_grads.reshape(MB, BATCH, D), updated[0][0], updated[0][1], updated[0][2], updated[0][3], updated[1][0], updated[1][1], updated[1][2], updated[1][3], updated[2][0], updated[2][1], updated[2][2], updated[2][3], updated[3][0], updated[3][1], updated[3][2], updated[3][3], updated[4][0], updated[4][1], updated[4][2], updated[4][3], updated[5][0], updated[5][1], updated[5][2], updated[5][3])
```

```python
import math

import jax
import jax.numpy as jnp
from jax import lax
from jax.sharding import PartitionSpec as P

HEAD_DIM = 64
STEP = 10

norm_eps = 1e-06
neg_large = -1e30
rates = (0.04, 0.06, 0.06, 0.6, 0.06, 0.03)
beta_first = 0.9
beta_second = 0.999
decay_rate = 0.01
adam_eps = 1e-08
low = jnp.bfloat16
f32 = jnp.float32


def bits_of(axis):
    count = lax.axis_size(axis).bit_length() - 1
    return [1 << place for place in reversed(range(count))]


def my_bit(axis, mask):
    return (lax.axis_index(axis) // mask) % 2


def swap(values, axis, mask):
    count = lax.axis_size(axis)
    return lax.ppermute(values, axis, [(i, i ^ mask) for i in range(count)])


def pick(values, index, dim):
    return lax.dynamic_index_in_dim(values, index, dim, keepdims=False)


def joined_pair(mine, other, bit, dim):
    first = jnp.where(bit == 1, other, mine)
    second = jnp.where(bit == 1, mine, other)
    return jnp.concatenate([first, second], axis=dim)


def gather_rows(shard, order):
    dp_bits, tensor_bits = bits_of("dp"), bits_of("tensor")
    pieces = {0: shard.reshape((1,) * len(dp_bits) + shard.shape)}
    for axis, mask in order:
        arrived = {key: swap(piece, axis, mask) for key, piece in pieces.items()}
        if axis == "tensor":
            pieces.update({key | mask: piece for key, piece in arrived.items()})
        else:
            bit = my_bit(axis, mask)
            pieces = {
                key: joined_pair(piece, arrived[key], bit, dp_bits.index(mask))
                for key, piece in pieces.items()
            }
    return [
        pieces[key].reshape(-1, shard.shape[1]) for key in range(1 << len(tensor_bits))
    ]


def gather_all(shard, order):
    dp_bits, tensor_bits = bits_of("dp"), bits_of("tensor")
    dims = [("dp", mask) for mask in dp_bits] + [("tensor", mask) for mask in tensor_bits]
    piece = shard.reshape((1,) * len(dims) + shard.shape)
    for axis, mask in order:
        arrived = swap(piece, axis, mask)
        piece = joined_pair(piece, arrived, my_bit(axis, mask), dims.index((axis, mask)))
    return piece.reshape(-1, shard.shape[1])


def scatter_rows(pieces, order):
    dp_bits = bits_of("dp")
    columns = pieces[0].shape[1]
    pieces = {
        key: piece.reshape((2,) * len(dp_bits) + (-1, columns)) for key, piece in enumerate(pieces)
    }
    for axis, mask in order:
        if axis == "tensor":
            arrived = {
                key ^ mask: swap(piece, axis, mask) for key, piece in pieces.items() if key & mask
            }
            kept = {key: piece for key, piece in pieces.items() if not key & mask}
        else:
            bit, dim = my_bit(axis, mask), dp_bits.index(mask)
            arrived = {
                key: swap(
                    lax.dynamic_slice_in_dim(piece, 1 - bit, 1, dim), axis, mask
                )
                for key, piece in pieces.items()
            }
            kept = {
                key: lax.dynamic_slice_in_dim(piece, bit, 1, dim) for key, piece in pieces.items()
            }
        pieces = {
            key: (piece.astype(f32) + arrived[key].astype(f32)).astype(piece.dtype)
            for key, piece in kept.items()
        }
    return pieces[0].reshape(-1, columns)


def scatter_all(total, order):
    dims = [("dp", mask) for mask in bits_of("dp")]
    dims += [("tensor", mask) for mask in bits_of("tensor")]
    columns = total.shape[1]
    piece = total.reshape((2,) * len(dims) + (-1, columns))
    for axis, mask in order:
        bit, dim = my_bit(axis, mask), dims.index((axis, mask))
        arrived = swap(lax.dynamic_slice_in_dim(piece, 1 - bit, 1, dim), axis, mask)
        kept = lax.dynamic_slice_in_dim(piece, bit, 1, dim)
        piece = (kept.astype(f32) + arrived.astype(f32)).astype(piece.dtype)
    return piece.reshape(-1, columns)


def to_owner(take):
    me = lax.axis_index("tensor")
    count = lax.axis_size("tensor")
    return [
        take(me) if step == 0 else swap(take(me ^ step), "tensor", step) for step in range(count)
    ]


def from_owner(blocks):
    me = lax.axis_index("tensor")
    arrived = [
        block if step == 0 else swap(block, "tensor", step) for step, block in enumerate(blocks)
    ]
    return unflip(jnp.stack(arrived), 0, "tensor")


def unflip(values, dim, axis):
    masks = bits_of(axis)
    shape = values.shape
    values = values.reshape(shape[:dim] + (2,) * len(masks) + shape[dim + 1 :])
    for place, mask in enumerate(masks):
        values = jnp.where(
            my_bit(axis, mask) == 1, jnp.flip(values, dim + place), values
        )
    return values.reshape(shape)


def exchange_all(values):
    shape = values.shape
    dims = [("dp", mask) for mask in bits_of("dp")]
    dims += [("tensor", mask) for mask in bits_of("tensor")]
    values = values.reshape((2,) * len(dims) + shape[2:])
    for dim, (axis, mask) in enumerate(dims):
        kept = lax.slice_in_dim(values, 0, 1, axis=dim)
        arrived = swap(lax.slice_in_dim(values, 1, 2, axis=dim), axis, mask)
        values = jnp.concatenate([kept, arrived], axis=dim)
    return values.reshape(shape)


def mean_last(values):
    return jnp.mean(values, axis=-1, keepdims=True)


def normalise(values):
    center = values - mean_last(values)
    inverse = lax.rsqrt(mean_last(center * center) + norm_eps)
    return center * inverse, inverse


def norm_back(normal, inverse, grad, scale):
    scaled = grad * (1.0 + scale)
    return inverse * (scaled - mean_last(scaled) - normal * mean_last(scaled * normal))


def turn(values, cosine, sine):
    half = HEAD_DIM // 2
    first, second = values[..., :half], values[..., half:]
    return jnp.concatenate([first * cosine - second * sine, second * cosine + first * sine], axis=-1)


def contract_last(left, right):
    return lax.dot_general(
        left, right, (((1,), (1,)), ((), ())), preferred_element_type=f32
    )


def contract_first(left, right):
    return lax.dot_general(
        left, right, (((0,), (0,)), ((), ())), preferred_element_type=f32
    )


def dot(left, right):
    return jnp.dot(left, right, preferred_element_type=f32)


def rounded_sum(terms):
    total = None
    for term in terms:
        term = term.astype(low).astype(f32)
        total = term if total is None else total + term
    return total


def scores_of(queries, keys, key_ok):
    scores = jnp.einsum("qhd,khd->hqk", queries, keys, preferred_element_type=f32)
    return jnp.where(key_ok[None, None, :], scores * HEAD_DIM**-0.5, neg_large)


def attend(queries, keys, values, key_ok):
    scores = scores_of(queries, keys, key_ok)
    top = jnp.max(scores, axis=-1, keepdims=True)
    weights = jnp.exp(scores - top)
    total = jnp.sum(weights, axis=-1, keepdims=True)
    shares = (weights / total).astype(low)
    mixed = jnp.einsum("hqk,khd->qhd", shares, values, preferred_element_type=f32)
    return mixed.astype(low), top + jnp.log(total)


def attend_back(queries, keys, values, key_ok, logsum, mixed_grad):
    scale = HEAD_DIM**-0.5
    shares = jnp.exp(scores_of(queries, keys, key_ok) - logsum)
    share_grad = jnp.einsum("qhd,khd->hqk", mixed_grad, values, preferred_element_type=f32)
    inner = jnp.sum(share_grad * shares, axis=-1, keepdims=True)
    score_grad = (shares * (share_grad - inner)).astype(low)
    query_grad = jnp.einsum("hqk,khd->qhd", score_grad, keys, preferred_element_type=f32)
    key_grad = jnp.einsum("hqk,qhd->khd", score_grad, queries, preferred_element_type=f32)
    value_grad = jnp.einsum(
        "hqk,qhd->khd", shares.astype(low), mixed_grad, preferred_element_type=f32
    )
    return query_grad * scale, key_grad * scale, value_grad


def gelu_pair(values):
    root = math.sqrt(2.0 / math.pi)
    cube = 0.044715 * values * values
    slope = jnp.tanh(root * values * (1.0 + cube))
    gate = 0.5 * (1.0 + slope)
    back = gate + 0.5 * values * (1.0 - slope * slope) * root * (1.0 + 3.0 * cube)
    return values * gate, back


def adam_update(master, first, second, grad, rate):
    first_new = beta_first * first + (1.0 - beta_first) * grad
    second_new = beta_second * second + (1.0 - beta_second) * grad * grad
    first_hat = first_new / (1.0 - beta_first**STEP)
    second_hat = second_new / (1.0 - beta_second**STEP)
    master_new = master - rate * (
        first_hat / (jnp.sqrt(second_hat) + adam_eps) + decay_rate * master
    )
    return (first_new, second_new, master_new, master_new.astype(low))


def orders():
    dp_bits, tensor_bits = bits_of("dp"), bits_of("tensor")
    far = [("dp", mask) for mask in dp_bits[:-2]]
    near = [("dp", mask) for mask in dp_bits[-2:]]
    across, core = ("tensor", tensor_bits[0]), ("tensor", tensor_bits[1])
    return (
        far + [across, near[0], near[1], core],
        far + [near[1], near[0], across, core],
    )


def body(
    frames,
    skip_frames,
    time_embed,
    lengths,
    out_grad,
    skip_weight,
    adapt_weight,
    input_weight,
    output_weight,
    up_weight,
    down_weight,
    skip_first,
    adapt_first,
    input_first,
    output_first,
    up_first,
    down_first,
    skip_second,
    adapt_second,
    input_second,
    output_second,
    up_second,
    down_second,
):
    micro, _, rows, width = frames.shape
    parts = lax.axis_size("tensor")
    groups = lax.axis_size("dp")
    length_all = rows * parts
    me = lax.axis_index("tensor")
    inner = input_weight.shape[2]
    heads = inner // HEAD_DIM
    highest = lax.Precision.HIGHEST
    order_p, order_q = orders()

    frame_blocks = to_owner(lambda index: pick(frames, index, 0)[0])
    skip_blocks = to_owner(lambda index: pick(skip_frames, index, 0)[0])
    joined = jnp.concatenate(
        [jnp.concatenate(frame_blocks, axis=0), jnp.concatenate(skip_blocks, axis=0)], axis=1
    )
    skip_all = gather_all(skip_weight.astype(low), order_p)

    adapt_low = adapt_weight.astype(low)
    time_values = time_embed[:, 0, :].astype(f32)
    time_low = jax.nn.silu(time_values).astype(low)
    time_all = unflip(time_low, 0, "tensor")[None]
    for mask in reversed(bits_of("dp")):
        time_all = jnp.concatenate([time_all, swap(time_all, "dp", mask)], axis=0)
    time_rows = time_all.reshape(groups * micro, width)
    adapt_mine = dot(time_rows, adapt_low).reshape(groups, micro, -1)
    adapt_vector = unflip(unflip(exchange_all(adapt_mine), 0, "dp"), 1, "tensor").reshape(-1)
    shift_one, scale_one, shift_two, scale_two = jnp.split(adapt_vector, 4)

    attention_shard = jnp.concatenate(
        [input_weight.reshape(-1, 3 * inner), output_weight.T], axis=1
    ).astype(low)
    attention_all = gather_rows(attention_shard, order_p)
    up_all = gather_rows(up_weight.astype(low), order_q)
    down_all = gather_rows(down_weight.T.astype(low), order_q)
    outer_blocks = to_owner(lambda index: pick(out_grad, index, 0)[0])

    row_index = jnp.concatenate(
        [(me ^ step) * rows + jnp.arange(rows, dtype=jnp.int32) for step in range(parts)]
    )
    length = pick(lengths, me, 0)[0]
    key_ok = row_index < length
    keep = key_ok.astype(f32)[:, None]
    half = HEAD_DIM // 2
    frequency = 10000.0 ** (-jnp.arange(half).astype(f32) / half)
    angles = row_index.astype(f32)[:, None] * frequency[None, :]
    cosine, sine = jnp.cos(angles)[:, None, :], jnp.sin(angles)[:, None, :]

    hidden = dot(joined, skip_all)
    normal_one, inverse_one = normalise(hidden)
    normed_one = (normal_one * (1.0 + scale_one) + shift_one).astype(low)
    shaped = (length_all, heads, HEAD_DIM)
    parted = []
    for weight in attention_all:
        project = dot(normed_one, weight[:, : 3 * inner])
        queries = turn(project[:, :inner].reshape(shaped), cosine, sine).astype(low)
        keys = turn(project[:, inner : 2 * inner].reshape(shaped), cosine, sine).astype(low)
        values = project[:, 2 * inner :].reshape(shaped).astype(low)
        mixed, logsum = attend(queries, keys, values, key_ok)
        parted.append((queries, keys, values, mixed.reshape(length_all, inner), logsum))
    attended = rounded_sum(
        contract_last(part[3], weight[:, 3 * inner :])
        for part, weight in zip(parted, attention_all)
    )
    middle = hidden + attended
    normal_two, inverse_two = normalise(middle)
    normed_two = (normal_two * (1.0 + scale_two) + shift_two).astype(low)
    outer_grad = keep * jnp.concatenate(outer_blocks, axis=0).astype(f32)
    outer_low = outer_grad.astype(low)
    gated, lifted_grad, up_grad, down_grad = [], [], [], []
    for up_part, down_part in zip(up_all, down_all):
        value, slope = gelu_pair(dot(normed_two, up_part))
        gated.append(value.astype(low))
        down_grad.append(contract_first(outer_low, gated[-1]).astype(low))
        lifted_grad.append((dot(outer_low, down_part) * slope).astype(low))
    down_sum = scatter_rows(down_grad, order_p[::-1]).T.astype(f32)
    for back in lifted_grad:
        up_grad.append(contract_first(normed_two, back).astype(low))
    up_sum = scatter_rows(up_grad, order_q[::-1]).astype(f32)
    normed_two_grad = rounded_sum(
        contract_last(back, up_part) for back, up_part in zip(lifted_grad, up_all)
    )
    fed = rounded_sum(contract_last(value, part) for value, part in zip(gated, down_all))
    result = (keep * (middle + fed)).astype(low)
    results = from_owner([result[step * rows : (step + 1) * rows] for step in range(parts)])

    middle_grad = outer_grad + norm_back(normal_two, inverse_two, normed_two_grad, scale_two)
    middle_low = middle_grad.astype(low)
    attention_grad, normed_one_terms = [], []
    for (queries, keys, values, mixed, logsum), weight in zip(parted, attention_all):
        mixed_grad = dot(middle_low, weight[:, 3 * inner :]).astype(low).reshape(shaped)
        query_grad, key_grad, value_grad = attend_back(
            queries, keys, values, key_ok, logsum, mixed_grad
        )
        project_grad = jnp.concatenate(
            [
                turn(query_grad, cosine, -sine).reshape(length_all, inner),
                turn(key_grad, cosine, -sine).reshape(length_all, inner),
                value_grad.reshape(length_all, inner),
            ],
            axis=1,
        ).astype(low)
        attention_grad.append(
            jnp.concatenate(
                [contract_first(normed_one, project_grad), contract_first(middle_low, mixed)],
                axis=1,
            ).astype(low)
        )
        normed_one_terms.append(contract_last(project_grad, weight[:, : 3 * inner]))
    attention_sum = scatter_rows(attention_grad, order_p[::-1]).astype(f32)
    input_sum = attention_sum[:, : 3 * inner].reshape(input_weight.shape)
    output_sum = attention_sum[:, 3 * inner :].T
    normed_one_grad = rounded_sum(normed_one_terms)
    hidden_grad = middle_grad + norm_back(normal_one, inverse_one, normed_one_grad, scale_one)
    hidden_low = hidden_grad.astype(low)
    skip_sum = scatter_all(contract_first(joined, hidden_low).astype(low), order_q[::-1]).astype(f32)
    hidden_back = from_owner([hidden_low[step * rows : (step + 1) * rows] for step in range(parts)])
    joined_grad = contract_last(hidden_back.reshape(micro * rows, width), skip_all)
    frame_grads = joined_grad[:, :width].reshape(frames.shape)
    skip_grads = joined_grad[:, width:].reshape(frames.shape)

    adapt_back = jnp.concatenate(
        [
            jnp.sum(normed_one_grad, axis=0),
            jnp.sum(normed_one_grad * normal_one, axis=0),
            jnp.sum(normed_two_grad, axis=0),
            jnp.sum(normed_two_grad * normal_two, axis=0),
        ]
    ).reshape(groups, parts, -1)
    adapt_rows = exchange_all(unflip(unflip(adapt_back, 0, "dp"), 1, "tensor"))
    adapt_rows = adapt_rows.reshape(groups * micro, -1)
    adapt_sum = lax.dot_general(
        time_rows.astype(f32), adapt_rows, (((0,), (0,)), ((), ())), precision=highest
    )
    time_part = lax.dot_general(
        adapt_rows, adapt_low.astype(f32), (((1,), (1,)), ((), ())), precision=highest
    ).reshape(groups, micro, width)
    for mask in bits_of("dp"):
        time_part = time_part[:mask] + swap(time_part[mask:], "dp", mask)
    time_part = unflip(time_part[0], 0, "tensor")
    for mask in bits_of("tensor"):
        time_part = time_part + swap(time_part, "tensor", mask)
    sigmoid = jax.nn.sigmoid(time_values)
    time_grad = time_part * (sigmoid * (1.0 + time_values * (1.0 - sigmoid)))

    skip_new = adam_update(skip_weight, skip_first, skip_second, skip_sum, rates[0])
    adapt_new = adam_update(adapt_weight, adapt_first, adapt_second, adapt_sum, rates[1])
    input_new = adam_update(input_weight, input_first, input_second, input_sum, rates[2])
    output_new = adam_update(output_weight, output_first, output_second, output_sum, rates[3])
    up_new = adam_update(up_weight, up_first, up_second, up_sum, rates[4])
    down_new = adam_update(down_weight, down_first, down_second, down_sum, rates[5])
    return (
        results[:, None],
        frame_grads,
        skip_grads,
        time_grad[:, None, :],
        *skip_new,
        *adapt_new,
        *input_new,
        *output_new,
        *up_new,
        *down_new,
    )


def solution(mesh):
    return jax.shard_map(
        body,
        mesh=mesh,
        in_specs=(
            P(None, "dp", "tensor", None),
            P(None, "dp", "tensor", None),
            P(None, "dp", None),
            P(None, "dp"),
            P(None, "dp", "tensor", None),
            P(("dp", "tensor"), None),
            P(None, ("dp", "tensor")),
            P("dp", None, "tensor"),
            P("tensor", "dp"),
            P("dp", "tensor"),
            P("tensor", "dp"),
            P(("dp", "tensor"), None),
            P(None, ("dp", "tensor")),
            P("dp", None, "tensor"),
            P("tensor", "dp"),
            P("dp", "tensor"),
            P("tensor", "dp"),
            P(("dp", "tensor"), None),
            P(None, ("dp", "tensor")),
            P("dp", None, "tensor"),
            P("tensor", "dp"),
            P("dp", "tensor"),
            P("tensor", "dp"),
        ),
        out_specs=(
            P(None, "dp", "tensor", None),
            P(None, "dp", "tensor", None),
            P(None, "dp", "tensor", None),
            P(None, "dp", None),
            P(("dp", "tensor"), None),
            P(("dp", "tensor"), None),
            P(("dp", "tensor"), None),
            P(("dp", "tensor"), None),
            P(None, ("dp", "tensor")),
            P(None, ("dp", "tensor")),
            P(None, ("dp", "tensor")),
            P(None, ("dp", "tensor")),
            P("dp", None, "tensor"),
            P("dp", None, "tensor"),
            P("dp", None, "tensor"),
            P("dp", None, "tensor"),
            P("tensor", "dp"),
            P("tensor", "dp"),
            P("tensor", "dp"),
            P("tensor", "dp"),
            P("dp", "tensor"),
            P("dp", "tensor"),
            P("dp", "tensor"),
            P("dp", "tensor"),
            P("tensor", "dp"),
            P("tensor", "dp"),
            P("tensor", "dp"),
            P("tensor", "dp"),
        ),
        check_vma=False,
    )
```

```python
import functools
import math

import jax
import jax.numpy as jnp
from jax import lax
from jax.experimental import pallas as pl
from jax.experimental.pallas import tpu as pltpu
from jax.sharding import PartitionSpec as P

HEAD_DIM = 64
STEP = 10
LIMIT = 56 * 1024 * 1024

norm_eps = 1e-06
neg_large = -1e30
rates = (0.04, 0.06, 0.06, 0.6, 0.06, 0.03)
beta_first = 0.9
beta_second = 0.999
decay_rate = 0.01
adam_eps = 1e-08
low = jnp.bfloat16
f32 = jnp.float32


def bits_of(axis):
    count = lax.axis_size(axis).bit_length() - 1
    return [1 << place for place in reversed(range(count))]


def my_bit(axis, mask):
    return (lax.axis_index(axis) // mask) % 2


def swap(values, axis, mask):
    count = lax.axis_size(axis)
    return lax.ppermute(values, axis, [(i, i ^ mask) for i in range(count)])


def pick(values, index, dim):
    return lax.dynamic_index_in_dim(values, index, dim, keepdims=False)


def struct(shape, dtype):
    return jax.ShapeDtypeStruct(shape, dtype)


def whole(array):
    shape = array.shape
    return pl.BlockSpec(shape, lambda *_: (0,) * len(shape))


def each(array):
    shape = array.shape[1:]
    return pl.BlockSpec((None,) + shape, lambda i, *_: (i,) + (0,) * len(shape))


class Line:
    def __init__(self):
        self.last = ()

    def run(self, kernel, outs, ins, *, grid=(1,), in_specs=None, out_specs=None, scratch=(), flops=0, prefetch=()):
        in_specs = [whole(value) for value in ins] if in_specs is None else in_specs
        out_specs = [whole(value) for value in outs] if out_specs is None else out_specs
        deps = self.last
        skip = len(prefetch) + len(ins)

        def inner(*refs):
            kernel(*refs[:skip], *refs[skip + len(deps) :])

        moved = sum(value.size * value.dtype.itemsize for value in (*ins, *outs))
        results = pl.pallas_call(
            inner,
            grid_spec=pltpu.PrefetchScalarGridSpec(
                num_scalar_prefetch=len(prefetch),
                grid=grid,
                in_specs=in_specs + [pl.BlockSpec(memory_space=pl.ANY)] * len(deps),
                out_specs=out_specs,
                scratch_shapes=list(scratch),
            ),
            out_shape=list(outs),
            cost_estimate=pl.CostEstimate(flops=flops, bytes_accessed=moved, transcendentals=0),
            compiler_params=pltpu.CompilerParams(vmem_limit_bytes=LIMIT),
        )(*prefetch, *ins, *deps)
        self.last = (results[-1],)
        return results

    def need(self, *values):
        self.last += values

    def tie(self, values):
        return lax.optimization_barrier((values, self.last))[0]


def merge(line, pairs, bits):
    count = len(pairs)

    def kernel(bits, *refs):
        for place in range(count):
            (mine, other), out = refs[2 * place : 2 * place + 2], refs[2 * count + place]
            out[:, pl.ds(bits[place], 1)] = mine[...][:, None]
            out[:, pl.ds(1 - bits[place], 1)] = other[...][:, None]

    outs = [struct((mine.shape[0], 2) + mine.shape[1:], low) for mine, _ in pairs]
    return line.run(kernel, outs, [value for pair in pairs for value in pair], prefetch=[bits])


def split(line, pairs, bits):
    count = len(pairs)

    def kernel(bits, *refs):
        for place in range(count):
            terms, outs = refs[2 * place : 2 * place + 2], refs[2 * (count + place) : 2 * (count + place) + 2]
            for index, out in zip((1 - bits[place], bits[place]), outs):
                total = sum(term[:, pl.ds(index, 1)].astype(f32) for term in terms)
                out[...] = total[:, 0].astype(low)

    outs = [struct(pair[0].shape[:1] + pair[0].shape[2:], low) for pair in pairs for _ in range(2)]
    results = line.run(kernel, outs, [value for pair in pairs for value in pair], prefetch=[bits])
    return list(zip(results[::2], results[1::2]))


def bit_array(axis, mask):
    return my_bit(axis, mask).astype(jnp.int32)[None]


def bit_of(step, relative):
    return jnp.zeros((1,), jnp.int32) if step in relative else bit_array(*step)


class Gather:
    def __init__(self, line, shard, order, dims, relative):
        self.line, self.order, self.dims, self.relative = line, list(order), dims, relative
        self.sizes = {dim: 1 for dim in dims}
        self.columns = shard.shape[1]
        self.mine = shard
        self.begin()

    def begin(self):
        self.step = self.order.pop(0)
        self.arrived = swap(self.mine, *self.step)

    def pair(self):
        place = self.dims.index(self.step)
        outer = math.prod(self.sizes[dim] for dim in self.dims[:place])
        shape = (outer, -1, self.columns)
        return self.mine.reshape(shape), self.arrived.reshape(shape)

    def end(self, piece):
        self.mine = piece.reshape(-1, self.columns)
        self.sizes[self.step] = 2
        self.begin()


class Scatter:
    def __init__(self, line, kept, sent, order, dims, relative):
        self.line, self.order, self.dims, self.relative = line, list(order), dims, relative
        self.sizes = {dim: 2 if dim in self.order else 1 for dim in dims}
        self.columns = kept.shape[-1]
        self.begin(kept, sent)

    def begin(self, kept, sent):
        self.step = self.order.pop(0)
        self.sizes[self.step] = 1
        flat = (-1, self.columns)
        self.terms = [kept.reshape(flat), swap(sent.reshape(flat), *self.step)]

    def pair(self):
        place = self.dims.index(self.order[0])
        outer = math.prod(self.sizes[dim] for dim in self.dims[:place])
        return [term.reshape(outer, 2, -1, self.columns) for term in self.terms]

    def end(self, halves):
        sent, kept = halves
        self.begin(kept, sent)


def go(line, *walks):
    gathers = isinstance(walks[0], Gather)
    steps = [walk.step if gathers else walk.order[0] for walk in walks]
    bits = jnp.concatenate([bit_of(step, walk.relative) for step, walk in zip(steps, walks)])
    results = (merge if gathers else split)(line, [walk.pair() for walk in walks], bits)
    for walk, result in zip(walks, results):
        walk.end(result)


class Weights:
    def __init__(self, pair, step, across):
        self.across = step == across
        self.mine, self.arrived = pair
        if not self.across:
            shape = (2, -1) + self.mine.shape[1:]
            self.mine, self.arrived = self.mine.reshape(shape), self.arrived.reshape(shape)

    def flip(self, core):
        other = object.__new__(Weights)
        other.across = self.across
        other.mine, other.arrived = swap(self.mine, *core), swap(self.arrived, *core)
        return other

    def ins(self):
        return [self.mine, self.arrived]

    def specs(self):
        return [whole(value) if self.across else each(value) for value in self.ins()]

    def scratch(self):
        shape = self.mine.shape[1:]
        return pltpu.VMEM((1,) + shape if self.across else (shape[0], 2) + shape[1:], low)

    def load(self, bit, refs, held):
        mine, arrived = refs
        if self.across:
            step = pl.program_id(0)

            @pl.when(step == 0)
            def _():
                held[...] = mine[...]

            @pl.when(step > 0)
            def _():
                held[...] = arrived[...]

        else:
            held[:, pl.ds(bit, 1)] = mine[...][:, None]
            held[:, pl.ds(1 - bit, 1)] = arrived[...][:, None]
        return held[...].reshape(-1, held.shape[-1])


class Halves:
    def __init__(self, weights, arrived=None):
        self.across, self.arrived = weights.across, arrived
        columns = weights.mine.shape[-1]
        width = weights.mine.shape[1] * (1 if self.across else 2 * weights.mine.shape[2])
        if arrived is None:
            self.outs = [struct((2, width, columns), low)]
        elif self.across:
            self.outs = [struct((width, columns), low)] * 2
        else:
            self.outs = [struct(weights.mine.shape, low)] * 2

    def ins(self):
        return [] if self.arrived is None else [self.arrived]

    def in_specs(self):
        return [each(value) for value in self.ins()]

    def specs(self):
        if self.arrived is not None and self.across:
            return [whole(value) for value in self.outs]
        return [each(value) for value in self.outs]

    def store(self, bit, ins, outs, total):
        if self.arrived is None:
            outs[0][...] = total.astype(low)
            return
        kept, sent = outs
        total = (total + ins[0][...].astype(f32)).astype(low)
        if self.across:
            step = pl.program_id(0)

            @pl.when(step == 0)
            def _():
                kept[...] = total

            @pl.when(step > 0)
            def _():
                sent[...] = total

        else:
            total = total.reshape(kept.shape[0], 2, *kept.shape[1:])
            kept[...] = jnp.where(bit == 1, total[:, 1], total[:, 0])
            sent[...] = jnp.where(bit == 1, total[:, 0], total[:, 1])


def to_owner(take):
    me = lax.axis_index("tensor")
    count = lax.axis_size("tensor")
    return [
        take(me) if step == 0 else swap(take(me ^ step), "tensor", step) for step in range(count)
    ]


def from_owner(blocks):
    return [block if step == 0 else swap(block, "tensor", step) for step, block in enumerate(blocks)]


def unflip(values, dim, axis):
    masks = bits_of(axis)
    shape = values.shape
    values = values.reshape(shape[:dim] + (2,) * len(masks) + shape[dim + 1 :])
    for place, mask in enumerate(masks):
        values = jnp.where(
            my_bit(axis, mask) == 1, jnp.flip(values, dim + place), values
        )
    return values.reshape(shape)


def exchange_all(values):
    shape = values.shape
    dims = [("dp", mask) for mask in bits_of("dp")]
    dims += [("tensor", mask) for mask in bits_of("tensor")]
    values = values.reshape((2,) * len(dims) + shape[2:])
    for dim, (axis, mask) in enumerate(dims):
        kept = lax.slice_in_dim(values, 0, 1, axis=dim)
        arrived = swap(lax.slice_in_dim(values, 1, 2, axis=dim), axis, mask)
        values = jnp.concatenate([kept, arrived], axis=dim)
    return values.reshape(shape)


def mean_last(values):
    return jnp.mean(values, axis=-1, keepdims=True)


def normalise(values):
    center = values - mean_last(values)
    inverse = lax.rsqrt(mean_last(center * center) + norm_eps)
    return center * inverse, inverse


def norm_back(normal, inverse, grad, scale):
    scaled = grad * (1.0 + scale)
    return inverse * (scaled - mean_last(scaled) - normal * mean_last(scaled * normal))


def dg(left, right, left_dim, right_dim):
    return lax.dot_general(
        left, right, (((left_dim,), (right_dim,)), ((), ())), preferred_element_type=f32
    )


def pack_attention_kernel(skip, inputs, output, *outs):
    *skip_outs, qk, vo = outs
    half = skip.shape[1] // 2
    inner = inputs.shape[2]
    for place, out in enumerate(skip_outs):
        out[...] = skip[:, place * half : (place + 1) * half].astype(low)
    qk[:, :inner] = inputs[0].astype(low)
    qk[:, inner:] = inputs[1].astype(low)
    vo[:, :inner] = inputs[2].astype(low)
    vo[:, inner:] = output[...].T.astype(low)


def pack_attention(line, skip, inputs, output):
    outs = [struct((skip.shape[0], skip.shape[1] // 2), low)] * 2
    outs += [struct((inputs.shape[1], 2 * inputs.shape[2]), low)] * 2
    return line.run(pack_attention_kernel, outs, [skip, inputs, output])


def pack_feed_kernel(up, down, *outs):
    half = up.shape[1] // 2
    for place, out in enumerate(outs):
        here = slice(place * half, (place + 1) * half)
        out[:, :half] = up[:, here].astype(low)
        out[:, half:] = down[here, :].T.astype(low)


def pack_feed(line, up, down):
    return line.run(pack_feed_kernel, [struct(up.shape, low)] * 2, [up, down])


def put_together(bit, pairs, held):
    for (mine, arrived), full in zip(pairs, held):
        full[:, pl.ds(bit, 1)] = mine[...][:, None]
        full[:, pl.ds(1 - bit, 1)] = arrived[...][:, None]
    return [full[...].reshape(-1, full.shape[-1]) for full in held]


def together(pairs):
    return [pltpu.VMEM((pair[0].shape[0], 2) + pair[0].shape[1:], low) for pair in pairs]


def enter(line, blocks, pairs, bit, keep):
    count = len(blocks)
    length, depth = sum(block.shape[0] for block in blocks), pairs[0][0].shape[0] * 2 * pairs[0][0].shape[1]
    half = pairs[0][0].shape[-1]

    def kernel(bit, *refs):
        blocks, skips, keep = refs[:count], refs[count : count + 4], refs[count + 4]
        hidden, outer, joined, *held = refs[count + 5 :]
        rows = blocks[0].shape[0]
        for place, block in enumerate(blocks):
            here = slice(place * rows, (place + 1) * rows)
            joined[here, :] = block[:, :depth]
            outer[here, :] = (keep[here, :] * block[:, depth:].astype(f32)).astype(low)
        first, second = put_together(bit[0], (skips[:2], skips[2:]), held)
        hidden[:, :half] = dg(joined[...], first, 1, 0)
        hidden[:, half:] = dg(joined[...], second, 1, 0)

    return line.run(
        kernel,
        [struct((length, 2 * half), f32), struct((length, 2 * half), low)],
        [*blocks, *pairs[0], *pairs[1], keep],
        prefetch=[bit],
        scratch=[pltpu.VMEM((length, depth), low), *together(pairs)],
        flops=4 * length * half * depth,
    )


def half_turn(values):
    lanes = lax.broadcasted_iota(jnp.int32, values.shape, 1) % HEAD_DIM
    width = values.shape[1]
    half = HEAD_DIM // 2
    return jnp.where(
        lanes < half, pltpu.roll(values, width - half, 1), pltpu.roll(values, half, 1)
    )


def shares_of(keys, queries, ok):
    scores = jnp.where(ok > 0, dg(keys, queries, 1, 1), neg_large)
    weights = jnp.exp(scores - jnp.max(scores, axis=0, keepdims=True))
    return weights * (1.0 / jnp.sum(weights, axis=0, keepdims=True))


def attend_piece(normed, qk, vo, cosine, sine, ok, held, mixed):
    inner = qk.shape[1] // 2
    rows = normed.shape[0]
    for part in range(3):
        weight = (qk[:, :inner], qk[:, inner:], vo[:, :inner])[part]
        project = dg(normed[...], weight, 1, 0)
        if part < 2:
            project = project * cosine[...] + half_turn(project) * sine[...]
        if part == 0:
            project = project * HEAD_DIM**-0.5
        held[:, part * inner : (part + 1) * inner] = project.astype(low)
    queries = held[:, :inner]
    keys = held[:, inner : 2 * inner]
    values = held[:, 2 * inner :]
    owner = lax.broadcasted_iota(jnp.int32, (rows, inner), 1) // HEAD_DIM
    zero = jnp.zeros((), low)
    total = None
    for head in range(inner // HEAD_DIM):
        mine = owner == head
        shares = shares_of(keys, jnp.where(mine, queries, zero), ok[...]).astype(low)
        term = dg(shares, jnp.where(mine, values, zero), 0, 0)
        total = term if total is None else total + term
    mixed[...] = total.astype(low)
    return dg(mixed[...], vo[:, inner:], 1, 1).astype(low).astype(f32)


def add_up(total, term, step):
    @pl.when(step == 0)
    def _():
        total[...] = term

    @pl.when(step > 0)
    def _():
        total[...] += term


def attend(line, qk, vo, bits, cosine, sine, ok, hidden, shift, scale, normed=None, before=None):
    rows, width = hidden.shape
    inner = qk.mine.shape[-1] // 2
    total = struct((rows, width), f32)
    outs = [struct((2, rows, 3 * inner), low), struct((2, rows, inner), low), total, struct((rows, width), low)]
    plain = [cosine, sine, ok, hidden, shift, scale]
    plain += [] if before is None else [normed, before]

    def kernel(bits, *refs):
        qk_refs, vo_refs, refs = refs[:2], refs[2:4], refs[4:]
        (cosine, sine, ok, hidden, shift, scale, *more), refs = refs[: len(plain)], refs[len(plain) :]
        held, mixed, out, after, qk_held, vo_held = refs
        step = pl.program_id(0)

        def modulate(values):
            normal, _ = normalise(values)
            after[...] = (normal * (1.0 + scale[...]) + shift[...]).astype(low)

        if not more:

            @pl.when(step == 0)
            def _():
                modulate(hidden[...])

        qk_now = qk.load(bits[0], qk_refs, qk_held)
        vo_now = vo.load(bits[1], vo_refs, vo_held)
        normed = more[0] if more else after
        add_up(out, attend_piece(normed, qk_now, vo_now, cosine, sine, ok, held, mixed), step)
        if more:

            @pl.when(step == pl.num_programs(0) - 1)
            def _():
                total = hidden[...] + (more[1][...] + out[...])
                out[...] = total
                modulate(total)

    return line.run(
        kernel,
        outs,
        [*qk.ins(), *vo.ins(), *plain],
        grid=(2,),
        in_specs=[*qk.specs(), *vo.specs(), *(whole(value) for value in plain)],
        out_specs=[each(outs[0]), each(outs[1]), whole(total), whole(total)],
        scratch=[qk.scratch(), vo.scratch()],
        prefetch=[bits],
        flops=2 * rows * (8 * width * inner + 16 * rows * inner),
    )


def gelu_pair(values):
    root = math.sqrt(2.0 / math.pi)
    cube = 0.044715 * values * values
    slope = jnp.tanh(root * values * (1.0 + cube))
    gate = 0.5 * (1.0 + slope)
    back = gate + 0.5 * values * (1.0 - slope * slope) * root * (1.0 + 3.0 * cube)
    return values * gate, back


def feed(line, normed, outer, weights, bits, place, halves):
    rows, width = normed.shape
    half = weights.mine.shape[-1] // 2
    end = struct((rows, width), low)
    extra = halves.ins()

    def kernel(bits, *refs):
        pair, (normed, outer), refs = refs[:2], refs[2:4], refs[4:]
        before, refs = refs[: len(extra)], refs[len(extra) :]
        outs, (fed, back, fed_total, back_total, held) = refs[: len(halves.outs)], refs[len(halves.outs) :]
        step = pl.program_id(0)
        now = weights.load(bits[place], pair, held)
        up, down = now[:, :half], now[:, half:]
        value, slope = gelu_pair(dg(normed[...], up, 1, 0))
        gated = value.astype(low)
        lifted = (dg(outer[...], down, 1, 0) * slope).astype(low)
        grad = jnp.concatenate([dg(normed[...], lifted, 0, 0), dg(outer[...], gated, 0, 0)], axis=1)
        halves.store(bits[place], before, outs, grad)
        add_up(fed_total, dg(gated, down, 1, 1), step)
        add_up(back_total, dg(lifted, up, 1, 1), step)

        @pl.when(step == pl.num_programs(0) - 1)
        def _():
            fed[...] = fed_total[...].astype(low)
            back[...] = back_total[...].astype(low)

    return line.run(
        kernel,
        [*halves.outs, end, end],
        [*weights.ins(), normed, outer, *extra],
        grid=(2,),
        in_specs=[*weights.specs(), whole(normed), whole(outer), *halves.in_specs()],
        out_specs=[*halves.specs(), whole(end), whole(end)],
        scratch=[pltpu.VMEM((rows, width), f32)] * 2 + [weights.scratch()],
        prefetch=[bits],
        flops=24 * rows * width * half,
    )


def bend_kernel(middle, outer, keep, scale, *refs):
    *parts, result, middle_grad, middle_low, sums = refs
    count = len(parts) // 2
    fed = sum(part[...].astype(f32) for part in parts[:count])
    grad = sum(part[...].astype(f32) for part in parts[count:])
    result[...] = (keep[...] * (middle[...] + fed)).astype(low)
    normal, inverse = normalise(middle[...])
    total = outer[...].astype(f32) + norm_back(normal, inverse, grad, scale[...])
    middle_grad[...] = total
    middle_low[...] = total.astype(low)
    sums[0:1, :] = jnp.sum(grad, axis=0, keepdims=True)
    sums[1:2, :] = jnp.sum(grad * normal, axis=0, keepdims=True)


def bend(line, middle, outer, keep, scale, fed, back):
    shape = middle.shape
    outs = [struct(shape, low), struct(shape, f32), struct((2, shape[1]), f32), struct(shape, low)]

    def kernel(*refs):
        *refs, sums, middle_low = refs
        bend_kernel(*refs, middle_low, sums)

    return line.run(kernel, outs, [middle, outer, keep, scale, *fed, *back])


def back_piece(normed, middle_low, qk, vo, held, mixed, cosine, sine, ok, project):
    inner = qk.shape[1] // 2
    rows = normed.shape[0]
    queries = held[:, :inner]
    keys = held[:, inner : 2 * inner]
    values = held[:, 2 * inner :]
    above = dg(middle_low[...], vo[:, inner:], 1, 0).astype(low)
    owner = lax.broadcasted_iota(jnp.int32, (rows, inner), 1) // HEAD_DIM
    zero = jnp.zeros((), low)
    query_grad = key_grad = value_grad = jnp.zeros((rows, inner), f32)
    for head in range(inner // HEAD_DIM):
        mine = owner == head
        queries_here = jnp.where(mine, queries, zero)
        above_here = jnp.where(mine, above, zero)
        shares = shares_of(keys, queries_here, ok[...])
        share_grad = dg(values, above_here, 1, 1)
        inside = jnp.sum(share_grad * shares, axis=0, keepdims=True)
        score_grad = (shares * (share_grad - inside)).astype(low)
        value_grad += dg(shares.astype(low), above_here, 1, 0)
        key_grad += dg(score_grad, queries_here, 1, 0)
        query_grad += dg(score_grad, jnp.where(mine, keys, zero), 0, 0)
    query_grad = query_grad * HEAD_DIM**-0.5
    for place, grad in enumerate((query_grad, key_grad)):
        turned = grad * cosine[...] - half_turn(grad) * sine[...]
        project[:, place * inner : (place + 1) * inner] = turned.astype(low)
    project[:, 2 * inner :] = value_grad.astype(low)
    qk_grad = dg(normed[...], project[:, : 2 * inner], 0, 0)
    vo_grad = jnp.concatenate(
        [dg(normed[...], project[:, 2 * inner :], 0, 0), dg(middle_low[...], mixed[...], 0, 0)], axis=1
    )
    term = dg(project[:, : 2 * inner], qk, 1, 1)
    term += dg(project[:, 2 * inner :], vo[:, :inner], 1, 1)
    return qk_grad, vo_grad, term.astype(low).astype(f32)


def attend_back(line, normed, middle_low, qk, vo, bits, held, mixed, cosine, sine, ok, qk_halves, vo_halves, last=()):
    rows, width = normed.shape
    inner = qk.mine.shape[-1] // 2
    plain = [normed, middle_low, held, mixed, cosine, sine, ok, *last]
    extra = [*qk_halves.ins(), *vo_halves.ins()]
    counts = len(qk_halves.outs), len(vo_halves.outs)
    scratch = [pltpu.VMEM((rows, 3 * inner), low), qk.scratch(), vo.scratch()]
    outs = [*qk_halves.outs, *vo_halves.outs]
    out_specs = [*qk_halves.specs(), *vo_halves.specs()]
    if last:
        ends = [struct((2, width), f32), struct((rows, width), low)]
        scratch = [pltpu.VMEM((rows, width), f32)] + scratch
    else:
        ends = [struct((rows, width), f32)]

    def kernel(bits, *refs):
        qk_refs, vo_refs, refs = refs[:2], refs[2:4], refs[4:]
        (*args, cosine, sine, ok), refs = refs[:7], refs[7:]
        more, refs = refs[: len(last)], refs[len(last) :]
        before, refs = refs[: len(extra)], refs[len(extra) :]
        qk_outs, refs = refs[: counts[0]], refs[counts[0] :]
        vo_outs, refs = refs[: counts[1]], refs[counts[1] :]
        *ends, total, project, qk_held, vo_held = refs
        step = pl.program_id(0)
        normed, middle_low, held, mixed = args
        qk_now = qk.load(bits[0], qk_refs, qk_held)
        vo_now = vo.load(bits[1], vo_refs, vo_held)
        qk_grad, vo_grad, term = back_piece(
            normed, middle_low, qk_now, vo_now, held, mixed, cosine, sine, ok, project
        )
        qk_halves.store(bits[0], before[:1], qk_outs, qk_grad)
        vo_halves.store(bits[1], before[1:], vo_outs, vo_grad)
        add_up(total, term, step)
        if last:
            ahead, hidden, middle_grad, scale = more
            sums, hidden_low = ends

            @pl.when(step == pl.num_programs(0) - 1)
            def _():
                grad = ahead[...] + total[...]
                normal, inverse = normalise(hidden[...])
                hidden_low[...] = (
                    middle_grad[...] + norm_back(normal, inverse, grad, scale[...])
                ).astype(low)
                sums[0:1, :] = jnp.sum(grad, axis=0, keepdims=True)
                sums[1:2, :] = jnp.sum(grad * normal, axis=0, keepdims=True)

    return line.run(
        kernel,
        [*outs, *ends],
        [*qk.ins(), *vo.ins(), *plain, *extra],
        grid=(2,),
        in_specs=[
            *qk.specs(),
            *vo.specs(),
            *(each(value) if value.ndim == 3 else whole(value) for value in plain),
            *qk_halves.in_specs(),
            *vo_halves.in_specs(),
        ],
        out_specs=out_specs + [whole(value) for value in ends],
        scratch=scratch,
        prefetch=[bits],
        flops=2 * rows * (16 * width * inner + 40 * rows * inner),
    )


def leave(line, blocks, hidden_low, bit, parts):
    count = len(blocks)
    length, width = hidden_low.shape
    depth = 2 * width
    half = width // 2

    def kernel(bit, *refs):
        blocks, hidden_low, outs, joined = refs[:count], refs[count], refs[count + 1 : count + 5], refs[-1]
        rows = blocks[0].shape[0]
        for place, block in enumerate(blocks):
            joined[place * rows : (place + 1) * rows, :] = block[:, :depth]
        mine = bit[0] == 1
        for place in range(2):
            sent, kept = outs[2 * place : 2 * place + 2]
            total = dg(joined[...], hidden_low[:, place * half : (place + 1) * half], 0, 0)
            total = total.reshape(sent.shape[0], 2, -1, half)
            sent[...] = jnp.where(mine, total[:, 0], total[:, 1]).astype(low)
            kept[...] = jnp.where(mine, total[:, 1], total[:, 0]).astype(low)

    return line.run(
        kernel,
        [struct((parts // 2, depth // parts, half), low)] * 4,
        [*blocks, hidden_low],
        prefetch=[bit],
        scratch=[pltpu.VMEM((length, depth), low)],
        flops=2 * length * width * depth,
    )


def inputs_back(line, blocks, pairs, bits):
    count = len(blocks)
    length, width = sum(block.shape[0] for block in blocks), blocks[0].shape[1]
    half = width // 2

    def kernel(bits, *refs):
        blocks, skips = refs[:count], refs[count : count + 4]
        frame_grad, skip_grad, hidden, *held = refs[count + 4 :]
        rows = blocks[0].shape[0]
        for place, block in enumerate(blocks):
            start = pl.multiple_of((bits[1] ^ place) * rows, rows)
            hidden[pl.ds(start, rows), :] = block[...]
        first, second = put_together(bits[0], (skips[:2], skips[2:]), held)
        for here, out in ((slice(0, width), frame_grad), (slice(width, 2 * width), skip_grad)):
            total = dg(hidden[:, :half], first[here, :], 1, 1)
            out[...] = total + dg(hidden[:, half:], second[here, :], 1, 1)

    return line.run(
        kernel,
        [struct((length, width), f32)] * 2,
        [*blocks, *pairs[0], *pairs[1]],
        prefetch=[bits],
        scratch=[pltpu.VMEM((length, width), low), *together(pairs)],
        flops=4 * length * width * width,
    )


def adam_update(master, first, second, grad, rate):
    first_new = beta_first * first + (1.0 - beta_first) * grad
    second_new = beta_second * second + (1.0 - beta_second) * grad * grad
    first_hat = first_new / (1.0 - beta_first**STEP)
    second_hat = second_new / (1.0 - beta_second**STEP)
    master_new = master - rate * (
        first_hat / (jnp.sqrt(second_hat) + adam_eps) + decay_rate * master
    )
    return (first_new, second_new, master_new, master_new.astype(low))


def added(pair):
    return pair[0][...].astype(f32) + pair[1][...].astype(f32)


def store_update(states, grad, rate, outs):
    for out, value in zip(outs, adam_update(*(state[...] for state in states), grad, rate)):
        out[...] = value


def update_outs(master):
    return [struct(master.shape, f32)] * 3 + [struct(master.shape, low)]


def update_feed(line, first, second, ups, downs):
    def kernel(*refs):
        pairs, ups, downs = (refs[:2], refs[2:4]), refs[4:7], refs[7:10]
        up_outs, down_outs = refs[10:14], refs[14:18]
        totals = [added(pair) for pair in pairs]
        half = totals[0].shape[1] // 2
        store_update(ups, jnp.concatenate([total[:, :half] for total in totals], axis=1), rates[4], up_outs)
        store_update(
            downs, jnp.concatenate([total[:, half:].T for total in totals], axis=0), rates[5], down_outs
        )

    return line.run(kernel, update_outs(ups[0]) + update_outs(downs[0]), [*first, *second, *ups, *downs])


def update_attention(line, qk, vo, inputs, outputs):
    def kernel(*refs):
        qk, vo, inputs, outputs = refs[:2], refs[2:4], refs[4:7], refs[7:10]
        input_outs, output_outs = refs[10:14], refs[14:18]
        qk, vo = added(qk), added(vo)
        inner = qk.shape[1] // 2
        for place, grad in enumerate((qk[:, :inner], qk[:, inner:], vo[:, :inner])):
            store_update(
                [state.at[place] for state in inputs], grad, rates[2], [out.at[place] for out in input_outs]
            )
        store_update(outputs, vo[:, inner:].T, rates[3], output_outs)

    return line.run(kernel, update_outs(inputs[0]) + update_outs(outputs[0]), [*qk, *vo, *inputs, *outputs])


def update_skip(line, first, second, skips):
    def kernel(*refs):
        grad = jnp.concatenate([added(refs[:2]), added(refs[2:4])], axis=1)
        store_update(refs[4:7], grad, rates[0], refs[7:11])

    return line.run(kernel, update_outs(skips[0]), [*first, *second, *skips])


def orders():
    dp_bits, tensor_bits = bits_of("dp"), bits_of("tensor")
    far = [("dp", mask) for mask in dp_bits[:-2]]
    near, next_near = ("dp", dp_bits[-1]), ("dp", dp_bits[-2])
    across = ("tensor", tensor_bits[0])
    return (
        far + [next_near, across, near],
        far + [next_near, near, across],
        far + [near, across, next_near],
    )


def body(
    frames,
    skip_frames,
    time_embed,
    lengths,
    out_grad,
    skip_weight,
    adapt_weight,
    input_weight,
    output_weight,
    up_weight,
    down_weight,
    skip_first,
    adapt_first,
    input_first,
    output_first,
    up_first,
    down_first,
    skip_second,
    adapt_second,
    input_second,
    output_second,
    up_second,
    down_second,
):
    micro, _, rows, width = frames.shape
    parts = lax.axis_size("tensor")
    groups = lax.axis_size("dp")
    me = lax.axis_index("tensor")
    inner = input_weight.shape[2]
    heads = inner // HEAD_DIM
    highest = lax.Precision.HIGHEST
    order_p, order_q, order_r = orders()
    core = ("tensor", bits_of("tensor")[-1])
    across = ("tensor", bits_of("tensor")[0])
    dims = [across] + [("dp", mask) for mask in bits_of("dp")]
    all_dims = dims[1:] + [across, core]
    core_bit = bit_array(*core)
    bits = jnp.concatenate([bit_of(order_p[-1], (across,)), bit_of(order_q[-1], (across,))])
    line = Line()

    skip_one, skip_two, qk_shard, vo_shard = pack_attention(
        line, skip_weight, input_weight.transpose(1, 0, 2), output_weight
    )
    skip_walks = (
        Gather(line, skip_one, order_p + [core], all_dims, ()),
        Gather(line, skip_two, order_r + [core], all_dims, ()),
    )
    blocks = to_owner(
        lambda index: jnp.concatenate(
            [pick(value, index, 0)[0] for value in (frames, skip_frames, out_grad)], axis=1
        )
    )
    attention_walks = (
        Gather(line, qk_shard, order_p, dims, (across,)),
        Gather(line, vo_shard, order_q, dims, (across,)),
    )
    adapt_low = adapt_weight.astype(low)
    time_values = time_embed[:, 0, :].astype(f32)
    time_low = jax.nn.silu(time_values).astype(low)
    time_all = line.tie(unflip(time_low, 0, "tensor"))[None]
    for mask in reversed(bits_of("dp")):
        time_all = jnp.concatenate([time_all, swap(time_all, "dp", mask)], axis=0)
    time_rows = time_all.reshape(groups * micro, width)
    adapt_mine = jnp.dot(time_rows, adapt_low, preferred_element_type=f32).reshape(groups, micro, -1)
    adapt_vector = unflip(unflip(exchange_all(adapt_mine), 0, "dp"), 1, "tensor").reshape(1, -1)
    shift_one, scale_one, shift_two, scale_two = jnp.split(adapt_vector, 4, axis=1)

    row_index = jnp.concatenate(
        [(me ^ step) * rows + jnp.arange(rows, dtype=jnp.int32) for step in range(parts)]
    )
    length = pick(lengths, me, 0)[0]
    keep = (row_index < length).astype(f32)[:, None]
    half = HEAD_DIM // 2
    frequency = 10000.0 ** (-jnp.arange(half).astype(f32) / half)
    angles = row_index.astype(f32)[:, None] * frequency[None, :]
    cosine = jnp.tile(jnp.cos(angles), (1, 2 * heads))
    sine = jnp.tile(jnp.concatenate([-jnp.sin(angles), jnp.sin(angles)], axis=1), (1, heads))

    more = range(len(bits_of("dp")) - 3)
    for _ in more:
        go(line, *skip_walks)
        go(line, *attention_walks)
    go(line, *skip_walks)
    go(line, *attention_walks)
    go(line, *skip_walks)
    go(line, *attention_walks)
    go(line, *skip_walks)
    feed_walks = [
        Gather(line, shard, order, dims, (across,))
        for shard, order in zip(pack_feed(line, up_weight, down_weight), (order_p, order_q))
    ]
    go(line, *skip_walks)
    go(line, *attention_walks)
    for _ in more:
        go(line, *feed_walks)
    go(line, *feed_walks)
    skip_pairs = [walk.pair() for walk in skip_walks]
    hidden, outer = enter(line, blocks, skip_pairs, core_bit, keep)
    go(line, *feed_walks)
    qk_own, vo_own = (Weights(walk.pair(), walk.step, across) for walk in attention_walks)
    qk_other, vo_other = qk_own.flip(core), vo_own.flip(core)
    held_own, mixed_own, attended, normed_one = attend(
        line, qk_own, vo_own, bits, cosine, sine, keep, hidden, shift_one, scale_one
    )
    go(line, *feed_walks)
    held_other, mixed_other, middle, normed_two = attend(
        line,
        qk_other,
        vo_other,
        bits,
        cosine,
        sine,
        keep,
        hidden,
        shift_two,
        scale_two,
        normed=normed_one,
        before=attended,
    )
    feed_own = [Weights(walk.pair(), walk.step, across) for walk in feed_walks]
    feed_other = [weights.flip(core) for weights in feed_own]
    fed, back, feed_arrived, feed_scatters = [], [], [], []
    for place, weights in enumerate(feed_other):
        grad, *ends = feed(line, normed_two, outer, weights, bits, place, Halves(weights))
        feed_arrived.append(swap(grad, *core))
        fed.append(ends[0])
        back.append(ends[1])
    for place, weights in enumerate(feed_own):
        kept, sent, *ends = feed(
            line, normed_two, outer, weights, bits, place, Halves(weights, feed_arrived[place])
        )
        feed_scatters.append(
            Scatter(line, kept, sent, (order_p, order_q)[place][::-1], dims, (across,))
        )
        fed.append(ends[0])
        back.append(ends[1])
    feed_one, feed_two = feed_scatters
    result, middle_grad, sums_two, middle_low = bend(line, middle, outer, keep, scale_two, fed, back)
    results = from_owner([result[step * rows : (step + 1) * rows] for step in range(parts)])
    results = unflip(jnp.stack(results), 0, "tensor")
    qk_grad, vo_grad, ahead = attend_back(
        line,
        normed_one,
        middle_low,
        qk_other,
        vo_other,
        bits,
        held_other,
        mixed_other,
        cosine,
        sine,
        keep,
        Halves(qk_other),
        Halves(vo_other),
    )
    qk_arrived, vo_arrived = swap(qk_grad, *core), swap(vo_grad, *core)
    go(line, feed_one)
    qk_kept, qk_sent, vo_kept, vo_sent, sums_one, hidden_low = attend_back(
        line,
        normed_one,
        middle_low,
        qk_own,
        vo_own,
        bits,
        held_own,
        mixed_own,
        cosine,
        sine,
        keep,
        Halves(qk_own, qk_arrived),
        Halves(vo_own, vo_arrived),
        last=(ahead, hidden, middle_grad, scale_one),
    )
    attention_scatters = [
        Scatter(line, qk_kept, qk_sent, order_p[::-1], dims, (across,)),
        Scatter(line, vo_kept, vo_sent, order_q[::-1], dims, (across,)),
    ]
    go(line, feed_one, feed_two)
    leaving = leave(line, blocks, hidden_low, core_bit, groups * parts)
    skip_scatters = [
        Scatter(line, kept, sent, [core] + order[::-1], all_dims, ())
        for sent, kept, order in zip(leaving[::2], leaving[1::2], (order_p, order_q))
    ]
    hidden_back = from_owner([hidden_low[step * rows : (step + 1) * rows] for step in range(parts)])
    go(line, *skip_scatters)
    go(line, *attention_scatters)
    frame_grads, skip_grads = inputs_back(
        line, hidden_back, skip_pairs, jnp.concatenate([core_bit, me.astype(jnp.int32)[None]])
    )
    frame_grads, skip_grads = frame_grads.reshape(frames.shape), skip_grads.reshape(frames.shape)
    go(line, feed_one, feed_two)
    go(line, *skip_scatters)
    go(line, *attention_scatters)
    go(line, feed_two)
    adapt_back = jnp.concatenate([sums_one.reshape(-1), sums_two.reshape(-1)]).reshape(
        groups, parts, -1
    )
    adapt_rows = exchange_all(unflip(unflip(adapt_back, 0, "dp"), 1, "tensor"))
    adapt_rows = adapt_rows.reshape(groups * micro, -1)
    adapt_sum = lax.dot_general(
        time_rows.astype(f32), adapt_rows, (((0,), (0,)), ((), ())), precision=highest
    )
    time_part = lax.dot_general(
        adapt_rows, adapt_low.astype(f32), (((1,), (1,)), ((), ())), precision=highest
    ).reshape(groups, micro, width)
    for mask in bits_of("dp"):
        time_part = time_part[:mask] + swap(time_part[mask:], "dp", mask)
    time_part = unflip(time_part[0], 0, "tensor")
    for mask in bits_of("tensor"):
        time_part = time_part + swap(time_part, "tensor", mask)
    sigmoid = jax.nn.sigmoid(time_values)
    time_grad = time_part * (sigmoid * (1.0 + time_values * (1.0 - sigmoid)))

    go(line, *skip_scatters)
    go(line, *attention_scatters)
    go(line, *skip_scatters)
    for _ in more:
        go(line, feed_one, feed_two)
        go(line, *attention_scatters)
        go(line, *skip_scatters)
    feed_new = update_feed(
        line,
        feed_one.terms,
        feed_two.terms,
        (up_weight, up_first, up_second),
        (down_weight, down_first, down_second),
    )
    attention_new = update_attention(
        line,
        attention_scatters[0].terms,
        attention_scatters[1].terms,
        [state.transpose(1, 0, 2) for state in (input_weight, input_first, input_second)],
        (output_weight, output_first, output_second),
    )
    skip_new = update_skip(
        line,
        skip_scatters[0].terms,
        skip_scatters[1].terms,
        (skip_weight, skip_first, skip_second),
    )
    adapt_new = adam_update(adapt_weight, adapt_first, adapt_second, adapt_sum, rates[1])
    return (
        results[:, None],
        frame_grads,
        skip_grads,
        time_grad[:, None, :],
        *skip_new,
        *adapt_new,
        *(value.transpose(1, 0, 2) for value in attention_new[:4]),
        *attention_new[4:],
        *feed_new,
    )


def solution(mesh):
    return jax.shard_map(
        body,
        mesh=mesh,
        in_specs=(
            P(None, "dp", "tensor", None),
            P(None, "dp", "tensor", None),
            P(None, "dp", None),
            P(None, "dp"),
            P(None, "dp", "tensor", None),
            P(("dp", "tensor"), None),
            P(None, ("dp", "tensor")),
            P("dp", None, "tensor"),
            P("tensor", "dp"),
            P("dp", "tensor"),
            P("tensor", "dp"),
            P(("dp", "tensor"), None),
            P(None, ("dp", "tensor")),
            P("dp", None, "tensor"),
            P("tensor", "dp"),
            P("dp", "tensor"),
            P("tensor", "dp"),
            P(("dp", "tensor"), None),
            P(None, ("dp", "tensor")),
            P("dp", None, "tensor"),
            P("tensor", "dp"),
            P("dp", "tensor"),
            P("tensor", "dp"),
        ),
        out_specs=(
            P(None, "dp", "tensor", None),
            P(None, "dp", "tensor", None),
            P(None, "dp", "tensor", None),
            P(None, "dp", None),
            P(("dp", "tensor"), None),
            P(("dp", "tensor"), None),
            P(("dp", "tensor"), None),
            P(("dp", "tensor"), None),
            P(None, ("dp", "tensor")),
            P(None, ("dp", "tensor")),
            P(None, ("dp", "tensor")),
            P(None, ("dp", "tensor")),
            P("dp", None, "tensor"),
            P("dp", None, "tensor"),
            P("dp", None, "tensor"),
            P("dp", None, "tensor"),
            P("tensor", "dp"),
            P("tensor", "dp"),
            P("tensor", "dp"),
            P("tensor", "dp"),
            P("dp", "tensor"),
            P("dp", "tensor"),
            P("dp", "tensor"),
            P("dp", "tensor"),
            P("tensor", "dp"),
            P("tensor", "dp"),
            P("tensor", "dp"),
            P("tensor", "dp"),
        ),
        check_vma=False,
    )
```

```python
import functools
import math

import jax
import jax.numpy as jnp
from jax import lax
from jax.experimental import pallas as pl
from jax.experimental.pallas import tpu as pltpu
from jax.sharding import Mesh
from jax.sharding import PartitionSpec as P

HEAD_DIM = 64
TENSOR = ("high", "low")
STEP = 10
MEBI = 1 << 20

norm_eps = 1e-06
neg_large = -1e30
rates = (0.04, 0.06, 0.06, 0.6, 0.06, 0.03)
beta_first = 0.9
beta_second = 0.999
decay_rate = 0.01
adam_eps = 1e-08
low = jnp.bfloat16
f32 = jnp.float32


def bits_of(axis):
    count = lax.axis_size(axis).bit_length() - 1
    return [1 << place for place in reversed(range(count))]


def my_bit(axis, mask):
    return (lax.axis_index(axis) // mask) % 2


def swap(values, axis, mask):
    count = lax.axis_size(axis)
    return lax.ppermute(values, axis, [(i, i ^ mask) for i in range(count)])


def pick(values, index, dim):
    return lax.dynamic_index_in_dim(values, index, dim, keepdims=False)


def struct(shape, dtype):
    return jax.ShapeDtypeStruct(shape, dtype)


class Whole:
    def __init__(self, array, each=False):
        self.each = each


def whole(array):
    return Whole(array)


def each(array):
    return Whole(array, each=True)


class Line:
    def __init__(self):
        self.last = ()
        steps = [("dp", mask) for mask in bits_of("dp")] + [(TENSOR, mask) for mask in bits_of(TENSOR)]
        self.place = {step: 2 + place for place, step in enumerate(steps)}
        me = lax.axis_index(TENSOR)
        self.bits = jnp.stack([jnp.zeros((), me.dtype), me] + [my_bit(*step) for step in steps])

    def run(self, kernel, outs, ins, *, grid=(1,), in_specs=None, out_specs=None, scratch=(), flops=0, limit=14):
        in_specs = [Whole(value) for value in ins] if in_specs is None else in_specs
        out_specs = [Whole(value) for value in outs] if out_specs is None else out_specs
        marks = [isinstance(spec, Whole) and spec.each for spec in (*in_specs, *out_specs)]
        in_specs, out_specs = (
            [pl.BlockSpec(memory_space=pltpu.VMEM) if isinstance(spec, Whole) else spec for spec in specs]
            for specs in (in_specs, out_specs)
        )
        deps = self.last
        skip = 1 + len(ins)

        def inner(*refs):
            bits, *refs = (*refs[:skip], *refs[skip + len(deps) :])
            parts = [ref.at[pl.program_id(0)] if mark else ref for ref, mark in zip(refs, marks)]
            kernel(bits, *parts, *refs[len(marks) :])

        moved = sum(value.size * value.dtype.itemsize for value in (*ins, *outs))
        results = pl.pallas_call(
            inner,
            grid_spec=pltpu.PrefetchScalarGridSpec(
                num_scalar_prefetch=1,
                grid=grid,
                in_specs=in_specs + [pl.BlockSpec(memory_space=pl.ANY)] * len(deps),
                out_specs=out_specs,
                scratch_shapes=list(scratch),
            ),
            out_shape=list(outs),
            cost_estimate=pl.CostEstimate(flops=flops, bytes_accessed=moved, transcendentals=0),
            compiler_params=pltpu.CompilerParams(vmem_limit_bytes=limit * MEBI),
        )(self.bits, *ins, *deps)
        self.last = (results[-1],)
        return results

    def need(self, *values):
        self.last += values

    def tie(self, values):
        return lax.optimization_barrier((values, self.last))[0]


def merge(line, pairs, places):
    count = len(pairs)

    def kernel(bits, *refs):
        for place in range(count):
            (mine, other), out = refs[2 * place : 2 * place + 2], refs[2 * count + place]
            bit = bits[places[place]]
            out[:, pl.ds(bit, 1)] = mine[...][:, None]
            out[:, pl.ds(1 - bit, 1)] = other[...][:, None]

    outs = [struct((mine.shape[0], 2) + mine.shape[1:], low) for mine, _ in pairs]
    return line.run(kernel, outs, [value for pair in pairs for value in pair])


def split(line, pairs, places):
    count = len(pairs)

    def kernel(bits, *refs):
        for place in range(count):
            terms, outs = refs[2 * place : 2 * place + 2], refs[2 * (count + place) : 2 * (count + place) + 2]
            bit = bits[places[place]]
            for index, out in zip((1 - bit, bit), outs):
                total = sum(term[:, pl.ds(index, 1)].astype(f32) for term in terms)
                out[...] = total[:, 0].astype(low)

    outs = [struct(pair[0].shape[:1] + pair[0].shape[2:], low) for pair in pairs for _ in range(2)]
    results = line.run(kernel, outs, [value for pair in pairs for value in pair])
    return list(zip(results[::2], results[1::2]))


class Gather:
    def __init__(self, line, shard, order, dims, relative):
        self.line, self.order, self.dims, self.relative = line, list(order), dims, relative
        self.sizes = {dim: 1 for dim in dims}
        self.columns = shard.shape[1]
        self.mine = line.tie(shard)
        self.begin()

    def begin(self):
        self.step = self.order.pop(0)
        self.arrived = swap(self.mine, *self.step)

    def pair(self):
        place = self.dims.index(self.step)
        outer = math.prod(self.sizes[dim] for dim in self.dims[:place])
        shape = (outer, -1, self.columns)
        return self.mine.reshape(shape), self.arrived.reshape(shape)

    def end(self, piece):
        self.mine = piece.reshape(-1, self.columns)
        self.sizes[self.step] = 2
        self.begin()


class Scatter:
    def __init__(self, line, kept, sent, order, dims, relative, arrived=None):
        self.line, self.order, self.dims, self.relative = line, list(order), dims, relative
        self.sizes = {dim: 2 if dim in self.order else 1 for dim in dims}
        self.columns = kept.shape[-1]
        self.begin(kept, sent, arrived)

    def begin(self, kept, sent, arrived=None):
        self.step = self.order.pop(0)
        self.sizes[self.step] = 1
        flat = (-1, self.columns)
        if arrived is None:
            arrived = swap(sent.reshape(flat), *self.step)
        self.terms = [kept.reshape(flat), arrived.reshape(flat)]

    def pair(self):
        place = self.dims.index(self.order[0])
        outer = math.prod(self.sizes[dim] for dim in self.dims[:place])
        return [term.reshape(outer, 2, -1, self.columns) for term in self.terms]

    def end(self, halves):
        sent, kept = halves
        self.begin(kept, sent)


def go(line, *walks):
    gathers = isinstance(walks[0], Gather)
    steps = [walk.step if gathers else walk.order[0] for walk in walks]
    places = [0 if step in walk.relative else line.place[step] for step, walk in zip(steps, walks)]
    results = (merge if gathers else split)(line, [walk.pair() for walk in walks], places)
    for walk, result in zip(walks, results):
        walk.end(result)


class Pieces:
    def __init__(self, line, walk, across, arrays=None):
        self.line, self.walk, self.across = line, walk, walk.step == across
        self.columns = walk.columns
        self.arrays = arrays
        if arrays is None:
            self.arrays = list(walk.pair())
            if not self.across:
                self.arrays = [value.reshape((2, -1) + value.shape[1:]) for value in self.arrays]

    def flip(self, core, tied=False):
        across = (TENSOR, bits_of(TENSOR)[0])
        arrays = self.line.tie(self.arrays) if tied else self.arrays
        return Pieces(self.line, self.walk, across, [swap(value, *core) for value in arrays])

    def specs(self):
        return [whole(value) if self.across else each(value) for value in self.arrays]

    def scratch(self):
        shape = self.arrays[0].shape[1:]
        return [pltpu.VMEM((1,) + shape if self.across else (shape[0], 2) + shape[1:], low)]

    def load(self, bits, refs, held):
        mine, arrived = refs
        if self.across:
            step = pl.program_id(0)

            @pl.when(step == 0)
            def _():
                held[0][...] = mine[...]

            @pl.when(step > 0)
            def _():
                held[0][...] = arrived[...]

            return held[0][...].reshape(-1, self.columns)
        return put_together(bits[self.line.place[self.walk.step]], mine, arrived, held[0])


class Both:
    def __init__(self, first, second):
        self.parts = first, second
        self.arrays = first.arrays + second.arrays
        self.columns = first.columns + second.columns

    def flip(self, core):
        return Both(*(part.flip(core) for part in self.parts))

    def specs(self):
        return [spec for part in self.parts for spec in part.specs()]

    def scratch(self):
        return [space for part in self.parts for space in part.scratch()]

    def load(self, bits, refs, held):
        first, second = self.parts
        return first.load(bits, refs[:2], held[:1]), second.load(bits, refs[2:], held[1:])


class Halves:
    def __init__(self, line, width, columns, step=None, dims=(), arrived=None, start=0):
        self.line, self.step, self.arrived, self.start, self.columns = line, step, arrived, start, columns
        self.across = step is not None and step == dims[0]
        if step is None:
            self.outs = [struct((2, width, columns), low)]
        elif self.across:
            self.outs = [struct((width, columns), low)] * 2
        else:
            outer = 1 << (dims.index(step) - 1)
            self.outs = [struct((2, outer, width // (2 * outer), columns), low)] * 2

    def specs(self):
        return [whole(value) if self.across else each(value) for value in self.outs]

    def store(self, bits, before, outs, total):
        if self.step is None:
            outs[0][...] = total.astype(low)
            return
        kept, sent = outs
        arrived = before[:, self.start : self.start + self.columns]
        total = (total + arrived.astype(f32)).astype(low)
        if self.across:
            step = pl.program_id(0)

            @pl.when(step == 0)
            def _():
                kept[...] = total

            @pl.when(step > 0)
            def _():
                sent[...] = total

        else:
            mine = bits[self.line.place[self.step]] == 1
            total = total.reshape(kept.shape[0], 2, *kept.shape[1:])
            kept[...] = jnp.where(mine, total[:, 1], total[:, 0])
            sent[...] = jnp.where(mine, total[:, 0], total[:, 1])


def from_owner(blocks):
    return [block if step == 0 else swap(block, TENSOR, step) for step, block in enumerate(blocks)]


def unflip(values, dim, axis):
    masks = bits_of(axis)
    shape = values.shape
    values = values.reshape(shape[:dim] + (2,) * len(masks) + shape[dim + 1 :])
    for place, mask in enumerate(masks):
        values = jnp.where(
            my_bit(axis, mask) == 1, jnp.flip(values, dim + place), values
        )
    return values.reshape(shape)


def exchange_steps(line, values):
    shape = values.shape
    dims = [("dp", mask) for mask in bits_of("dp")]
    dims += [(TENSOR, mask) for mask in bits_of(TENSOR)]
    values = values.reshape((2,) * len(dims) + shape[2:])
    for dim, (axis, mask) in enumerate(dims):
        values = line.tie(values)
        kept = lax.slice_in_dim(values, 0, 1, axis=dim)
        arrived = swap(lax.slice_in_dim(values, 1, 2, axis=dim), axis, mask)
        values = jnp.concatenate([kept, arrived], axis=dim)
        line.need(values)
        yield None
    yield values.reshape(shape)


def mean_last(values):
    return jnp.mean(values, axis=-1, keepdims=True)


def normalise(values):
    center = values - mean_last(values)
    inverse = lax.rsqrt(mean_last(center * center) + norm_eps)
    return center * inverse, inverse


def norm_back(normal, inverse, grad, scale):
    scaled = grad * (1.0 + scale)
    return inverse * (scaled - mean_last(scaled) - normal * mean_last(scaled * normal))


def dg(left, right, left_dim, right_dim):
    return lax.dot_general(
        left, right, (((left_dim,), (right_dim,)), ((), ())), preferred_element_type=f32
    )


def pack(line, skip, inputs, output, up, down):
    inner, block = inputs.shape[2], up.shape[1] // 2

    def kernel(bits, skip, inputs, output, up, down, skip_out, qk, vo, *feeds):
        skip_out[...] = skip[...].astype(low)
        qk[:, :inner] = inputs[0].astype(low)
        qk[:, inner:] = inputs[1].astype(low)
        vo[:, :inner] = inputs[2].astype(low)
        vo[:, inner:] = output[...].T.astype(low)
        for place, out in enumerate(feeds):
            here = slice(place * block, (place + 1) * block)
            out[:, :block] = up[:, here].astype(low)
            out[:, block:] = down[here, :].T.astype(low)

    outs = [struct(skip.shape, low)] + [struct((inputs.shape[1], 2 * inner), low)] * 2 + [struct(up.shape, low)] * 2
    return line.run(kernel, outs, [skip, inputs, output, up, down])


def cut(line, arrays):
    count, _, rows, width = arrays[0].shape

    def kernel(bits, *refs):
        for place in range(count):

            @pl.when(pl.program_id(0) == place)
            def _():
                for index in range(len(arrays)):
                    here = slice(index * width, (index + 1) * width)
                    refs[len(arrays) + place][:, here] = refs[index][0, 0]

    out = struct((rows, len(arrays) * width), low)
    return line.run(
        kernel,
        [out] * count,
        list(arrays),
        grid=(count,),
        in_specs=[pl.BlockSpec((1, 1, rows, width), lambda i, bits: (bits[1] ^ i, 0, 0, 0))] * len(arrays),
    )


def put_together(bit, mine, arrived, held):
    held[:, pl.ds(bit, 1)] = mine[...][:, None]
    held[:, pl.ds(1 - bit, 1)] = arrived[...][:, None]
    return held[...].reshape(-1, held.shape[-1])


def together(pair):
    return pltpu.VMEM((pair[0].shape[0], 2) + pair[0].shape[1:], low)


def enter(line, blocks, pair, place, keep):
    count = len(blocks)
    length, width = sum(block.shape[0] for block in blocks), pair[0].shape[-1]
    depth = 2 * width

    def kernel(bits, *refs):
        blocks, skips, keep = refs[:count], refs[count : count + 2], refs[count + 2]
        hidden, outer, joined, held = refs[count + 3 :]
        rows = blocks[0].shape[0]
        for index, block in enumerate(blocks):
            here = slice(index * rows, (index + 1) * rows)
            joined[here, :] = block[:, :depth]
            outer[here, :] = (keep[here, :] * block[:, depth:].astype(f32)).astype(low)
        put_together(bits[place], *skips, held)
        half = width // 2
        for here in (slice(0, half), slice(half, width)):
            hidden[:, here] = dg(joined[...], held[:, :, :, here].reshape(depth, half), 1, 0)

    return line.run(
        kernel,
        [struct((length, width), f32), struct((length, width), low)],
        [*blocks, *pair, keep],
        scratch=[pltpu.VMEM((length, depth), low), together(pair)],
        flops=2 * length * width * depth,
        limit=14,
    )


def half_turn(values):
    lanes = lax.broadcasted_iota(jnp.int32, values.shape, 1) % HEAD_DIM
    width = values.shape[1]
    half = HEAD_DIM // 2
    return jnp.where(
        lanes < half, pltpu.roll(values, width - half, 1), pltpu.roll(values, half, 1)
    )


def shares_of(keys, queries, ok):
    scores = jnp.where(ok > 0, dg(keys, queries, 1, 1), neg_large)
    weights = jnp.exp(scores - jnp.max(scores, axis=0, keepdims=True))
    return weights * (1.0 / jnp.sum(weights, axis=0, keepdims=True))


def attend_piece(normed, qk, vo, cosine, sine, ok, held, mixed):
    inner = qk.shape[1] // 2
    rows = normed.shape[0]
    for part in range(3):
        weight = (qk[:, :inner], qk[:, inner:], vo[:, :inner])[part]
        project = dg(normed[...], weight, 1, 0)
        if part < 2:
            project = project * cosine[...] + half_turn(project) * sine[...]
        if part == 0:
            project = project * HEAD_DIM**-0.5
        held[:, part * inner : (part + 1) * inner] = project.astype(low)
    queries = held[:, :inner]
    keys = held[:, inner : 2 * inner]
    values = held[:, 2 * inner :]
    owner = lax.broadcasted_iota(jnp.int32, (rows, inner), 1) // HEAD_DIM
    zero = jnp.zeros((), low)
    total = None
    for head in range(inner // HEAD_DIM):
        mine = owner == head
        shares = shares_of(keys, jnp.where(mine, queries, zero), ok[...]).astype(low)
        term = dg(shares, jnp.where(mine, values, zero), 0, 0)
        total = term if total is None else total + term
    mixed[...] = total.astype(low)
    return dg(mixed[...], vo[:, inner:], 1, 1).astype(low).astype(f32)


def add_up(total, term, step):
    @pl.when(step == 0)
    def _():
        total[...] = term

    @pl.when(step > 0)
    def _():
        total[...] += term


def attend(line, weights, cosine, sine, ok, hidden, shift, scale, normed=None, before=None):
    rows, width = hidden.shape
    inner = weights.columns // 4
    total = struct((rows, width), f32)
    outs = [struct((2, rows, 3 * inner), low), struct((2, rows, inner), low), total, struct((rows, width), low)]
    plain = [cosine, sine, ok, hidden, shift, scale]
    plain += [] if before is None else [normed, before]
    arrays = weights.arrays

    def kernel(bits, *refs):
        tables, refs = refs[: len(arrays)], refs[len(arrays) :]
        (cosine, sine, ok, hidden, shift, scale, *more), refs = refs[: len(plain)], refs[len(plain) :]
        held, mixed, out, after, *scratch = refs
        step = pl.program_id(0)

        def modulate(values):
            normal, _ = normalise(values)
            after[...] = (normal * (1.0 + scale[...]) + shift[...]).astype(low)

        if not more:

            @pl.when(step == 0)
            def _():
                modulate(hidden[...])

        qk, vo = weights.load(bits, tables, scratch)
        normed = more[0] if more else after
        term = attend_piece(normed, qk, vo, cosine, sine, ok, held, mixed)
        add_up(out, term, step)
        if more:

            @pl.when(step == pl.num_programs(0) - 1)
            def _():
                total = hidden[...] + (more[1][...] + out[...])
                out[...] = total
                modulate(total)

    return line.run(
        kernel,
        outs,
        [*arrays, *plain],
        grid=(2,),
        in_specs=[*weights.specs(), *(whole(value) for value in plain)],
        out_specs=[each(outs[0]), each(outs[1]), whole(total), whole(total)],
        scratch=weights.scratch(),
        flops=2 * rows * (8 * width * inner + 16 * rows * inner),
        limit=20,
    )


def gelu_pair(values):
    root = math.sqrt(2.0 / math.pi)
    cube = 0.044715 * values * values
    slope = jnp.tanh(root * values * (1.0 + cube))
    gate = 0.5 * (1.0 + slope)
    back = gate + 0.5 * values * (1.0 - slope * slope) * root * (1.0 + 3.0 * cube)
    return values * gate, back


def feed(line, normed, outer, weights, halves, before=None):
    rows, width = normed.shape
    half = weights.columns // 2
    end = struct((rows, width), low)
    arrays = weights.arrays
    extra = [] if before is None else [before]

    def kernel(bits, *refs):
        tables, (normed, outer, *refs) = refs[: len(arrays)], refs[len(arrays) :]
        before, refs = refs[: len(extra)], refs[len(extra) :]
        outs, (fed, back, fed_total, back_total, *scratch) = refs[: len(halves.outs)], refs[len(halves.outs) :]
        step = pl.program_id(0)
        now = weights.load(bits, tables, scratch)
        up, down = now[:, :half], now[:, half:]
        value, slope = gelu_pair(dg(normed[...], up, 1, 0))
        gated = value.astype(low)
        lifted = (dg(outer[...], down, 1, 0) * slope).astype(low)
        grad = jnp.concatenate([dg(normed[...], lifted, 0, 0), dg(outer[...], gated, 0, 0)], axis=1)
        halves.store(bits, *(before or (None,)), outs, grad)
        add_up(fed_total, dg(gated, down, 1, 1), step)
        add_up(back_total, dg(lifted, up, 1, 1), step)

        @pl.when(step == pl.num_programs(0) - 1)
        def _():
            fed[...] = fed_total[...].astype(low)
            back[...] = back_total[...].astype(low)

    return line.run(
        kernel,
        [*halves.outs, end, end],
        [*arrays, normed, outer, *extra],
        grid=(2,),
        in_specs=[*weights.specs(), whole(normed), whole(outer), *(each(value) for value in extra)],
        out_specs=[*halves.specs(), whole(end), whole(end)],
        scratch=[pltpu.VMEM((rows, width), f32)] * 2 + weights.scratch(),
        flops=24 * rows * width * half,
        limit=22,
    )


def bend_kernel(middle, outer, keep, scale, *refs):
    *parts, result, middle_grad, middle_low, sums = refs
    count = len(parts) // 2
    fed = sum(part[...].astype(f32) for part in parts[:count])
    grad = sum(part[...].astype(f32) for part in parts[count:])
    result[...] = (keep[...] * (middle[...] + fed)).astype(low)
    normal, inverse = normalise(middle[...])
    total = outer[...].astype(f32) + norm_back(normal, inverse, grad, scale[...])
    middle_grad[...] = total
    middle_low[...] = total.astype(low)
    sums[0:1, :] = jnp.sum(grad, axis=0, keepdims=True)
    sums[1:2, :] = jnp.sum(grad * normal, axis=0, keepdims=True)


def bend(line, middle, outer, keep, scale, fed, back):
    shape = middle.shape
    outs = [struct(shape, low), struct(shape, f32), struct((2, shape[1]), f32), struct(shape, low)]

    def kernel(bits, *refs):
        *refs, sums, middle_low = refs
        bend_kernel(*refs, middle_low, sums)

    return line.run(kernel, outs, [middle, outer, keep, scale, *fed, *back], limit=14)


def back_piece(normed, middle_low, qk, vo, held, mixed, cosine, sine, ok, project):
    inner = qk.shape[1] // 2
    rows = normed.shape[0]
    queries = held[:, :inner]
    keys = held[:, inner : 2 * inner]
    values = held[:, 2 * inner :]
    above = dg(middle_low[...], vo[:, inner:], 1, 0).astype(low)
    owner = lax.broadcasted_iota(jnp.int32, (rows, inner), 1) // HEAD_DIM
    zero = jnp.zeros((), low)
    query_grad = key_grad = value_grad = jnp.zeros((rows, inner), f32)
    for head in range(inner // HEAD_DIM):
        mine = owner == head
        queries_here = jnp.where(mine, queries, zero)
        above_here = jnp.where(mine, above, zero)
        shares = shares_of(keys, queries_here, ok[...])
        share_grad = dg(values, above_here, 1, 1)
        inside = jnp.sum(share_grad * shares, axis=0, keepdims=True)
        score_grad = (shares * (share_grad - inside)).astype(low)
        value_grad += dg(shares.astype(low), above_here, 1, 0)
        key_grad += dg(score_grad, queries_here, 1, 0)
        query_grad += dg(score_grad, jnp.where(mine, keys, zero), 0, 0)
    query_grad = query_grad * HEAD_DIM**-0.5
    for place, grad in enumerate((query_grad, key_grad)):
        turned = grad * cosine[...] - half_turn(grad) * sine[...]
        project[:, place * inner : (place + 1) * inner] = turned.astype(low)
    project[:, 2 * inner :] = value_grad.astype(low)
    qk_grad = dg(normed[...], project[:, : 2 * inner], 0, 0)
    vo_grad = jnp.concatenate(
        [dg(normed[...], project[:, 2 * inner :], 0, 0), dg(middle_low[...], mixed[...], 0, 0)], axis=1
    )
    term = dg(project[:, : 2 * inner], qk, 1, 1)
    term += dg(project[:, 2 * inner :], vo[:, :inner], 1, 1)
    return qk_grad, vo_grad, term.astype(low).astype(f32)


def attend_back(line, normed, middle_low, weights, held, mixed, cosine, sine, ok, parts, before=None, last=()):
    rows, width = normed.shape
    inner = weights.columns // 4
    arrays = weights.arrays
    plain = [normed, middle_low, held, mixed, cosine, sine, ok, *last]
    extra = [] if before is None else [before]
    scratch = [pltpu.VMEM((rows, 3 * inner), low), *weights.scratch()]
    if last:
        ends = [struct((2, width), f32), struct((rows, width), low)]
        scratch = [pltpu.VMEM((rows, width), f32)] + scratch
    else:
        ends = [struct((rows, width), f32)]

    def kernel(bits, *refs):
        tables, refs = refs[: len(arrays)], refs[len(arrays) :]
        (*args, cosine, sine, ok), refs = refs[:7], refs[7:]
        more, refs = refs[: len(last)], refs[len(last) :]
        before, refs = refs[: len(extra)], refs[len(extra) :]
        outs = []
        for part in parts:
            outs.append(refs[: len(part.outs)])
            refs = refs[len(part.outs) :]
        marks, (total, project, *scratch) = (refs[:2], refs[2:]) if last else ((), refs)
        step = pl.program_id(0)
        normed, middle_low, held, mixed = args
        qk, vo = weights.load(bits, tables, scratch)
        *grads, term = back_piece(
            normed, middle_low, qk, vo, held, mixed, cosine, sine, ok, project
        )
        if len(parts) == 1:
            grads = [jnp.concatenate(grads, axis=1)]
        for part, out, grad in zip(parts, outs, grads):
            part.store(bits, *(before or (None,)), out, grad)
        add_up(total, term, step)
        if last:
            ahead, hidden, middle_grad, scale = more
            sums, hidden_low = marks

            @pl.when(step == pl.num_programs(0) - 1)
            def _():
                grad = ahead[...] + total[...]
                normal, inverse = normalise(hidden[...])
                hidden_low[...] = (
                    middle_grad[...] + norm_back(normal, inverse, grad, scale[...])
                ).astype(low)
                sums[0:1, :] = jnp.sum(grad, axis=0, keepdims=True)
                sums[1:2, :] = jnp.sum(grad * normal, axis=0, keepdims=True)

    outs = [value for part in parts for value in part.outs]
    return line.run(
        kernel,
        [*outs, *ends],
        [*arrays, *plain, *extra],
        grid=(2,),
        in_specs=[
            *weights.specs(),
            *(each(value) if value.ndim == 3 else whole(value) for value in plain),
            *(each(value) for value in extra),
        ],
        out_specs=[spec for part in parts for spec in part.specs()] + [whole(value) for value in ends],
        scratch=scratch,
        flops=2 * rows * (16 * width * inner + 40 * rows * inner),
        limit=24,
    )


def leave(line, blocks, hidden_low, place, parts):
    count = len(blocks)
    length, width = hidden_low.shape
    depth = 2 * width

    def kernel(bits, *refs):
        blocks, hidden_low, sent, kept, joined = refs[:count], *refs[count:]
        rows = blocks[0].shape[0]
        for index, block in enumerate(blocks):
            joined[index * rows : (index + 1) * rows, :] = block[:, :depth]
        mine = bits[place] == 1
        half = width // 2
        for here in (slice(0, half), slice(half, width)):
            total = dg(joined[...], hidden_low[:, here], 0, 0)
            total = total.reshape(sent.shape[0], 2, -1, half)
            sent[:, :, here] = jnp.where(mine, total[:, 0], total[:, 1]).astype(low)
            kept[:, :, here] = jnp.where(mine, total[:, 1], total[:, 0]).astype(low)

    return line.run(
        kernel,
        [struct((parts // 2, depth // parts, width), low)] * 2,
        [*blocks, hidden_low],
        scratch=[pltpu.VMEM((length, depth), low)],
        flops=2 * length * width * depth,
        limit=16,
    )


def inputs_back(line, blocks, results, pair, place):
    count = len(blocks)
    length, width = sum(block.shape[0] for block in blocks), blocks[0].shape[1]

    def kernel(bits, *refs):
        blocks, results, skips = refs[:count], refs[count : 2 * count], refs[2 * count : 2 * count + 2]
        frame_grad, skip_grad, result, hidden, held = refs[2 * count + 2 :]
        rows = blocks[0].shape[0]
        for index in range(count):
            start = pl.multiple_of((bits[1] ^ index) * rows, rows)
            hidden[pl.ds(start, rows), :] = blocks[index][...]
            result[pl.ds(start, rows), :] = results[index][...]
        skip = put_together(bits[place], *skips, held)
        frame_grad[...] = dg(hidden[...], skip[:width], 1, 1)
        skip_grad[...] = dg(hidden[...], skip[width:], 1, 1)

    return line.run(
        kernel,
        [struct((length, width), f32)] * 2 + [struct((length, width), low)],
        [*blocks, *results, *pair],
        scratch=[pltpu.VMEM((length, width), low), together(pair)],
        flops=4 * length * width * width,
        limit=14,
    )


def adam_update(master, first, second, grad, rate):
    first_new = beta_first * first + (1.0 - beta_first) * grad
    second_new = beta_second * second + (1.0 - beta_second) * grad * grad
    first_hat = first_new / (1.0 - beta_first**STEP)
    second_hat = second_new / (1.0 - beta_second**STEP)
    master_new = master - rate * (
        first_hat / (jnp.sqrt(second_hat) + adam_eps) + decay_rate * master
    )
    return (first_new, second_new, master_new, master_new.astype(low))


def added(pair):
    return pair[0][...].astype(f32) + pair[1][...].astype(f32)


def store_update(states, grad, rate, outs):
    for out, value in zip(outs, adam_update(*(state[...] for state in states), grad, rate)):
        out[...] = value


def update_outs(master):
    return [struct(master.shape, f32)] * 3 + [struct(master.shape, low)]


def update_feed(line, first, second, ups, downs):
    def kernel(bits, *refs):
        pairs, ups, downs = (refs[:2], refs[2:4]), refs[4:7], refs[7:10]
        up_outs, down_outs = refs[10:14], refs[14:18]
        totals = [added(pair) for pair in pairs]
        half = totals[0].shape[1] // 2
        store_update(ups, jnp.concatenate([total[:, :half] for total in totals], axis=1), rates[4], up_outs)
        store_update(
            downs, jnp.concatenate([total[:, half:].T for total in totals], axis=0), rates[5], down_outs
        )

    return line.run(kernel, update_outs(ups[0]) + update_outs(downs[0]), [*first, *second, *ups, *downs], limit=10)


def update_attention(line, qk, vo, inputs, outputs):
    def kernel(bits, *refs):
        qk, vo, inputs, outputs = refs[:2], refs[2:4], refs[4:7], refs[7:10]
        input_outs, output_outs = refs[10:14], refs[14:18]
        qk, vo = added(qk), added(vo)
        inner = qk.shape[1] // 2
        for place, grad in enumerate((qk[:, :inner], qk[:, inner:], vo[:, :inner])):
            store_update(
                [state.at[place] for state in inputs], grad, rates[2], [out.at[place] for out in input_outs]
            )
        store_update(outputs, vo[:, inner:].T, rates[3], output_outs)

    return line.run(kernel, update_outs(inputs[0]) + update_outs(outputs[0]), [*qk, *vo, *inputs, *outputs], limit=10)


def update_skip(line, pair, skips):
    def kernel(bits, *refs):
        store_update(refs[2:5], added(refs[:2]), rates[0], refs[5:9])

    return line.run(kernel, update_outs(skips[0]), [*pair, *skips], limit=8)


def orders():
    dp_bits, tensor_bits = bits_of("dp"), bits_of(TENSOR)
    far = [("dp", mask) for mask in dp_bits[:-2]]
    y, z = ("dp", dp_bits[-1]), ("dp", dp_bits[-2])
    x = (TENSOR, tensor_bits[0])
    return {
        "xzy": far + [x, z, y],
        "yzx": far + [y, z, x],
        "zxy": far + [z, x, y],
        "zyx": far + [z, y, x],
        "yxz": far + [y, x, z],
        "xyz": far + [x, y, z],
    }


def body(
    frames,
    skip_frames,
    time_embed,
    lengths,
    out_grad,
    skip_weight,
    adapt_weight,
    input_weight,
    output_weight,
    up_weight,
    down_weight,
    skip_first,
    adapt_first,
    input_first,
    output_first,
    up_first,
    down_first,
    skip_second,
    adapt_second,
    input_second,
    output_second,
    up_second,
    down_second,
):
    micro, _, rows, width = frames.shape
    parts = lax.axis_size(TENSOR)
    groups = lax.axis_size("dp")
    me = lax.axis_index(TENSOR)
    inner = input_weight.shape[2]
    heads = inner // HEAD_DIM
    highest = lax.Precision.HIGHEST
    order = orders()
    skip_order, skip_back_order = order["xzy"], order["zyx"]
    attention_orders, attention_back_orders = (order["xyz"], order["xzy"]), (order["xzy"], order["yzx"])
    feed_orders, feed_back_orders = (order["yzx"], order["zxy"]), (order["zxy"], order["zyx"])
    core = (TENSOR, bits_of(TENSOR)[-1])
    across = (TENSOR, bits_of(TENSOR)[0])
    dims = [across] + [("dp", mask) for mask in bits_of("dp")]
    all_dims = dims[1:] + [across, core]
    line = Line()

    adapt_low = adapt_weight.astype(low)
    time_values = time_embed[:, 0, :].astype(f32)
    time_low = jax.nn.silu(time_values).astype(low)

    def modulation():
        time_all = unflip(time_low, 0, TENSOR)[None]
        for mask in reversed(bits_of("dp")):
            time_all = line.tie(time_all)
            time_all = jnp.concatenate([time_all, swap(time_all, "dp", mask)], axis=0)
            line.need(time_all)
            yield None
        time_rows = time_all.reshape(groups * micro, width)
        adapt_mine = jnp.dot(time_rows, adapt_low, preferred_element_type=f32).reshape(groups, micro, -1)
        for adapt_all in exchange_steps(line, adapt_mine):
            yield time_rows, adapt_all

    modulate = modulation()

    row_index = jnp.concatenate(
        [(me ^ step) * rows + jnp.arange(rows, dtype=jnp.int32) for step in range(parts)]
    )
    length = pick(lengths, me, 0)[0]
    keep = (row_index < length).astype(f32)[:, None]
    half = HEAD_DIM // 2
    frequency = 10000.0 ** (-jnp.arange(half).astype(f32) / half)
    angles = row_index.astype(f32)[:, None] * frequency[None, :]
    cosine = jnp.tile(jnp.cos(angles), (1, 2 * heads))
    sine = jnp.tile(jnp.concatenate([-jnp.sin(angles), jnp.sin(angles)], axis=1), (1, heads))

    next(modulate)
    skip_shard, qk_shard, vo_shard, *feed_shards = pack(
        line, skip_weight, input_weight.transpose(1, 0, 2), output_weight, up_weight, down_weight
    )
    skip_walk = Gather(line, skip_shard, skip_order + [core], all_dims, ())
    attention_walks = [
        Gather(line, shard, each_order, dims, (across,))
        for shard, each_order in zip((qk_shard, vo_shard), attention_orders)
    ]
    next(modulate)
    blocks = list(cut(line, (frames, skip_frames, out_grad)))
    blocks[2] = swap(blocks[2], TENSOR, 2)
    feed_walks = [
        Gather(line, shard, each_order, dims, (across,))
        for shard, each_order in zip(feed_shards, feed_orders)
    ]
    next(modulate)
    more = range(len(bits_of("dp")) - 3)
    for _ in more:
        go(line, skip_walk)
        go(line, *attention_walks)
        go(line, *feed_walks)
    go(line, skip_walk)
    next(modulate)
    go(line, *attention_walks)
    next(modulate)
    go(line, skip_walk)
    next(modulate)
    go(line, *feed_walks)
    next(modulate)
    line.need(blocks[2])
    blocks[3] = swap(line.tie(blocks[3]), TENSOR, 3)
    go(line, *attention_walks)
    for time_rows, adapt_all in modulate:
        pass
    go(line, skip_walk)
    adapt_vector = unflip(unflip(adapt_all, 0, "dp"), 1, TENSOR).reshape(1, -1)
    shift_one, scale_one, shift_two, scale_two = jnp.split(adapt_vector, 4, axis=1)
    go(line, *feed_walks)
    line.need(blocks[3])
    blocks[1] = swap(line.tie(blocks[1]), TENSOR, 1)
    go(line, *attention_walks)
    go(line, skip_walk)
    skip_pair = skip_walk.pair()
    hidden, outer = enter(line, blocks, skip_pair, line.place[core], keep)
    go(line, *feed_walks)
    attention_own = Both(*(Pieces(line, walk, across) for walk in attention_walks))
    held_own, mixed_own, attended, normed_one = attend(
        line, attention_own, cosine, sine, keep, hidden, shift_one, scale_one
    )
    attention_other = attention_own.flip(core)
    held_other, mixed_other, middle, normed_two = attend(
        line, attention_other, cosine, sine, keep, hidden, shift_two, scale_two, normed=normed_one, before=attended
    )
    fed, back, feed_arrived, feed_scatters = [], [], [], []
    feed_own = [Pieces(line, walk, across) for walk in feed_walks]
    columns = feed_shards[0].shape[1]
    feed_other = [pieces.flip(core, tied=True) for pieces in feed_own]
    for pieces in feed_other:
        grad, *ends = feed(line, normed_two, outer, pieces, Halves(line, width, columns))
        feed_arrived.append(swap(grad, *core))
        fed.append(ends[0])
        back.append(ends[1])
    for pieces, arrived, each_order in zip(feed_own, feed_arrived, feed_back_orders):
        halves = Halves(line, width, columns, each_order[-1], dims, arrived)
        kept, sent, *ends = feed(line, normed_two, outer, pieces, halves, arrived)
        feed_scatters.append(Scatter(line, kept, sent, each_order[::-1], dims, (across,)))
        fed.append(ends[0])
        back.append(ends[1])
    feed_one, feed_two = feed_scatters
    result, middle_grad, sums_two, middle_low = bend(line, middle, outer, keep, scale_two, fed, back)
    results = from_owner([result[step * rows : (step + 1) * rows] for step in range(parts)])
    qk_other, vo_other, ahead = attend_back(
        line,
        normed_one,
        middle_low,
        attention_other,
        held_other,
        mixed_other,
        cosine,
        sine,
        keep,
        [Halves(line, width, 2 * inner)] * 2,
    )
    attention_arrived = [swap(grad, *core) for grad in (qk_other, vo_other)]
    go(line, feed_one)
    go(line, feed_two)
    qk_grad, vo_grad, sums_one, hidden_low = attend_back(
        line,
        normed_one,
        middle_low,
        attention_own,
        held_own,
        mixed_own,
        cosine,
        sine,
        keep,
        [Halves(line, width, 2 * inner)] * 2,
        last=(ahead, hidden, middle_grad, scale_one),
    )
    attention_scatters = [
        Scatter(line, grad, None, [core] + each_order[::-1], dims, (across,), arrived)
        for grad, arrived, each_order in zip((qk_grad, vo_grad), attention_arrived, attention_back_orders)
    ]
    go(line, *attention_scatters)
    go(line, feed_one, feed_two)
    line.need(*results[1:])
    skip_sent, skip_kept = leave(line, blocks, hidden_low, line.place[core], groups * parts)
    skip_scatter = Scatter(line, skip_kept, skip_sent, [core] + skip_back_order[::-1], all_dims, ())
    hidden_back = from_owner([hidden_low[step * rows : (step + 1) * rows] for step in range(parts)])

    def modulation_back():
        adapt_back = jnp.concatenate([sums_one.reshape(-1), sums_two.reshape(-1)]).reshape(
            groups, parts, -1
        )
        for adapt_rows in exchange_steps(line, unflip(unflip(adapt_back, 0, "dp"), 1, TENSOR)):
            yield None
        adapt_rows = adapt_rows.reshape(groups * micro, -1)
        adapt_sum = lax.dot_general(
            time_rows.astype(f32), adapt_rows, (((0,), (0,)), ((), ())), precision=highest
        )
        time_part = lax.dot_general(
            adapt_rows, adapt_low.astype(f32), (((1,), (1,)), ((), ())), precision=highest
        ).reshape(groups, micro, width)
        for mask in bits_of("dp"):
            time_part = line.tie(time_part)
            time_part = time_part[:mask] + swap(time_part[mask:], "dp", mask)
            yield None
        time_part = unflip(time_part[0], 0, TENSOR)
        for mask in bits_of(TENSOR):
            time_part = line.tie(time_part)
            time_part = time_part + swap(time_part, TENSOR, mask)
            yield None
        yield adapt_sum, time_part

    modulate_back = modulation_back()
    go(line, skip_scatter)
    next(modulate_back)
    go(line, *attention_scatters)
    next(modulate_back)
    go(line, feed_one, feed_two)
    next(modulate_back)
    go(line, skip_scatter)
    next(modulate_back)
    go(line, *attention_scatters)
    next(modulate_back)
    line.need(feed_one.terms[1], feed_two.terms[1])
    line.need(*hidden_back[1:])
    frame_grads, skip_grads, results = inputs_back(
        line, hidden_back, results, skip_pair, line.place[core]
    )
    frame_grads, skip_grads = frame_grads.reshape(frames.shape), skip_grads.reshape(frames.shape)
    next(modulate_back)
    go(line, skip_scatter)
    next(modulate_back)
    go(line, *attention_scatters)
    next(modulate_back)
    go(line, skip_scatter)
    for _ in more:
        go(line, feed_one, feed_two)
        go(line, *attention_scatters)
        go(line, skip_scatter)
    next(modulate_back)
    line.need(*(walk.terms[1] for walk in attention_scatters))
    feed_new = update_feed(
        line,
        feed_one.terms,
        feed_two.terms,
        (up_weight, up_first, up_second),
        (down_weight, down_first, down_second),
    )
    for ends in modulate_back:
        pass
    adapt_sum, time_part = ends
    sigmoid = jax.nn.sigmoid(time_values)
    time_grad = time_part * (sigmoid * (1.0 + time_values * (1.0 - sigmoid)))
    attention_new = update_attention(
        line,
        attention_scatters[0].terms,
        attention_scatters[1].terms,
        [state.transpose(1, 0, 2) for state in (input_weight, input_first, input_second)],
        (output_weight, output_first, output_second),
    )
    skip_new = update_skip(line, skip_scatter.terms, (skip_weight, skip_first, skip_second))
    adapt_new = adam_update(adapt_weight, adapt_first, adapt_second, adapt_sum, rates[1])
    return (
        results.reshape(frames.shape),
        frame_grads,
        skip_grads,
        time_grad[:, None, :],
        *skip_new,
        *adapt_new,
        *(value.transpose(1, 0, 2) for value in attention_new[:4]),
        *attention_new[4:],
        *feed_new,
    )


def solution(mesh):
    groups, parts = mesh.devices.shape
    split_mesh = Mesh(mesh.devices.reshape(groups, parts // 2, 2), ("dp", *TENSOR))
    return jax.shard_map(
        body,
        mesh=split_mesh,
        in_specs=(
            P(None, "dp", TENSOR, None),
            P(None, "dp", TENSOR, None),
            P(None, "dp", None),
            P(None, "dp"),
            P(None, "dp", TENSOR, None),
            P(("dp", *TENSOR), None),
            P(None, ("dp", *TENSOR)),
            P("dp", None, TENSOR),
            P(TENSOR, "dp"),
            P("dp", TENSOR),
            P(TENSOR, "dp"),
            P(("dp", *TENSOR), None),
            P(None, ("dp", *TENSOR)),
            P("dp", None, TENSOR),
            P(TENSOR, "dp"),
            P("dp", TENSOR),
            P(TENSOR, "dp"),
            P(("dp", *TENSOR), None),
            P(None, ("dp", *TENSOR)),
            P("dp", None, TENSOR),
            P(TENSOR, "dp"),
            P("dp", TENSOR),
            P(TENSOR, "dp"),
        ),
        out_specs=(
            P(None, "dp", TENSOR, None),
            P(None, "dp", TENSOR, None),
            P(None, "dp", TENSOR, None),
            P(None, "dp", None),
            P(("dp", *TENSOR), None),
            P(("dp", *TENSOR), None),
            P(("dp", *TENSOR), None),
            P(("dp", *TENSOR), None),
            P(None, ("dp", *TENSOR)),
            P(None, ("dp", *TENSOR)),
            P(None, ("dp", *TENSOR)),
            P(None, ("dp", *TENSOR)),
            P("dp", None, TENSOR),
            P("dp", None, TENSOR),
            P("dp", None, TENSOR),
            P("dp", None, TENSOR),
            P(TENSOR, "dp"),
            P(TENSOR, "dp"),
            P(TENSOR, "dp"),
            P(TENSOR, "dp"),
            P("dp", TENSOR),
            P("dp", TENSOR),
            P("dp", TENSOR),
            P("dp", TENSOR),
            P(TENSOR, "dp"),
            P(TENSOR, "dp"),
            P(TENSOR, "dp"),
            P(TENSOR, "dp"),
        ),
        check_vma=False,
    )
```

```python
import functools
import math

import jax
import jax.numpy as jnp
from jax import lax
from jax.experimental import pallas as pl
from jax.experimental.pallas import tpu as pltpu
from jax.sharding import Mesh
from jax.sharding import PartitionSpec as P

HEAD_DIM = 64
TENSOR = ("high", "low")
STEP = 10
MEBI = 1 << 20

norm_eps = 1e-06
neg_large = -1e30
rates = (0.04, 0.06, 0.06, 0.6, 0.06, 0.03)
beta_first = 0.9
beta_second = 0.999
decay_rate = 0.01
adam_eps = 1e-08
low = jnp.bfloat16
f32 = jnp.float32


def bits_of(axis):
    count = lax.axis_size(axis).bit_length() - 1
    return [1 << place for place in reversed(range(count))]


def my_bit(axis, mask):
    return (lax.axis_index(axis) // mask) % 2


def swap(values, axis, mask):
    count = lax.axis_size(axis)
    return lax.ppermute(values, axis, [(i, i ^ mask) for i in range(count)])


def pick(values, index, dim):
    return lax.dynamic_index_in_dim(values, index, dim, keepdims=False)


def struct(shape, dtype):
    return jax.ShapeDtypeStruct(shape, dtype)


class Whole:
    def __init__(self, array, each=False):
        self.each = each


def whole(array):
    return Whole(array)


def each(array):
    return Whole(array, each=True)


class Line:
    def __init__(self):
        self.last = ()
        steps = [("dp", mask) for mask in bits_of("dp")] + [(TENSOR, mask) for mask in bits_of(TENSOR)]
        self.place = {step: 2 + place for place, step in enumerate(steps)}
        me = lax.axis_index(TENSOR)
        self.bits = jnp.stack([jnp.zeros((), me.dtype), me] + [my_bit(*step) for step in steps])

    def run(self, kernel, outs, ins, *, grid=(1,), in_specs=None, out_specs=None, scratch=(), flops=0, limit=14):
        in_specs = [Whole(value) for value in ins] if in_specs is None else in_specs
        out_specs = [Whole(value) for value in outs] if out_specs is None else out_specs
        marks = [isinstance(spec, Whole) and spec.each for spec in (*in_specs, *out_specs)]
        in_specs, out_specs = (
            [pl.BlockSpec(memory_space=pltpu.VMEM) if isinstance(spec, Whole) else spec for spec in specs]
            for specs in (in_specs, out_specs)
        )
        deps = self.last
        skip = 1 + len(ins)

        def inner(*refs):
            bits, *refs = (*refs[:skip], *refs[skip + len(deps) :])
            parts = [ref.at[pl.program_id(0)] if mark else ref for ref, mark in zip(refs, marks)]
            kernel(bits, *parts, *refs[len(marks) :])

        moved = sum(value.size * value.dtype.itemsize for value in (*ins, *outs))
        results = pl.pallas_call(
            inner,
            grid_spec=pltpu.PrefetchScalarGridSpec(
                num_scalar_prefetch=1,
                grid=grid,
                in_specs=in_specs + [pl.BlockSpec(memory_space=pl.ANY)] * len(deps),
                out_specs=out_specs,
                scratch_shapes=list(scratch),
            ),
            out_shape=list(outs),
            cost_estimate=pl.CostEstimate(flops=flops, bytes_accessed=moved, transcendentals=0),
            compiler_params=pltpu.CompilerParams(vmem_limit_bytes=limit * MEBI),
        )(self.bits, *ins, *deps)
        self.last = (results[-1],)
        return results

    def need(self, *values):
        self.last += values

    def tie(self, values):
        return lax.optimization_barrier((values, self.last))[0]


def merge(line, pairs, places):
    count = len(pairs)

    def kernel(bits, *refs):
        for place in range(count):
            (mine, other), out = refs[2 * place : 2 * place + 2], refs[2 * count + place]
            bit = bits[places[place]]
            out[:, pl.ds(bit, 1)] = mine[...][:, None]
            out[:, pl.ds(1 - bit, 1)] = other[...][:, None]

    outs = [struct((mine.shape[0], 2) + mine.shape[1:], low) for mine, _ in pairs]
    return line.run(kernel, outs, [value for pair in pairs for value in pair])


def split(line, pairs, places):
    count = len(pairs)

    def kernel(bits, *refs):
        for place in range(count):
            terms, outs = refs[2 * place : 2 * place + 2], refs[2 * (count + place) : 2 * (count + place) + 2]
            bit = bits[places[place]]
            for index, out in zip((1 - bit, bit), outs):
                total = sum(term[:, pl.ds(index, 1)].astype(f32) for term in terms)
                out[...] = total[:, 0].astype(low)

    outs = [struct(pair[0].shape[:1] + pair[0].shape[2:], low) for pair in pairs for _ in range(2)]
    results = line.run(kernel, outs, [value for pair in pairs for value in pair])
    return list(zip(results[::2], results[1::2]))


class Gather:
    def __init__(self, line, shard, order, dims, relative):
        self.line, self.order, self.dims, self.relative = line, list(order), dims, relative
        self.sizes = {dim: 1 for dim in dims}
        self.columns = shard.shape[1]
        self.mine = line.tie(shard)
        self.begin()

    def begin(self):
        self.step = self.order.pop(0)
        self.arrived = swap(self.mine, *self.step)

    def pair(self):
        place = self.dims.index(self.step)
        outer = math.prod(self.sizes[dim] for dim in self.dims[:place])
        shape = (outer, -1, self.columns)
        return self.mine.reshape(shape), self.arrived.reshape(shape)

    def end(self, piece):
        self.mine = piece.reshape(-1, self.columns)
        self.sizes[self.step] = 2
        self.begin()


class Scatter:
    def __init__(self, line, kept, sent, order, dims, relative, arrived=None):
        self.line, self.order, self.dims, self.relative = line, list(order), dims, relative
        self.sizes = {dim: 2 if dim in self.order else 1 for dim in dims}
        self.columns = kept.shape[-1]
        self.begin(kept, sent, arrived)

    def begin(self, kept, sent, arrived=None):
        self.step = self.order.pop(0)
        self.sizes[self.step] = 1
        flat = (-1, self.columns)
        if arrived is None:
            arrived = swap(sent.reshape(flat), *self.step)
        self.terms = [kept.reshape(flat), arrived.reshape(flat)]

    def pair(self):
        place = self.dims.index(self.order[0])
        outer = math.prod(self.sizes[dim] for dim in self.dims[:place])
        return [term.reshape(outer, 2, -1, self.columns) for term in self.terms]

    def end(self, halves):
        sent, kept = halves
        self.begin(kept, sent)


def go(line, *walks):
    gathers = isinstance(walks[0], Gather)
    steps = [walk.step if gathers else walk.order[0] for walk in walks]
    places = [0 if step in walk.relative else line.place[step] for step, walk in zip(steps, walks)]
    results = (merge if gathers else split)(line, [walk.pair() for walk in walks], places)
    for walk, result in zip(walks, results):
        walk.end(result)


class Pieces:
    def __init__(self, line, walk, across, arrays=None):
        self.line, self.walk, self.across = line, walk, walk.step == across
        self.columns = walk.columns
        self.arrays = arrays
        if arrays is None:
            self.arrays = list(walk.pair())
            if not self.across:
                self.arrays = [value.reshape((2, -1) + value.shape[1:]) for value in self.arrays]

    def flip(self, core, tied=False):
        across = (TENSOR, bits_of(TENSOR)[0])
        arrays = self.line.tie(self.arrays) if tied else self.arrays
        return Pieces(self.line, self.walk, across, [swap(value, *core) for value in arrays])

    def specs(self):
        return [whole(value) if self.across else each(value) for value in self.arrays]

    def scratch(self):
        shape = self.arrays[0].shape[1:]
        return [pltpu.VMEM((1,) + shape if self.across else (shape[0], 2) + shape[1:], low)]

    def load(self, bits, refs, held):
        mine, arrived = refs
        if self.across:
            step = pl.program_id(0)

            @pl.when(step == 0)
            def _():
                held[0][...] = mine[...]

            @pl.when(step > 0)
            def _():
                held[0][...] = arrived[...]

            return held[0][...].reshape(-1, self.columns)
        return put_together(bits[self.line.place[self.walk.step]], mine, arrived, held[0])


class Both:
    def __init__(self, first, second):
        self.parts = first, second
        self.arrays = first.arrays + second.arrays
        self.columns = first.columns + second.columns

    def flip(self, core):
        return Both(*(part.flip(core) for part in self.parts))

    def specs(self):
        return [spec for part in self.parts for spec in part.specs()]

    def scratch(self):
        return [space for part in self.parts for space in part.scratch()]

    def load(self, bits, refs, held):
        first, second = self.parts
        return first.load(bits, refs[:2], held[:1]), second.load(bits, refs[2:], held[1:])


class Halves:
    def __init__(self, line, width, columns, step=None, dims=(), arrived=None, start=0):
        self.line, self.step, self.arrived, self.start, self.columns = line, step, arrived, start, columns
        self.across = step is not None and step == dims[0]
        if step is None:
            self.outs = [struct((2, width, columns), low)]
        elif self.across:
            self.outs = [struct((width, columns), low)] * 2
        else:
            outer = 1 << (dims.index(step) - 1)
            self.outs = [struct((2, outer, width // (2 * outer), columns), low)] * 2

    def specs(self):
        return [whole(value) if self.across else each(value) for value in self.outs]

    def store(self, bits, before, outs, total):
        if self.step is None:
            outs[0][...] = total.astype(low)
            return
        kept, sent = outs
        arrived = before[:, self.start : self.start + self.columns]
        total = (total + arrived.astype(f32)).astype(low)
        if self.across:
            step = pl.program_id(0)

            @pl.when(step == 0)
            def _():
                kept[...] = total

            @pl.when(step > 0)
            def _():
                sent[...] = total

        else:
            mine = bits[self.line.place[self.step]] == 1
            total = total.reshape(kept.shape[0], 2, *kept.shape[1:])
            kept[...] = jnp.where(mine, total[:, 1], total[:, 0])
            sent[...] = jnp.where(mine, total[:, 0], total[:, 1])


def from_owner(blocks):
    return [block if step == 0 else swap(block, TENSOR, step) for step, block in enumerate(blocks)]


def unflip(values, dim, axis):
    masks = bits_of(axis)
    shape = values.shape
    values = values.reshape(shape[:dim] + (2,) * len(masks) + shape[dim + 1 :])
    for place, mask in enumerate(masks):
        values = jnp.where(
            my_bit(axis, mask) == 1, jnp.flip(values, dim + place), values
        )
    return values.reshape(shape)


def exchange_steps(line, values, needed=False):
    shape = values.shape
    dims = [("dp", mask) for mask in bits_of("dp")]
    dims += [(TENSOR, mask) for mask in bits_of(TENSOR)]
    values = values.reshape((2,) * len(dims) + shape[2:])
    turns = list(range(len(dims)))
    if not needed:
        turns = turns[-1:] + turns[-3:-1][::-1] + turns[:-3]
        turns = turns[:1] + turns[2:] + turns[1:2]
    for dim, (axis, mask) in [(dim, dims[dim]) for dim in turns]:
        values = line.tie(values)
        kept = lax.slice_in_dim(values, 0, 1, axis=dim)
        arrived = swap(lax.slice_in_dim(values, 1, 2, axis=dim), axis, mask)
        values = jnp.concatenate([kept, arrived], axis=dim)
        if needed:
            line.need(values)
        yield None
    yield values.reshape(shape)


def mean_last(values):
    return jnp.mean(values, axis=-1, keepdims=True)


def normalise(values):
    center = values - mean_last(values)
    inverse = lax.rsqrt(mean_last(center * center) + norm_eps)
    return center * inverse, inverse


def norm_back(normal, inverse, grad, scale):
    scaled = grad * (1.0 + scale)
    return inverse * (scaled - mean_last(scaled) - normal * mean_last(scaled * normal))


def dg(left, right, left_dim, right_dim):
    return lax.dot_general(
        left, right, (((left_dim,), (right_dim,)), ((), ())), preferred_element_type=f32
    )


def pack(line, skip, inputs, output, up, down):
    inner, block = inputs.shape[2], up.shape[1] // 2

    def kernel(bits, skip, inputs, output, up, down, skip_out, qk, vo, *feeds):
        skip_out[...] = skip[...].astype(low)
        qk[:, :inner] = inputs[0].astype(low)
        qk[:, inner:] = inputs[1].astype(low)
        vo[:, :inner] = inputs[2].astype(low)
        vo[:, inner:] = output[...].T.astype(low)
        for place, out in enumerate(feeds):
            here = slice(place * block, (place + 1) * block)
            out[:, :block] = up[:, here].astype(low)
            out[:, block:] = down[here, :].T.astype(low)

    outs = [struct(skip.shape, low)] + [struct((inputs.shape[1], 2 * inner), low)] * 2 + [struct(up.shape, low)] * 2
    return line.run(kernel, outs, [skip, inputs, output, up, down])


def cut(line, arrays):
    count, _, rows, width = arrays[0].shape

    def kernel(bits, *refs):
        for place in range(count):

            @pl.when(pl.program_id(0) == place)
            def _():
                for index in range(len(arrays)):
                    here = slice(index * width, (index + 1) * width)
                    refs[len(arrays) + place][:, here] = refs[index][0, 0]

    out = struct((rows, len(arrays) * width), low)
    return line.run(
        kernel,
        [out] * count,
        list(arrays),
        grid=(count,),
        in_specs=[pl.BlockSpec((1, 1, rows, width), lambda i, bits: (bits[1] ^ i, 0, 0, 0))] * len(arrays),
    )


def put_together(bit, mine, arrived, held):
    held[:, pl.ds(bit, 1)] = mine[...][:, None]
    held[:, pl.ds(1 - bit, 1)] = arrived[...][:, None]
    return held[...].reshape(-1, held.shape[-1])


def together(pair):
    return pltpu.VMEM((pair[0].shape[0], 2) + pair[0].shape[1:], low)


def enter(line, blocks, pair, place, keep):
    count = len(blocks)
    length, width = sum(block.shape[0] for block in blocks), pair[0].shape[-1]
    depth = 2 * width

    def kernel(bits, *refs):
        blocks, skips, keep = refs[:count], refs[count : count + 2], refs[count + 2]
        hidden, outer, joined, held = refs[count + 3 :]
        rows = blocks[0].shape[0]
        for index, block in enumerate(blocks):
            here = slice(index * rows, (index + 1) * rows)
            joined[here, :] = block[:, :depth]
            outer[here, :] = (keep[here, :] * block[:, depth:].astype(f32)).astype(low)
        put_together(bits[place], *skips, held)
        half = width // 2
        for here in (slice(0, half), slice(half, width)):
            hidden[:, here] = dg(joined[...], held[:, :, :, here].reshape(depth, half), 1, 0)

    return line.run(
        kernel,
        [struct((length, width), f32), struct((length, width), low)],
        [*blocks, *pair, keep],
        scratch=[pltpu.VMEM((length, depth), low), together(pair)],
        flops=2 * length * width * depth,
        limit=14,
    )


def half_turn(values):
    lanes = lax.broadcasted_iota(jnp.int32, values.shape, 1) % HEAD_DIM
    width = values.shape[1]
    half = HEAD_DIM // 2
    return jnp.where(
        lanes < half, pltpu.roll(values, width - half, 1), pltpu.roll(values, half, 1)
    )


def shares_of(keys, queries, ok):
    scores = jnp.where(ok > 0, dg(keys, queries, 1, 1), neg_large)
    weights = jnp.exp(scores - jnp.max(scores, axis=0, keepdims=True))
    return weights * (1.0 / jnp.sum(weights, axis=0, keepdims=True))


def attend_piece(normed, qk, vo, cosine, sine, ok, held, mixed):
    inner = qk.shape[1] // 2
    rows = normed.shape[0]
    for part in range(3):
        weight = (qk[:, :inner], qk[:, inner:], vo[:, :inner])[part]
        project = dg(normed[...], weight, 1, 0)
        if part < 2:
            project = project * cosine[...] + half_turn(project) * sine[...]
        if part == 0:
            project = project * HEAD_DIM**-0.5
        held[:, part * inner : (part + 1) * inner] = project.astype(low)
    queries = held[:, :inner]
    keys = held[:, inner : 2 * inner]
    values = held[:, 2 * inner :]
    owner = lax.broadcasted_iota(jnp.int32, (rows, inner), 1) // HEAD_DIM
    zero = jnp.zeros((), low)
    total = None
    for head in range(inner // HEAD_DIM):
        mine = owner == head
        shares = shares_of(keys, jnp.where(mine, queries, zero), ok[...]).astype(low)
        term = dg(shares, jnp.where(mine, values, zero), 0, 0)
        total = term if total is None else total + term
    mixed[...] = total.astype(low)
    return dg(mixed[...], vo[:, inner:], 1, 1).astype(low).astype(f32)


def add_up(total, term, step):
    @pl.when(step == 0)
    def _():
        total[...] = term

    @pl.when(step > 0)
    def _():
        total[...] += term


def attend(line, weights, cosine, sine, ok, hidden, shift, scale, normed=None, before=None):
    rows, width = hidden.shape
    inner = weights.columns // 4
    total = struct((rows, width), f32)
    outs = [struct((2, rows, 3 * inner), low), struct((2, rows, inner), low), total, struct((rows, width), low)]
    plain = [cosine, sine, ok, hidden, shift, scale]
    plain += [] if before is None else [normed, before]
    arrays = weights.arrays

    def kernel(bits, *refs):
        tables, refs = refs[: len(arrays)], refs[len(arrays) :]
        (cosine, sine, ok, hidden, shift, scale, *more), refs = refs[: len(plain)], refs[len(plain) :]
        held, mixed, out, after, *scratch = refs
        step = pl.program_id(0)

        def modulate(values):
            normal, _ = normalise(values)
            after[...] = (normal * (1.0 + scale[...]) + shift[...]).astype(low)

        if not more:

            @pl.when(step == 0)
            def _():
                modulate(hidden[...])

        qk, vo = weights.load(bits, tables, scratch)
        normed = more[0] if more else after
        term = attend_piece(normed, qk, vo, cosine, sine, ok, held, mixed)
        add_up(out, term, step)
        if more:

            @pl.when(step == pl.num_programs(0) - 1)
            def _():
                total = hidden[...] + (more[1][...] + out[...])
                out[...] = total
                modulate(total)

    return line.run(
        kernel,
        outs,
        [*arrays, *plain],
        grid=(2,),
        in_specs=[*weights.specs(), *(whole(value) for value in plain)],
        out_specs=[each(outs[0]), each(outs[1]), whole(total), whole(total)],
        scratch=weights.scratch(),
        flops=2 * rows * (8 * width * inner + 16 * rows * inner),
        limit=20,
    )


def gelu_pair(values):
    root = math.sqrt(2.0 / math.pi)
    cube = 0.044715 * values * values
    slope = jnp.tanh(root * values * (1.0 + cube))
    gate = 0.5 * (1.0 + slope)
    back = gate + 0.5 * values * (1.0 - slope * slope) * root * (1.0 + 3.0 * cube)
    return values * gate, back


def feed(line, normed, outer, weights, halves, before=None):
    rows, width = normed.shape
    half = weights.columns // 2
    end = struct((rows, width), low)
    arrays = weights.arrays
    extra = [] if before is None else [before]

    def kernel(bits, *refs):
        tables, (normed, outer, *refs) = refs[: len(arrays)], refs[len(arrays) :]
        before, refs = refs[: len(extra)], refs[len(extra) :]
        outs, (fed, back, fed_total, back_total, *scratch) = refs[: len(halves.outs)], refs[len(halves.outs) :]
        step = pl.program_id(0)
        now = weights.load(bits, tables, scratch)
        up, down = now[:, :half], now[:, half:]
        value, slope = gelu_pair(dg(normed[...], up, 1, 0))
        gated = value.astype(low)
        lifted = (dg(outer[...], down, 1, 0) * slope).astype(low)
        grad = jnp.concatenate([dg(normed[...], lifted, 0, 0), dg(outer[...], gated, 0, 0)], axis=1)
        halves.store(bits, *(before or (None,)), outs, grad)
        add_up(fed_total, dg(gated, down, 1, 1), step)
        add_up(back_total, dg(lifted, up, 1, 1), step)

        @pl.when(step == pl.num_programs(0) - 1)
        def _():
            fed[...] = fed_total[...].astype(low)
            back[...] = back_total[...].astype(low)

    return line.run(
        kernel,
        [*halves.outs, end, end],
        [*arrays, normed, outer, *extra],
        grid=(2,),
        in_specs=[*weights.specs(), whole(normed), whole(outer), *(each(value) for value in extra)],
        out_specs=[*halves.specs(), whole(end), whole(end)],
        scratch=[pltpu.VMEM((rows, width), f32)] * 2 + weights.scratch(),
        flops=24 * rows * width * half,
        limit=22,
    )


def bend_kernel(middle, outer, keep, scale, *refs):
    *parts, result, middle_grad, middle_low, sums = refs
    count = len(parts) // 2
    fed = sum(part[...].astype(f32) for part in parts[:count])
    grad = sum(part[...].astype(f32) for part in parts[count:])
    result[...] = (keep[...] * (middle[...] + fed)).astype(low)
    normal, inverse = normalise(middle[...])
    total = outer[...].astype(f32) + norm_back(normal, inverse, grad, scale[...])
    middle_grad[...] = total
    middle_low[...] = total.astype(low)
    sums[0:1, :] = jnp.sum(grad, axis=0, keepdims=True)
    sums[1:2, :] = jnp.sum(grad * normal, axis=0, keepdims=True)


def bend(line, middle, outer, keep, scale, fed, back):
    shape = middle.shape
    outs = [struct(shape, low), struct(shape, f32), struct((2, shape[1]), f32), struct(shape, low)]

    def kernel(bits, *refs):
        *refs, sums, middle_low = refs
        bend_kernel(*refs, middle_low, sums)

    return line.run(kernel, outs, [middle, outer, keep, scale, *fed, *back], limit=14)


def back_piece(normed, middle_low, qk, vo, held, mixed, cosine, sine, ok, project):
    inner = qk.shape[1] // 2
    rows = normed.shape[0]
    queries = held[:, :inner]
    keys = held[:, inner : 2 * inner]
    values = held[:, 2 * inner :]
    above = dg(middle_low[...], vo[:, inner:], 1, 0).astype(low)
    owner = lax.broadcasted_iota(jnp.int32, (rows, inner), 1) // HEAD_DIM
    zero = jnp.zeros((), low)
    query_grad = key_grad = value_grad = jnp.zeros((rows, inner), f32)
    for head in range(inner // HEAD_DIM):
        mine = owner == head
        queries_here = jnp.where(mine, queries, zero)
        above_here = jnp.where(mine, above, zero)
        shares = shares_of(keys, queries_here, ok[...])
        share_grad = dg(values, above_here, 1, 1)
        inside = jnp.sum(share_grad * shares, axis=0, keepdims=True)
        score_grad = (shares * (share_grad - inside)).astype(low)
        value_grad += dg(shares.astype(low), above_here, 1, 0)
        key_grad += dg(score_grad, queries_here, 1, 0)
        query_grad += dg(score_grad, jnp.where(mine, keys, zero), 0, 0)
    query_grad = query_grad * HEAD_DIM**-0.5
    for place, grad in enumerate((query_grad, key_grad)):
        turned = grad * cosine[...] - half_turn(grad) * sine[...]
        project[:, place * inner : (place + 1) * inner] = turned.astype(low)
    project[:, 2 * inner :] = value_grad.astype(low)
    qk_grad = dg(normed[...], project[:, : 2 * inner], 0, 0)
    vo_grad = jnp.concatenate(
        [dg(normed[...], project[:, 2 * inner :], 0, 0), dg(middle_low[...], mixed[...], 0, 0)], axis=1
    )
    term = dg(project[:, : 2 * inner], qk, 1, 1)
    term += dg(project[:, 2 * inner :], vo[:, :inner], 1, 1)
    return qk_grad, vo_grad, term.astype(low).astype(f32)


def attend_back(line, normed, middle_low, weights, held, mixed, cosine, sine, ok, parts, before=None, last=()):
    rows, width = normed.shape
    inner = weights.columns // 4
    arrays = weights.arrays
    plain = [normed, middle_low, held, mixed, cosine, sine, ok, *last]
    extra = [] if before is None else [before]
    scratch = [pltpu.VMEM((rows, 3 * inner), low), *weights.scratch()]
    if last:
        ends = [struct((2, width), f32), struct((rows, width), low)]
        scratch = [pltpu.VMEM((rows, width), f32)] + scratch
    else:
        ends = [struct((rows, width), f32)]

    def kernel(bits, *refs):
        tables, refs = refs[: len(arrays)], refs[len(arrays) :]
        (*args, cosine, sine, ok), refs = refs[:7], refs[7:]
        more, refs = refs[: len(last)], refs[len(last) :]
        before, refs = refs[: len(extra)], refs[len(extra) :]
        outs = []
        for part in parts:
            outs.append(refs[: len(part.outs)])
            refs = refs[len(part.outs) :]
        marks, (total, project, *scratch) = (refs[:2], refs[2:]) if last else ((), refs)
        step = pl.program_id(0)
        normed, middle_low, held, mixed = args
        qk, vo = weights.load(bits, tables, scratch)
        *grads, term = back_piece(
            normed, middle_low, qk, vo, held, mixed, cosine, sine, ok, project
        )
        if len(parts) == 1:
            grads = [jnp.concatenate(grads, axis=1)]
        for part, out, grad in zip(parts, outs, grads):
            part.store(bits, *(before or (None,)), out, grad)
        add_up(total, term, step)
        if last:
            ahead, hidden, middle_grad, scale = more
            sums, hidden_low = marks

            @pl.when(step == pl.num_programs(0) - 1)
            def _():
                grad = ahead[...] + total[...]
                normal, inverse = normalise(hidden[...])
                hidden_low[...] = (
                    middle_grad[...] + norm_back(normal, inverse, grad, scale[...])
                ).astype(low)
                sums[0:1, :] = jnp.sum(grad, axis=0, keepdims=True)
                sums[1:2, :] = jnp.sum(grad * normal, axis=0, keepdims=True)

    outs = [value for part in parts for value in part.outs]
    return line.run(
        kernel,
        [*outs, *ends],
        [*arrays, *plain, *extra],
        grid=(2,),
        in_specs=[
            *weights.specs(),
            *(each(value) if value.ndim == 3 else whole(value) for value in plain),
            *(each(value) for value in extra),
        ],
        out_specs=[spec for part in parts for spec in part.specs()] + [whole(value) for value in ends],
        scratch=scratch,
        flops=2 * rows * (16 * width * inner + 40 * rows * inner),
        limit=24,
    )


def leave(line, blocks, hidden_low, place, parts):
    count = len(blocks)
    length, width = hidden_low.shape
    depth = 2 * width

    def kernel(bits, *refs):
        blocks, hidden_low, sent, kept, joined = refs[:count], *refs[count:]
        rows = blocks[0].shape[0]
        for index, block in enumerate(blocks):
            joined[index * rows : (index + 1) * rows, :] = block[:, :depth]
        mine = bits[place] == 1
        half = width // 2
        for here in (slice(0, half), slice(half, width)):
            total = dg(joined[...], hidden_low[:, here], 0, 0)
            total = total.reshape(sent.shape[0], 2, -1, half)
            sent[:, :, here] = jnp.where(mine, total[:, 0], total[:, 1]).astype(low)
            kept[:, :, here] = jnp.where(mine, total[:, 1], total[:, 0]).astype(low)

    return line.run(
        kernel,
        [struct((parts // 2, depth // parts, width), low)] * 2,
        [*blocks, hidden_low],
        scratch=[pltpu.VMEM((length, depth), low)],
        flops=2 * length * width * depth,
        limit=16,
    )


def inputs_back(line, blocks, results, pair, place):
    count = len(blocks)
    length, width = sum(block.shape[0] for block in blocks), blocks[0].shape[1]

    def kernel(bits, *refs):
        blocks, results, skips = refs[:count], refs[count : 2 * count], refs[2 * count : 2 * count + 2]
        frame_grad, skip_grad, result, hidden, held = refs[2 * count + 2 :]
        rows = blocks[0].shape[0]
        for index in range(count):
            start = pl.multiple_of((bits[1] ^ index) * rows, rows)
            hidden[pl.ds(start, rows), :] = blocks[index][...]
            result[pl.ds(start, rows), :] = results[index][...]
        skip = put_together(bits[place], *skips, held)
        frame_grad[...] = dg(hidden[...], skip[:width], 1, 1)
        skip_grad[...] = dg(hidden[...], skip[width:], 1, 1)

    return line.run(
        kernel,
        [struct((length, width), f32)] * 2 + [struct((length, width), low)],
        [*blocks, *results, *pair],
        scratch=[pltpu.VMEM((length, width), low), together(pair)],
        flops=4 * length * width * width,
        limit=14,
    )


def adam_update(master, first, second, grad, rate):
    first_new = beta_first * first + (1.0 - beta_first) * grad
    second_new = beta_second * second + (1.0 - beta_second) * grad * grad
    first_hat = first_new / (1.0 - beta_first**STEP)
    second_hat = second_new / (1.0 - beta_second**STEP)
    master_new = master - rate * (
        first_hat / (jnp.sqrt(second_hat) + adam_eps) + decay_rate * master
    )
    return (first_new, second_new, master_new, master_new.astype(low))


def added(pair):
    return pair[0][...].astype(f32) + pair[1][...].astype(f32)


def store_update(states, grad, rate, outs):
    for out, value in zip(outs, adam_update(*(state[...] for state in states), grad, rate)):
        out[...] = value


def update_outs(master):
    return [struct(master.shape, f32)] * 3 + [struct(master.shape, low)]


def update_feed(line, first, second, ups, downs):
    def kernel(bits, *refs):
        pairs, ups, downs = (refs[:2], refs[2:4]), refs[4:7], refs[7:10]
        up_outs, down_outs = refs[10:14], refs[14:18]
        totals = [added(pair) for pair in pairs]
        half = totals[0].shape[1] // 2
        store_update(ups, jnp.concatenate([total[:, :half] for total in totals], axis=1), rates[4], up_outs)
        store_update(
            downs, jnp.concatenate([total[:, half:].T for total in totals], axis=0), rates[5], down_outs
        )

    return line.run(kernel, update_outs(ups[0]) + update_outs(downs[0]), [*first, *second, *ups, *downs], limit=10)


def update_attention(line, qk, vo, inputs, outputs):
    def kernel(bits, *refs):
        qk, vo, inputs, outputs = refs[:2], refs[2:4], refs[4:7], refs[7:10]
        input_outs, output_outs = refs[10:14], refs[14:18]
        qk, vo = added(qk), added(vo)
        inner = qk.shape[1] // 2
        for place, grad in enumerate((qk[:, :inner], qk[:, inner:], vo[:, :inner])):
            store_update(
                [state.at[place] for state in inputs], grad, rates[2], [out.at[place] for out in input_outs]
            )
        store_update(outputs, vo[:, inner:].T, rates[3], output_outs)

    return line.run(kernel, update_outs(inputs[0]) + update_outs(outputs[0]), [*qk, *vo, *inputs, *outputs], limit=10)


def update_skip(line, pair, skips):
    def kernel(bits, *refs):
        store_update(refs[2:5], added(refs[:2]), rates[0], refs[5:9])

    return line.run(kernel, update_outs(skips[0]), [*pair, *skips], limit=8)


def orders():
    dp_bits, tensor_bits = bits_of("dp"), bits_of(TENSOR)
    far = [("dp", mask) for mask in dp_bits[:-2]]
    y, z = ("dp", dp_bits[-1]), ("dp", dp_bits[-2])
    x = (TENSOR, tensor_bits[0])
    return {
        "xzy": far + [x, z, y],
        "yzx": far + [y, z, x],
        "zxy": far + [z, x, y],
        "zyx": far + [z, y, x],
        "yxz": far + [y, x, z],
        "xyz": far + [x, y, z],
    }


def body(
    frames,
    skip_frames,
    time_embed,
    lengths,
    out_grad,
    skip_weight,
    adapt_weight,
    input_weight,
    output_weight,
    up_weight,
    down_weight,
    skip_first,
    adapt_first,
    input_first,
    output_first,
    up_first,
    down_first,
    skip_second,
    adapt_second,
    input_second,
    output_second,
    up_second,
    down_second,
):
    micro, _, rows, width = frames.shape
    parts = lax.axis_size(TENSOR)
    groups = lax.axis_size("dp")
    me = lax.axis_index(TENSOR)
    inner = input_weight.shape[2]
    heads = inner // HEAD_DIM
    highest = lax.Precision.HIGHEST
    order = orders()
    skip_order, skip_back_order = order["xyz"], order["yzx"]
    attention_orders, attention_back_orders = (order["xyz"], order["xzy"]), (order["xyz"], order["zxy"])
    feed_orders, feed_back_orders = (order["yzx"], order["zxy"]), (order["zxy"], order["xyz"])
    core = (TENSOR, bits_of(TENSOR)[-1])
    across = (TENSOR, bits_of(TENSOR)[0])
    dims = [across] + [("dp", mask) for mask in bits_of("dp")]
    all_dims = dims[1:] + [across, core]
    line = Line()

    adapt_low = adapt_weight.astype(low)
    time_values = time_embed[:, 0, :].astype(f32)
    time_low = jax.nn.silu(time_values).astype(low)

    def modulation():
        dp_bits = bits_of("dp")
        time_all = unflip(time_low, 0, TENSOR).reshape((1,) * len(dp_bits) + time_low.shape)
        for dim, mask in enumerate(dp_bits):
            time_all = line.tie(time_all)
            time_all = jnp.concatenate([time_all, swap(time_all, "dp", mask)], axis=dim)
            line.need(time_all)
            yield None
        time_rows = time_all.reshape(groups * micro, width)
        adapt_mine = jnp.dot(time_rows, adapt_low, preferred_element_type=f32).reshape(groups, micro, -1)
        for adapt_all in exchange_steps(line, adapt_mine, needed=True):
            yield time_rows, adapt_all

    modulate = modulation()

    row_index = jnp.concatenate(
        [(me ^ step) * rows + jnp.arange(rows, dtype=jnp.int32) for step in range(parts)]
    )
    length = pick(lengths, me, 0)[0]
    keep = (row_index < length).astype(f32)[:, None]
    half = HEAD_DIM // 2
    frequency = 10000.0 ** (-jnp.arange(half).astype(f32) / half)
    angles = row_index.astype(f32)[:, None] * frequency[None, :]
    cosine = jnp.tile(jnp.cos(angles), (1, 2 * heads))
    sine = jnp.tile(jnp.concatenate([-jnp.sin(angles), jnp.sin(angles)], axis=1), (1, heads))

    next(modulate)
    skip_shard, qk_shard, vo_shard, *feed_shards = pack(
        line, skip_weight, input_weight.transpose(1, 0, 2), output_weight, up_weight, down_weight
    )
    skip_walk = Gather(line, skip_shard, skip_order + [core], all_dims, ())
    attention_walks = [
        Gather(line, shard, each_order, dims, (across,))
        for shard, each_order in zip((qk_shard, vo_shard), attention_orders)
    ]
    next(modulate)
    blocks = list(cut(line, (frames, skip_frames, out_grad)))
    feed_walks = [
        Gather(line, shard, each_order, dims, (across,))
        for shard, each_order in zip(feed_shards, feed_orders)
    ]
    next(modulate)
    more = range(len(bits_of("dp")) - 3)
    for _ in more:
        go(line, skip_walk)
        go(line, *attention_walks)
        go(line, *feed_walks)
    line.need(cosine, sine, keep)
    go(line, skip_walk)
    next(modulate)
    go(line, *attention_walks)
    blocks[2] = swap(line.tie(blocks[2]), TENSOR, 2)
    next(modulate)
    go(line, skip_walk)
    next(modulate)
    go(line, *attention_walks)
    next(modulate)
    go(line, *feed_walks)
    for time_rows, adapt_all in modulate:
        pass
    blocks[3] = swap(line.tie(blocks[3]), TENSOR, 3)
    go(line, skip_walk)
    go(line, *feed_walks)
    adapt_vector = unflip(unflip(adapt_all, 0, "dp"), 1, TENSOR).reshape(1, -1)
    shift_one, scale_one, shift_two, scale_two = jnp.split(adapt_vector, 4, axis=1)
    line.need(blocks[2])
    go(line, *attention_walks)
    blocks[1] = swap(line.tie(blocks[1]), TENSOR, 1)
    line.need(blocks[3])
    go(line, skip_walk)
    skip_pair = skip_walk.pair()
    hidden, outer = enter(line, blocks, skip_pair, line.place[core], keep)
    go(line, *feed_walks)
    attention_own = Both(*(Pieces(line, walk, across) for walk in attention_walks))
    held_own, mixed_own, attended, normed_one = attend(
        line, attention_own, cosine, sine, keep, hidden, shift_one, scale_one
    )
    attention_other = attention_own.flip(core)
    held_other, mixed_other, middle, normed_two = attend(
        line, attention_other, cosine, sine, keep, hidden, shift_two, scale_two, normed=normed_one, before=attended
    )
    fed, back, feed_arrived, feed_scatters = [], [], [], []
    feed_own = [Pieces(line, walk, across) for walk in feed_walks]
    columns = feed_shards[0].shape[1]
    feed_other = [pieces.flip(core, tied=True) for pieces in feed_own]
    for pieces in feed_other:
        grad, *ends = feed(line, normed_two, outer, pieces, Halves(line, width, columns))
        feed_arrived.append(swap(grad, *core))
        fed.append(ends[0])
        back.append(ends[1])
    for pieces, arrived, each_order in zip(feed_own, feed_arrived, feed_back_orders):
        halves = Halves(line, width, columns, each_order[-1], dims, arrived)
        kept, sent, *ends = feed(line, normed_two, outer, pieces, halves, arrived)
        feed_scatters.append(Scatter(line, kept, sent, each_order[::-1], dims, (across,)))
        fed.append(ends[0])
        back.append(ends[1])
    feed_one, feed_two = feed_scatters
    result, middle_grad, sums_two, middle_low = bend(line, middle, outer, keep, scale_two, fed, back)
    results = from_owner([result[step * rows : (step + 1) * rows] for step in range(parts)])
    qk_other, vo_other, ahead = attend_back(
        line,
        normed_one,
        middle_low,
        attention_other,
        held_other,
        mixed_other,
        cosine,
        sine,
        keep,
        [Halves(line, width, 2 * inner)] * 2,
    )
    attention_arrived = [swap(grad, *core) for grad in (qk_other, vo_other)]
    line.need(*results[1:])
    qk_grad, vo_grad, sums_one, hidden_low = attend_back(
        line,
        normed_one,
        middle_low,
        attention_own,
        held_own,
        mixed_own,
        cosine,
        sine,
        keep,
        [Halves(line, width, 2 * inner)] * 2,
        last=(ahead, hidden, middle_grad, scale_one),
    )
    attention_scatters = [
        Scatter(line, grad, None, [core] + each_order[::-1], dims, (across,), arrived)
        for grad, arrived, each_order in zip((qk_grad, vo_grad), attention_arrived, attention_back_orders)
    ]
    go(line, feed_one, feed_two)
    skip_sent, skip_kept = leave(line, blocks, hidden_low, line.place[core], groups * parts)
    skip_scatter = Scatter(line, skip_kept, skip_sent, [core] + skip_back_order[::-1], all_dims, ())
    hidden_back = from_owner([hidden_low[step * rows : (step + 1) * rows] for step in range(parts)])

    def modulation_back():
        adapt_back = jnp.concatenate([sums_one.reshape(-1), sums_two.reshape(-1)]).reshape(
            groups, parts, -1
        )
        for adapt_rows in exchange_steps(line, unflip(unflip(adapt_back, 0, "dp"), 1, TENSOR)):
            yield None
        adapt_rows = adapt_rows.reshape(groups * micro, -1)
        adapt_sum = lax.dot_general(
            time_rows.astype(f32), adapt_rows, (((0,), (0,)), ((), ())), precision=highest
        )
        time_part = lax.dot_general(
            adapt_rows, adapt_low.astype(f32), (((1,), (1,)), ((), ())), precision=highest
        ).reshape(groups, micro, width)
        for mask in bits_of("dp"):
            time_part = line.tie(time_part)
            time_part = time_part[:mask] + swap(time_part[mask:], "dp", mask)
            yield None
        time_part = unflip(time_part[0], 0, TENSOR)
        for mask in bits_of(TENSOR):
            time_part = line.tie(time_part)
            time_part = time_part + swap(time_part, TENSOR, mask)
            yield None
        yield adapt_sum, time_part

    modulate_back = modulation_back()
    go(line, *attention_scatters)
    go(line, skip_scatter)
    next(modulate_back)
    go(line, feed_one, feed_two)
    next(modulate_back)
    go(line, *attention_scatters)
    next(modulate_back)
    go(line, skip_scatter)
    next(modulate_back)
    go(line, feed_one, feed_two)
    next(modulate_back)
    go(line, *attention_scatters)
    next(modulate_back)
    go(line, skip_scatter)
    next(modulate_back)
    go(line, *attention_scatters)
    go(line, skip_scatter)
    next(modulate_back)
    frame_grads, skip_grads, results = inputs_back(
        line, hidden_back, results, skip_pair, line.place[core]
    )
    frame_grads, skip_grads = frame_grads.reshape(frames.shape), skip_grads.reshape(frames.shape)
    for _ in more:
        go(line, feed_one, feed_two)
        go(line, *attention_scatters)
        go(line, skip_scatter)
    next(modulate_back)
    line.need(*(walk.terms[1] for walk in attention_scatters))
    feed_new = update_feed(
        line,
        feed_one.terms,
        feed_two.terms,
        (up_weight, up_first, up_second),
        (down_weight, down_first, down_second),
    )
    for ends in modulate_back:
        pass
    adapt_sum, time_part = ends
    sigmoid = jax.nn.sigmoid(time_values)
    time_grad = time_part * (sigmoid * (1.0 + time_values * (1.0 - sigmoid)))
    attention_new = update_attention(
        line,
        attention_scatters[0].terms,
        attention_scatters[1].terms,
        [state.transpose(1, 0, 2) for state in (input_weight, input_first, input_second)],
        (output_weight, output_first, output_second),
    )
    skip_new = update_skip(line, skip_scatter.terms, (skip_weight, skip_first, skip_second))
    adapt_new = adam_update(adapt_weight, adapt_first, adapt_second, adapt_sum, rates[1])
    return (
        results.reshape(frames.shape),
        frame_grads,
        skip_grads,
        time_grad[:, None, :],
        *skip_new,
        *adapt_new,
        *(value.transpose(1, 0, 2) for value in attention_new[:4]),
        *attention_new[4:],
        *feed_new,
    )


def solution(mesh):
    groups, parts = mesh.devices.shape
    split_mesh = Mesh(mesh.devices.reshape(groups, parts // 2, 2), ("dp", *TENSOR))
    return jax.shard_map(
        body,
        mesh=split_mesh,
        in_specs=(
            P(None, "dp", TENSOR, None),
            P(None, "dp", TENSOR, None),
            P(None, "dp", None),
            P(None, "dp"),
            P(None, "dp", TENSOR, None),
            P(("dp", *TENSOR), None),
            P(None, ("dp", *TENSOR)),
            P("dp", None, TENSOR),
            P(TENSOR, "dp"),
            P("dp", TENSOR),
            P(TENSOR, "dp"),
            P(("dp", *TENSOR), None),
            P(None, ("dp", *TENSOR)),
            P("dp", None, TENSOR),
            P(TENSOR, "dp"),
            P("dp", TENSOR),
            P(TENSOR, "dp"),
            P(("dp", *TENSOR), None),
            P(None, ("dp", *TENSOR)),
            P("dp", None, TENSOR),
            P(TENSOR, "dp"),
            P("dp", TENSOR),
            P(TENSOR, "dp"),
        ),
        out_specs=(
            P(None, "dp", TENSOR, None),
            P(None, "dp", TENSOR, None),
            P(None, "dp", TENSOR, None),
            P(None, "dp", None),
            P(("dp", *TENSOR), None),
            P(("dp", *TENSOR), None),
            P(("dp", *TENSOR), None),
            P(("dp", *TENSOR), None),
            P(None, ("dp", *TENSOR)),
            P(None, ("dp", *TENSOR)),
            P(None, ("dp", *TENSOR)),
            P(None, ("dp", *TENSOR)),
            P("dp", None, TENSOR),
            P("dp", None, TENSOR),
            P("dp", None, TENSOR),
            P("dp", None, TENSOR),
            P(TENSOR, "dp"),
            P(TENSOR, "dp"),
            P(TENSOR, "dp"),
            P(TENSOR, "dp"),
            P("dp", TENSOR),
            P("dp", TENSOR),
            P("dp", TENSOR),
            P("dp", TENSOR),
            P(TENSOR, "dp"),
            P(TENSOR, "dp"),
            P(TENSOR, "dp"),
            P(TENSOR, "dp"),
        ),
        check_vma=False,
    )
```

```python
import functools
import math

import jax
import jax.numpy as jnp
from jax import lax
from jax.experimental import pallas as pl
from jax.experimental.pallas import tpu as pltpu
from jax.sharding import Mesh
from jax.sharding import PartitionSpec as P

HEAD_DIM = 64
TENSOR = ("high", "low")
STEP = 10
MEBI = 1 << 20

norm_eps = 1e-06
neg_large = -1e30
rates = (0.04, 0.06, 0.06, 0.6, 0.06, 0.03)
beta_first = 0.9
beta_second = 0.999
decay_rate = 0.01
adam_eps = 1e-08
low = jnp.bfloat16
f32 = jnp.float32


def bits_of(axis):
    count = lax.axis_size(axis).bit_length() - 1
    return [1 << place for place in reversed(range(count))]


def my_bit(axis, mask):
    return (lax.axis_index(axis) // mask) % 2


def swap(values, axis, mask):
    count = lax.axis_size(axis)
    return lax.ppermute(values, axis, [(i, i ^ mask) for i in range(count)])


def pick(values, index, dim):
    return lax.dynamic_index_in_dim(values, index, dim, keepdims=False)


def struct(shape, dtype):
    return jax.ShapeDtypeStruct(shape, dtype)


class Whole:
    def __init__(self, array, each=False):
        self.each = each


def whole(array):
    return Whole(array)


def each(array):
    return Whole(array, each=True)


class Line:
    def __init__(self):
        self.last = ()
        steps = [("dp", mask) for mask in bits_of("dp")] + [(TENSOR, mask) for mask in bits_of(TENSOR)]
        self.place = {step: 2 + place for place, step in enumerate(steps)}
        me = lax.axis_index(TENSOR)
        self.bits = jnp.stack([jnp.zeros((), me.dtype), me] + [my_bit(*step) for step in steps])

    def run(self, kernel, outs, ins, *, grid=(1,), in_specs=None, out_specs=None, scratch=(), flops=0, limit=14):
        in_specs = [Whole(value) for value in ins] if in_specs is None else in_specs
        out_specs = [Whole(value) for value in outs] if out_specs is None else out_specs
        marks = [isinstance(spec, Whole) and spec.each for spec in (*in_specs, *out_specs)]
        in_specs, out_specs = (
            [pl.BlockSpec(memory_space=pltpu.VMEM) if isinstance(spec, Whole) else spec for spec in specs]
            for specs in (in_specs, out_specs)
        )
        deps = self.last
        skip = 1 + len(ins)

        def inner(*refs):
            bits, *refs = (*refs[:skip], *refs[skip + len(deps) :])
            parts = [ref.at[pl.program_id(0)] if mark else ref for ref, mark in zip(refs, marks)]
            kernel(bits, *parts, *refs[len(marks) :])

        moved = sum(value.size * value.dtype.itemsize for value in (*ins, *outs))
        results = pl.pallas_call(
            inner,
            grid_spec=pltpu.PrefetchScalarGridSpec(
                num_scalar_prefetch=1,
                grid=grid,
                in_specs=in_specs + [pl.BlockSpec(memory_space=pl.ANY)] * len(deps),
                out_specs=out_specs,
                scratch_shapes=list(scratch),
            ),
            out_shape=list(outs),
            cost_estimate=pl.CostEstimate(flops=flops, bytes_accessed=moved, transcendentals=0),
            compiler_params=pltpu.CompilerParams(vmem_limit_bytes=limit * MEBI),
        )(self.bits, *ins, *deps)
        self.last = (results[-1],)
        return results

    def need(self, *values):
        self.last += values

    def tie(self, values):
        return lax.optimization_barrier((values, self.last))[0]


def merge(line, pairs, places):
    count = len(pairs)

    def kernel(bits, *refs):
        for place in range(count):
            (mine, other), out = refs[2 * place : 2 * place + 2], refs[2 * count + place]
            bit = bits[places[place]]
            out[:, pl.ds(bit, 1)] = mine[...][:, None]
            out[:, pl.ds(1 - bit, 1)] = other[...][:, None]

    outs = [struct((mine.shape[0], 2) + mine.shape[1:], low) for mine, _ in pairs]
    return line.run(kernel, outs, [value for pair in pairs for value in pair])


def split(line, pairs, places):
    count = len(pairs)

    def kernel(bits, *refs):
        for place in range(count):
            terms, outs = refs[2 * place : 2 * place + 2], refs[2 * (count + place) : 2 * (count + place) + 2]
            bit = bits[places[place]]
            for index, out in zip((1 - bit, bit), outs):
                total = sum(term[:, pl.ds(index, 1)].astype(f32) for term in terms)
                out[...] = total[:, 0].astype(low)

    outs = [struct(pair[0].shape[:1] + pair[0].shape[2:], low) for pair in pairs for _ in range(2)]
    results = line.run(kernel, outs, [value for pair in pairs for value in pair])
    return list(zip(results[::2], results[1::2]))


class Gather:
    def __init__(self, line, shard, order, dims, relative):
        self.line, self.order, self.dims, self.relative = line, list(order), dims, relative
        self.sizes = {dim: 1 for dim in dims}
        self.columns = shard.shape[1]
        self.mine = line.tie(shard)
        self.begin()

    def begin(self):
        self.step = self.order.pop(0)
        self.arrived = swap(self.mine, *self.step)

    def pair(self):
        place = self.dims.index(self.step)
        outer = math.prod(self.sizes[dim] for dim in self.dims[:place])
        shape = (outer, -1, self.columns)
        return self.mine.reshape(shape), self.arrived.reshape(shape)

    def end(self, piece):
        self.mine = piece.reshape(-1, self.columns)
        self.sizes[self.step] = 2
        self.begin()


class Scatter:
    def __init__(self, line, kept, sent, order, dims, relative, arrived=None):
        self.line, self.order, self.dims, self.relative = line, list(order), dims, relative
        self.sizes = {dim: 2 if dim in self.order else 1 for dim in dims}
        self.columns = kept.shape[-1]
        self.begin(kept, sent, arrived)

    def begin(self, kept, sent, arrived=None):
        self.step = self.order.pop(0)
        self.sizes[self.step] = 1
        flat = (-1, self.columns)
        if arrived is None:
            arrived = swap(sent.reshape(flat), *self.step)
        self.terms = [kept.reshape(flat), arrived.reshape(flat)]

    def pair(self):
        place = self.dims.index(self.order[0])
        outer = math.prod(self.sizes[dim] for dim in self.dims[:place])
        return [term.reshape(outer, 2, -1, self.columns) for term in self.terms]

    def end(self, halves):
        sent, kept = halves
        self.begin(kept, sent)


def go(line, *walks):
    gathers = isinstance(walks[0], Gather)
    steps = [walk.step if gathers else walk.order[0] for walk in walks]
    places = [0 if step in walk.relative else line.place[step] for step, walk in zip(steps, walks)]
    results = (merge if gathers else split)(line, [walk.pair() for walk in walks], places)
    for walk, result in zip(walks, results):
        walk.end(result)


class Pieces:
    def __init__(self, line, walk, across, arrays=None):
        self.line, self.walk, self.across = line, walk, walk.step == across
        self.columns = walk.columns
        self.arrays = arrays
        if arrays is None:
            self.arrays = list(walk.pair())
            if not self.across:
                self.arrays = [value.reshape((2, -1) + value.shape[1:]) for value in self.arrays]

    def flip(self, core, tied=False):
        across = (TENSOR, bits_of(TENSOR)[0])
        arrays = self.line.tie(self.arrays) if tied else self.arrays
        return Pieces(self.line, self.walk, across, [swap(value, *core) for value in arrays])

    def specs(self):
        return [whole(value) if self.across else each(value) for value in self.arrays]

    def scratch(self):
        shape = self.arrays[0].shape[1:]
        return [pltpu.VMEM((1,) + shape if self.across else (shape[0], 2) + shape[1:], low)]

    def load(self, bits, refs, held):
        mine, arrived = refs
        if self.across:
            step = pl.program_id(0)

            @pl.when(step == 0)
            def _():
                held[0][...] = mine[...]

            @pl.when(step > 0)
            def _():
                held[0][...] = arrived[...]

            return held[0][...].reshape(-1, self.columns)
        return put_together(bits[self.line.place[self.walk.step]], mine, arrived, held[0])


class Both:
    def __init__(self, first, second):
        self.parts = first, second
        self.arrays = first.arrays + second.arrays
        self.columns = first.columns + second.columns

    def flip(self, core):
        return Both(*(part.flip(core) for part in self.parts))

    def specs(self):
        return [spec for part in self.parts for spec in part.specs()]

    def scratch(self):
        return [space for part in self.parts for space in part.scratch()]

    def load(self, bits, refs, held):
        first, second = self.parts
        return first.load(bits, refs[:2], held[:1]), second.load(bits, refs[2:], held[1:])


class Halves:
    def __init__(self, line, width, columns, step=None, dims=(), arrived=None, start=0):
        self.line, self.step, self.arrived, self.start, self.columns = line, step, arrived, start, columns
        self.across = step is not None and step == dims[0]
        if step is None:
            self.outs = [struct((2, width, columns), low)]
        elif self.across:
            self.outs = [struct((width, columns), low)] * 2
        else:
            outer = 1 << (dims.index(step) - 1)
            self.outs = [struct((2, outer, width // (2 * outer), columns), low)] * 2

    def specs(self):
        return [whole(value) if self.across else each(value) for value in self.outs]

    def store(self, bits, before, outs, total):
        if self.step is None:
            outs[0][...] = total.astype(low)
            return
        kept, sent = outs
        arrived = before[:, self.start : self.start + self.columns]
        total = (total + arrived.astype(f32)).astype(low)
        if self.across:
            step = pl.program_id(0)

            @pl.when(step == 0)
            def _():
                kept[...] = total

            @pl.when(step > 0)
            def _():
                sent[...] = total

        else:
            mine = bits[self.line.place[self.step]] == 1
            total = total.reshape(kept.shape[0], 2, *kept.shape[1:])
            kept[...] = jnp.where(mine, total[:, 1], total[:, 0])
            sent[...] = jnp.where(mine, total[:, 0], total[:, 1])


def from_owner(blocks):
    return [block if step == 0 else swap(block, TENSOR, step) for step, block in enumerate(blocks)]


def unflip(values, dim, axis):
    masks = bits_of(axis)
    shape = values.shape
    values = values.reshape(shape[:dim] + (2,) * len(masks) + shape[dim + 1 :])
    for place, mask in enumerate(masks):
        values = jnp.where(
            my_bit(axis, mask) == 1, jnp.flip(values, dim + place), values
        )
    return values.reshape(shape)


def exchange_steps(line, values, needed=False):
    shape = values.shape
    dims = [("dp", mask) for mask in bits_of("dp")]
    dims += [(TENSOR, mask) for mask in bits_of(TENSOR)]
    values = values.reshape((2,) * len(dims) + shape[2:])
    turns = list(range(len(dims)))
    if not needed:
        turns = turns[-1:] + turns[-3:-1][::-1] + turns[:-3]
        turns = turns[:1] + turns[2:] + turns[1:2]
    for dim, (axis, mask) in [(dim, dims[dim]) for dim in turns]:
        values = line.tie(values)
        kept = lax.slice_in_dim(values, 0, 1, axis=dim)
        arrived = swap(lax.slice_in_dim(values, 1, 2, axis=dim), axis, mask)
        values = jnp.concatenate([kept, arrived], axis=dim)
        if needed:
            line.need(values)
        yield None
    yield values.reshape(shape)


def mean_last(values):
    return jnp.mean(values, axis=-1, keepdims=True)


def normalise(values):
    center = values - mean_last(values)
    inverse = lax.rsqrt(mean_last(center * center) + norm_eps)
    return center * inverse, inverse


def norm_back(normal, inverse, grad, scale):
    scaled = grad * (1.0 + scale)
    return inverse * (scaled - mean_last(scaled) - normal * mean_last(scaled * normal))


def dg(left, right, left_dim, right_dim):
    return lax.dot_general(
        left, right, (((left_dim,), (right_dim,)), ((), ())), preferred_element_type=f32
    )


def pack(line, skip, inputs, output, up, down):
    inner, block = inputs.shape[2], up.shape[1] // 2

    def kernel(bits, skip, inputs, output, up, down, skip_out, qk, vo, *feeds):
        skip_out[...] = skip[...].astype(low)
        qk[:, :inner] = inputs[0].astype(low)
        qk[:, inner:] = inputs[1].astype(low)
        vo[:, :inner] = inputs[2].astype(low)
        vo[:, inner:] = output[...].T.astype(low)
        for place, out in enumerate(feeds):
            here = slice(place * block, (place + 1) * block)
            out[:, :block] = up[:, here].astype(low)
            out[:, block:] = down[here, :].T.astype(low)

    outs = [struct(skip.shape, low)] + [struct((inputs.shape[1], 2 * inner), low)] * 2 + [struct(up.shape, low)] * 2
    return line.run(kernel, outs, [skip, inputs, output, up, down])


def cut(line, arrays):
    count, _, rows, width = arrays[0].shape

    def kernel(bits, *refs):
        for place in range(count):

            @pl.when(pl.program_id(0) == place)
            def _():
                for index in range(len(arrays)):
                    here = slice(index * width, (index + 1) * width)
                    refs[len(arrays) + place][:, here] = refs[index][0, 0]

    out = struct((rows, len(arrays) * width), low)
    return line.run(
        kernel,
        [out] * count,
        list(arrays),
        grid=(count,),
        in_specs=[pl.BlockSpec((1, 1, rows, width), lambda i, bits: (bits[1] ^ i, 0, 0, 0))] * len(arrays),
    )


def put_together(bit, mine, arrived, held):
    held[:, pl.ds(bit, 1)] = mine[...][:, None]
    held[:, pl.ds(1 - bit, 1)] = arrived[...][:, None]
    return held[...].reshape(-1, held.shape[-1])


def together(pair):
    return pltpu.VMEM((pair[0].shape[0], 2) + pair[0].shape[1:], low)


def enter(line, blocks, pair, place, keep):
    count = len(blocks)
    length, width = sum(block.shape[0] for block in blocks), pair[0].shape[-1]
    depth = 2 * width

    def kernel(bits, *refs):
        blocks, skips, keep = refs[:count], refs[count : count + 2], refs[count + 2]
        hidden, outer, joined, held = refs[count + 3 :]
        rows = blocks[0].shape[0]
        for index, block in enumerate(blocks):
            here = slice(index * rows, (index + 1) * rows)
            joined[here, :] = block[:, :depth]
            outer[here, :] = (keep[here, :] * block[:, depth:].astype(f32)).astype(low)
        put_together(bits[place], *skips, held)
        half = width // 2
        for here in (slice(0, half), slice(half, width)):
            hidden[:, here] = dg(joined[...], held[:, :, :, here].reshape(depth, half), 1, 0)

    return line.run(
        kernel,
        [struct((length, width), f32), struct((length, width), low)],
        [*blocks, *pair, keep],
        scratch=[pltpu.VMEM((length, depth), low), together(pair)],
        flops=2 * length * width * depth,
        limit=14,
    )


def half_turn(values):
    lanes = lax.broadcasted_iota(jnp.int32, values.shape, 1) % HEAD_DIM
    width = values.shape[1]
    half = HEAD_DIM // 2
    return jnp.where(
        lanes < half, pltpu.roll(values, width - half, 1), pltpu.roll(values, half, 1)
    )


def shares_of(keys, queries, ok):
    scores = jnp.where(ok > 0, dg(keys, queries, 1, 1), neg_large)
    weights = jnp.exp(scores - jnp.max(scores, axis=0, keepdims=True))
    return weights * (1.0 / jnp.sum(weights, axis=0, keepdims=True))


def attend_piece(normed, qk, vo, cosine, sine, ok, held, mixed):
    inner = qk.shape[1] // 2
    rows = normed.shape[0]
    for part in range(3):
        weight = (qk[:, :inner], qk[:, inner:], vo[:, :inner])[part]
        project = dg(normed[...], weight, 1, 0)
        if part < 2:
            project = project * cosine[...] + half_turn(project) * sine[...]
        if part == 0:
            project = project * HEAD_DIM**-0.5
        held[:, part * inner : (part + 1) * inner] = project.astype(low)
    queries = held[:, :inner]
    keys = held[:, inner : 2 * inner]
    values = held[:, 2 * inner :]
    owner = lax.broadcasted_iota(jnp.int32, (rows, inner), 1) // HEAD_DIM
    zero = jnp.zeros((), low)
    total = None
    for head in range(inner // HEAD_DIM):
        mine = owner == head
        shares = shares_of(keys, jnp.where(mine, queries, zero), ok[...]).astype(low)
        term = dg(shares, jnp.where(mine, values, zero), 0, 0)
        total = term if total is None else total + term
    mixed[...] = total.astype(low)
    return dg(mixed[...], vo[:, inner:], 1, 1).astype(low).astype(f32)


def add_up(total, term, step):
    @pl.when(step == 0)
    def _():
        total[...] = term

    @pl.when(step > 0)
    def _():
        total[...] += term


def attend(line, weights, cosine, sine, ok, hidden, shift, scale, normed=None, before=None):
    rows, width = hidden.shape
    inner = weights.columns // 4
    total = struct((rows, width), f32)
    outs = [struct((2, rows, 3 * inner), low), struct((2, rows, inner), low), total, struct((rows, width), low)]
    plain = [cosine, sine, ok, hidden, shift, scale]
    plain += [] if before is None else [normed, before]
    arrays = weights.arrays

    def kernel(bits, *refs):
        tables, refs = refs[: len(arrays)], refs[len(arrays) :]
        (cosine, sine, ok, hidden, shift, scale, *more), refs = refs[: len(plain)], refs[len(plain) :]
        held, mixed, out, after, *scratch = refs
        step = pl.program_id(0)

        def modulate(values):
            normal, _ = normalise(values)
            after[...] = (normal * (1.0 + scale[...]) + shift[...]).astype(low)

        if not more:

            @pl.when(step == 0)
            def _():
                modulate(hidden[...])

        qk, vo = weights.load(bits, tables, scratch)
        normed = more[0] if more else after
        term = attend_piece(normed, qk, vo, cosine, sine, ok, held, mixed)
        add_up(out, term, step)
        if more:

            @pl.when(step == pl.num_programs(0) - 1)
            def _():
                total = hidden[...] + (more[1][...] + out[...])
                out[...] = total
                modulate(total)

    return line.run(
        kernel,
        outs,
        [*arrays, *plain],
        grid=(2,),
        in_specs=[*weights.specs(), *(whole(value) for value in plain)],
        out_specs=[each(outs[0]), each(outs[1]), whole(total), whole(total)],
        scratch=weights.scratch(),
        flops=2 * rows * (8 * width * inner + 16 * rows * inner),
        limit=20,
    )


def gelu_pair(values):
    root = math.sqrt(2.0 / math.pi)
    cube = 0.044715 * values * values
    slope = jnp.tanh(root * values * (1.0 + cube))
    gate = 0.5 * (1.0 + slope)
    back = gate + 0.5 * values * (1.0 - slope * slope) * root * (1.0 + 3.0 * cube)
    return values * gate, back


def feed(line, normed, outer, weights, halves, before=None):
    rows, width = normed.shape
    half = weights.columns // 2
    end = struct((rows, width), low)
    arrays = weights.arrays
    extra = [] if before is None else [before]

    def kernel(bits, *refs):
        tables, (normed, outer, *refs) = refs[: len(arrays)], refs[len(arrays) :]
        before, refs = refs[: len(extra)], refs[len(extra) :]
        outs, (fed, back, fed_total, back_total, *scratch) = refs[: len(halves.outs)], refs[len(halves.outs) :]
        step = pl.program_id(0)
        now = weights.load(bits, tables, scratch)
        up, down = now[:, :half], now[:, half:]
        value, slope = gelu_pair(dg(normed[...], up, 1, 0))
        gated = value.astype(low)
        lifted = (dg(outer[...], down, 1, 0) * slope).astype(low)
        grad = jnp.concatenate([dg(normed[...], lifted, 0, 0), dg(outer[...], gated, 0, 0)], axis=1)
        halves.store(bits, *(before or (None,)), outs, grad)
        add_up(fed_total, dg(gated, down, 1, 1), step)
        add_up(back_total, dg(lifted, up, 1, 1), step)

        @pl.when(step == pl.num_programs(0) - 1)
        def _():
            fed[...] = fed_total[...].astype(low)
            back[...] = back_total[...].astype(low)

    return line.run(
        kernel,
        [*halves.outs, end, end],
        [*arrays, normed, outer, *extra],
        grid=(2,),
        in_specs=[*weights.specs(), whole(normed), whole(outer), *(each(value) for value in extra)],
        out_specs=[*halves.specs(), whole(end), whole(end)],
        scratch=[pltpu.VMEM((rows, width), f32)] * 2 + weights.scratch(),
        flops=24 * rows * width * half,
        limit=22,
    )


def bend_kernel(middle, outer, keep, scale, *refs):
    *parts, result, middle_grad, middle_low, sums = refs
    count = len(parts) // 2
    fed = sum(part[...].astype(f32) for part in parts[:count])
    grad = sum(part[...].astype(f32) for part in parts[count:])
    result[...] = (keep[...] * (middle[...] + fed)).astype(low)
    normal, inverse = normalise(middle[...])
    total = outer[...].astype(f32) + norm_back(normal, inverse, grad, scale[...])
    middle_grad[...] = total
    middle_low[...] = total.astype(low)
    sums[0:1, :] = jnp.sum(grad, axis=0, keepdims=True)
    sums[1:2, :] = jnp.sum(grad * normal, axis=0, keepdims=True)


def bend(line, middle, outer, keep, scale, fed, back):
    shape = middle.shape
    outs = [struct(shape, low), struct(shape, f32), struct((2, shape[1]), f32), struct(shape, low)]

    def kernel(bits, *refs):
        *refs, sums, middle_low = refs
        bend_kernel(*refs, middle_low, sums)

    return line.run(kernel, outs, [middle, outer, keep, scale, *fed, *back], limit=14)


def back_piece(normed, middle_low, qk, vo, held, mixed, cosine, sine, ok, project):
    inner = qk.shape[1] // 2
    rows = normed.shape[0]
    queries = held[:, :inner]
    keys = held[:, inner : 2 * inner]
    values = held[:, 2 * inner :]
    above = dg(middle_low[...], vo[:, inner:], 1, 0).astype(low)
    owner = lax.broadcasted_iota(jnp.int32, (rows, inner), 1) // HEAD_DIM
    zero = jnp.zeros((), low)
    query_grad = key_grad = value_grad = jnp.zeros((rows, inner), f32)
    for head in range(inner // HEAD_DIM):
        mine = owner == head
        queries_here = jnp.where(mine, queries, zero)
        above_here = jnp.where(mine, above, zero)
        shares = shares_of(keys, queries_here, ok[...])
        share_grad = dg(values, above_here, 1, 1)
        inside = jnp.sum(share_grad * shares, axis=0, keepdims=True)
        score_grad = (shares * (share_grad - inside)).astype(low)
        value_grad += dg(shares.astype(low), above_here, 1, 0)
        key_grad += dg(score_grad, queries_here, 1, 0)
        query_grad += dg(score_grad, jnp.where(mine, keys, zero), 0, 0)
    query_grad = query_grad * HEAD_DIM**-0.5
    for place, grad in enumerate((query_grad, key_grad)):
        turned = grad * cosine[...] - half_turn(grad) * sine[...]
        project[:, place * inner : (place + 1) * inner] = turned.astype(low)
    project[:, 2 * inner :] = value_grad.astype(low)
    qk_grad = dg(normed[...], project[:, : 2 * inner], 0, 0)
    vo_grad = jnp.concatenate(
        [dg(normed[...], project[:, 2 * inner :], 0, 0), dg(middle_low[...], mixed[...], 0, 0)], axis=1
    )
    term = dg(project[:, : 2 * inner], qk, 1, 1)
    term += dg(project[:, 2 * inner :], vo[:, :inner], 1, 1)
    return qk_grad, vo_grad, term.astype(low).astype(f32)


def attend_back(line, normed, middle_low, weights, held, mixed, cosine, sine, ok, parts, before=None, last=()):
    rows, width = normed.shape
    inner = weights.columns // 4
    arrays = weights.arrays
    plain = [normed, middle_low, held, mixed, cosine, sine, ok, *last]
    extra = [] if before is None else [before]
    scratch = [pltpu.VMEM((rows, 3 * inner), low), *weights.scratch()]
    if last:
        ends = [struct((2, width), f32), struct((rows, width), low)]
        scratch = [pltpu.VMEM((rows, width), f32)] + scratch
    else:
        ends = [struct((rows, width), f32)]

    def kernel(bits, *refs):
        tables, refs = refs[: len(arrays)], refs[len(arrays) :]
        (*args, cosine, sine, ok), refs = refs[:7], refs[7:]
        more, refs = refs[: len(last)], refs[len(last) :]
        before, refs = refs[: len(extra)], refs[len(extra) :]
        outs = []
        for part in parts:
            outs.append(refs[: len(part.outs)])
            refs = refs[len(part.outs) :]
        marks, (total, project, *scratch) = (refs[:2], refs[2:]) if last else ((), refs)
        step = pl.program_id(0)
        normed, middle_low, held, mixed = args
        qk, vo = weights.load(bits, tables, scratch)
        *grads, term = back_piece(
            normed, middle_low, qk, vo, held, mixed, cosine, sine, ok, project
        )
        if len(parts) == 1:
            grads = [jnp.concatenate(grads, axis=1)]
        for part, out, grad in zip(parts, outs, grads):
            part.store(bits, *(before or (None,)), out, grad)
        add_up(total, term, step)
        if last:
            ahead, hidden, middle_grad, scale = more
            sums, hidden_low = marks

            @pl.when(step == pl.num_programs(0) - 1)
            def _():
                grad = ahead[...] + total[...]
                normal, inverse = normalise(hidden[...])
                hidden_low[...] = (
                    middle_grad[...] + norm_back(normal, inverse, grad, scale[...])
                ).astype(low)
                sums[0:1, :] = jnp.sum(grad, axis=0, keepdims=True)
                sums[1:2, :] = jnp.sum(grad * normal, axis=0, keepdims=True)

    outs = [value for part in parts for value in part.outs]
    return line.run(
        kernel,
        [*outs, *ends],
        [*arrays, *plain, *extra],
        grid=(2,),
        in_specs=[
            *weights.specs(),
            *(each(value) if value.ndim == 3 else whole(value) for value in plain),
            *(each(value) for value in extra),
        ],
        out_specs=[spec for part in parts for spec in part.specs()] + [whole(value) for value in ends],
        scratch=scratch,
        flops=2 * rows * (16 * width * inner + 40 * rows * inner),
        limit=24,
    )


def leave(line, blocks, hidden_low, place, parts):
    count = len(blocks)
    length, width = hidden_low.shape
    depth = 2 * width

    def kernel(bits, *refs):
        blocks, hidden_low, sent, kept, joined = refs[:count], *refs[count:]
        rows = blocks[0].shape[0]
        for index, block in enumerate(blocks):
            joined[index * rows : (index + 1) * rows, :] = block[:, :depth]
        mine = bits[place] == 1
        half = width // 2
        for here in (slice(0, half), slice(half, width)):
            total = dg(joined[...], hidden_low[:, here], 0, 0)
            total = total.reshape(sent.shape[0], 2, -1, half)
            sent[:, :, here] = jnp.where(mine, total[:, 0], total[:, 1]).astype(low)
            kept[:, :, here] = jnp.where(mine, total[:, 1], total[:, 0]).astype(low)

    return line.run(
        kernel,
        [struct((parts // 2, depth // parts, width), low)] * 2,
        [*blocks, hidden_low],
        scratch=[pltpu.VMEM((length, depth), low)],
        flops=2 * length * width * depth,
        limit=16,
    )


def inputs_back(line, blocks, results, pair, place):
    count = len(blocks)
    length, width = sum(block.shape[0] for block in blocks), blocks[0].shape[1]

    def kernel(bits, *refs):
        blocks, results, skips = refs[:count], refs[count : 2 * count], refs[2 * count : 2 * count + 2]
        frame_grad, skip_grad, result, hidden, held = refs[2 * count + 2 :]
        rows = blocks[0].shape[0]
        for index in range(count):
            start = pl.multiple_of((bits[1] ^ index) * rows, rows)
            hidden[pl.ds(start, rows), :] = blocks[index][...]
            result[pl.ds(start, rows), :] = results[index][...]
        skip = put_together(bits[place], *skips, held)
        frame_grad[...] = dg(hidden[...], skip[:width], 1, 1)
        skip_grad[...] = dg(hidden[...], skip[width:], 1, 1)

    return line.run(
        kernel,
        [struct((length, width), f32)] * 2 + [struct((length, width), low)],
        [*blocks, *results, *pair],
        scratch=[pltpu.VMEM((length, width), low), together(pair)],
        flops=4 * length * width * width,
        limit=14,
    )


def adam_update(master, first, second, grad, rate):
    first_new = beta_first * first + (1.0 - beta_first) * grad
    second_new = beta_second * second + (1.0 - beta_second) * grad * grad
    first_hat = first_new / (1.0 - beta_first**STEP)
    second_hat = second_new / (1.0 - beta_second**STEP)
    master_new = master - rate * (
        first_hat / (jnp.sqrt(second_hat) + adam_eps) + decay_rate * master
    )
    return (first_new, second_new, master_new, master_new.astype(low))


def added(pair):
    return pair[0][...].astype(f32) + pair[1][...].astype(f32)


def store_update(states, grad, rate, outs):
    for out, value in zip(outs, adam_update(*(state[...] for state in states), grad, rate)):
        out[...] = value


def update_outs(master):
    return [struct(master.shape, f32)] * 3 + [struct(master.shape, low)]


def update_feed(line, first, second, ups, downs):
    def kernel(bits, *refs):
        pairs, ups, downs = (refs[:2], refs[2:4]), refs[4:7], refs[7:10]
        up_outs, down_outs = refs[10:14], refs[14:18]
        totals = [added(pair) for pair in pairs]
        half = totals[0].shape[1] // 2
        store_update(ups, jnp.concatenate([total[:, :half] for total in totals], axis=1), rates[4], up_outs)
        store_update(
            downs, jnp.concatenate([total[:, half:].T for total in totals], axis=0), rates[5], down_outs
        )

    return line.run(kernel, update_outs(ups[0]) + update_outs(downs[0]), [*first, *second, *ups, *downs], limit=10)


def update_attention(line, qk, vo, inputs, outputs):
    def kernel(bits, *refs):
        qk, vo, inputs, outputs = refs[:2], refs[2:4], refs[4:7], refs[7:10]
        input_outs, output_outs = refs[10:14], refs[14:18]
        qk, vo = added(qk), added(vo)
        inner = qk.shape[1] // 2
        for place, grad in enumerate((qk[:, :inner], qk[:, inner:], vo[:, :inner])):
            store_update(
                [state.at[place] for state in inputs], grad, rates[2], [out.at[place] for out in input_outs]
            )
        store_update(outputs, vo[:, inner:].T, rates[3], output_outs)

    return line.run(kernel, update_outs(inputs[0]) + update_outs(outputs[0]), [*qk, *vo, *inputs, *outputs], limit=10)


def update_skip(line, pair, skips):
    def kernel(bits, *refs):
        store_update(refs[2:5], added(refs[:2]), rates[0], refs[5:9])

    return line.run(kernel, update_outs(skips[0]), [*pair, *skips], limit=8)


def orders():
    dp_bits, tensor_bits = bits_of("dp"), bits_of(TENSOR)
    far = [("dp", mask) for mask in dp_bits[:-2]]
    y, z = ("dp", dp_bits[-1]), ("dp", dp_bits[-2])
    x = (TENSOR, tensor_bits[0])
    return {
        "xzy": far + [x, z, y],
        "yzx": far + [y, z, x],
        "zxy": far + [z, x, y],
        "zyx": far + [z, y, x],
        "yxz": far + [y, x, z],
        "xyz": far + [x, y, z],
    }


def body(
    frames,
    skip_frames,
    time_embed,
    lengths,
    out_grad,
    skip_weight,
    adapt_weight,
    input_weight,
    output_weight,
    up_weight,
    down_weight,
    skip_first,
    adapt_first,
    input_first,
    output_first,
    up_first,
    down_first,
    skip_second,
    adapt_second,
    input_second,
    output_second,
    up_second,
    down_second,
):
    micro, _, rows, width = frames.shape
    parts = lax.axis_size(TENSOR)
    groups = lax.axis_size("dp")
    me = lax.axis_index(TENSOR)
    inner = input_weight.shape[2]
    heads = inner // HEAD_DIM
    highest = lax.Precision.HIGHEST
    order = orders()
    skip_order, skip_back_order = order["xyz"], order["yzx"]
    attention_orders, attention_back_orders = (order["xyz"], order["xzy"]), (order["xyz"], order["zxy"])
    feed_orders, feed_back_orders = (order["yzx"], order["zxy"]), (order["zxy"], order["xyz"])
    core = (TENSOR, bits_of(TENSOR)[-1])
    across = (TENSOR, bits_of(TENSOR)[0])
    dims = [across] + [("dp", mask) for mask in bits_of("dp")]
    all_dims = dims[1:] + [across, core]
    line = Line()

    adapt_low = adapt_weight.astype(low)
    time_values = time_embed[:, 0, :].astype(f32)
    time_low = jax.nn.silu(time_values).astype(low)

    def modulation():
        dp_bits = bits_of("dp")
        time_all = unflip(time_low, 0, TENSOR).reshape((1,) * len(dp_bits) + time_low.shape)
        for dim, mask in enumerate(dp_bits):
            time_all = line.tie(time_all)
            time_all = jnp.concatenate([time_all, swap(time_all, "dp", mask)], axis=dim)
            line.need(time_all)
            yield None
        time_rows = time_all.reshape(groups * micro, width)
        adapt_mine = jnp.dot(time_rows, adapt_low, preferred_element_type=f32).reshape(groups, micro, -1)
        for adapt_all in exchange_steps(line, adapt_mine, needed=True):
            yield time_rows, adapt_all

    modulate = modulation()

    row_index = jnp.concatenate(
        [(me ^ step) * rows + jnp.arange(rows, dtype=jnp.int32) for step in range(parts)]
    )
    length = pick(lengths, me, 0)[0]
    keep = (row_index < length).astype(f32)[:, None]
    half = HEAD_DIM // 2
    frequency = 10000.0 ** (-jnp.arange(half).astype(f32) / half)
    angles = row_index.astype(f32)[:, None] * frequency[None, :]
    cosine = jnp.tile(jnp.cos(angles), (1, 2 * heads))
    sine = jnp.tile(jnp.concatenate([-jnp.sin(angles), jnp.sin(angles)], axis=1), (1, heads))

    next(modulate)
    skip_shard, qk_shard, vo_shard, *feed_shards = pack(
        line, skip_weight, input_weight.transpose(1, 0, 2), output_weight, up_weight, down_weight
    )
    skip_walk = Gather(line, skip_shard, skip_order + [core], all_dims, ())
    attention_walks = [
        Gather(line, shard, each_order, dims, (across,))
        for shard, each_order in zip((qk_shard, vo_shard), attention_orders)
    ]
    next(modulate)
    blocks = list(cut(line, (frames, skip_frames, out_grad)))
    feed_walks = [
        Gather(line, shard, each_order, dims, (across,))
        for shard, each_order in zip(feed_shards, feed_orders)
    ]
    next(modulate)
    more = range(len(bits_of("dp")) - 3)
    for _ in more:
        go(line, skip_walk)
        go(line, *attention_walks)
        go(line, *feed_walks)
    line.need(cosine, sine, keep)
    go(line, skip_walk)
    next(modulate)
    go(line, *attention_walks)
    blocks[2] = swap(line.tie(blocks[2]), TENSOR, 2)
    next(modulate)
    go(line, skip_walk)
    next(modulate)
    go(line, *attention_walks)
    next(modulate)
    go(line, *feed_walks)
    for time_rows, adapt_all in modulate:
        pass
    blocks[3] = swap(line.tie(blocks[3]), TENSOR, 3)
    go(line, skip_walk)
    go(line, *feed_walks)
    adapt_vector = unflip(unflip(adapt_all, 0, "dp"), 1, TENSOR).reshape(1, -1)
    shift_one, scale_one, shift_two, scale_two = jnp.split(adapt_vector, 4, axis=1)
    line.need(blocks[2])
    go(line, *attention_walks)
    blocks[1] = swap(line.tie(blocks[1]), TENSOR, 1)
    line.need(blocks[3])
    go(line, skip_walk)
    skip_pair = skip_walk.pair()
    hidden, outer = enter(line, blocks, skip_pair, line.place[core], keep)
    go(line, *feed_walks)
    attention_own = Both(*(Pieces(line, walk, across) for walk in attention_walks))
    held_own, mixed_own, attended, normed_one = attend(
        line, attention_own, cosine, sine, keep, hidden, shift_one, scale_one
    )
    attention_other = attention_own.flip(core)
    held_other, mixed_other, middle, normed_two = attend(
        line, attention_other, cosine, sine, keep, hidden, shift_two, scale_two, normed=normed_one, before=attended
    )
    fed, back, feed_arrived, feed_scatters = [], [], [], []
    feed_own = [Pieces(line, walk, across) for walk in feed_walks]
    columns = feed_shards[0].shape[1]
    feed_other = [pieces.flip(core, tied=True) for pieces in feed_own]
    for pieces in feed_other:
        grad, *ends = feed(line, normed_two, outer, pieces, Halves(line, width, columns))
        feed_arrived.append(swap(grad, *core))
        fed.append(ends[0])
        back.append(ends[1])
    for pieces, arrived, each_order in zip(feed_own, feed_arrived, feed_back_orders):
        halves = Halves(line, width, columns, each_order[-1], dims, arrived)
        kept, sent, *ends = feed(line, normed_two, outer, pieces, halves, arrived)
        feed_scatters.append(Scatter(line, kept, sent, each_order[::-1], dims, (across,)))
        fed.append(ends[0])
        back.append(ends[1])
    feed_one, feed_two = feed_scatters
    result, middle_grad, sums_two, middle_low = bend(line, middle, outer, keep, scale_two, fed, back)
    results = from_owner([result[step * rows : (step + 1) * rows] for step in range(parts)])
    qk_other, vo_other, ahead = attend_back(
        line,
        normed_one,
        middle_low,
        attention_other,
        held_other,
        mixed_other,
        cosine,
        sine,
        keep,
        [Halves(line, width, 2 * inner)] * 2,
    )
    attention_arrived = [swap(grad, *core) for grad in (qk_other, vo_other)]
    line.need(*results[1:])
    qk_grad, vo_grad, sums_one, hidden_low = attend_back(
        line,
        normed_one,
        middle_low,
        attention_own,
        held_own,
        mixed_own,
        cosine,
        sine,
        keep,
        [Halves(line, width, 2 * inner)] * 2,
        last=(ahead, hidden, middle_grad, scale_one),
    )
    attention_scatters = [
        Scatter(line, grad, None, [core] + each_order[::-1], dims, (across,), arrived)
        for grad, arrived, each_order in zip((qk_grad, vo_grad), attention_arrived, attention_back_orders)
    ]
    go(line, feed_one, feed_two)
    skip_sent, skip_kept = leave(line, blocks, hidden_low, line.place[core], groups * parts)
    skip_scatter = Scatter(line, skip_kept, skip_sent, [core] + skip_back_order[::-1], all_dims, ())
    hidden_back = from_owner([hidden_low[step * rows : (step + 1) * rows] for step in range(parts)])

    def modulation_back():
        adapt_back = jnp.concatenate([sums_one.reshape(-1), sums_two.reshape(-1)]).reshape(
            groups, parts, -1
        )
        for adapt_rows in exchange_steps(line, unflip(unflip(adapt_back, 0, "dp"), 1, TENSOR)):
            yield None
        adapt_rows = adapt_rows.reshape(groups * micro, -1)
        adapt_sum = lax.dot_general(
            time_rows.astype(f32), adapt_rows, (((0,), (0,)), ((), ())), precision=highest
        )
        time_part = lax.dot_general(
            adapt_rows, adapt_low.astype(f32), (((1,), (1,)), ((), ())), precision=highest
        ).reshape(groups, micro, width)
        for mask in bits_of("dp"):
            time_part = line.tie(time_part)
            time_part = time_part[:mask] + swap(time_part[mask:], "dp", mask)
            yield None
        time_part = unflip(time_part[0], 0, TENSOR)
        for mask in bits_of(TENSOR):
            time_part = line.tie(time_part)
            time_part = time_part + swap(time_part, TENSOR, mask)
            yield None
        yield adapt_sum, time_part

    modulate_back = modulation_back()
    go(line, *attention_scatters)
    go(line, skip_scatter)
    next(modulate_back)
    go(line, feed_one, feed_two)
    next(modulate_back)
    go(line, *attention_scatters)
    next(modulate_back)
    go(line, skip_scatter)
    next(modulate_back)
    go(line, feed_one, feed_two)
    next(modulate_back)
    go(line, *attention_scatters)
    next(modulate_back)
    go(line, skip_scatter)
    next(modulate_back)
    go(line, *attention_scatters)
    go(line, skip_scatter)
    next(modulate_back)
    frame_grads, skip_grads, results = inputs_back(
        line, hidden_back, results, skip_pair, line.place[core]
    )
    frame_grads, skip_grads = frame_grads.reshape(frames.shape), skip_grads.reshape(frames.shape)
    for _ in more:
        go(line, feed_one, feed_two)
        go(line, *attention_scatters)
        go(line, skip_scatter)
    next(modulate_back)
    line.need(*(walk.terms[1] for walk in (*attention_scatters, skip_scatter)))
    feed_new = update_feed(
        line,
        feed_one.terms,
        feed_two.terms,
        (up_weight, up_first, up_second),
        (down_weight, down_first, down_second),
    )
    for ends in modulate_back:
        pass
    adapt_sum, time_part = ends
    sigmoid = jax.nn.sigmoid(time_values)
    time_grad = time_part * (sigmoid * (1.0 + time_values * (1.0 - sigmoid)))
    attention_new = update_attention(
        line,
        attention_scatters[0].terms,
        attention_scatters[1].terms,
        [state.transpose(1, 0, 2) for state in (input_weight, input_first, input_second)],
        (output_weight, output_first, output_second),
    )
    skip_new = update_skip(line, skip_scatter.terms, (skip_weight, skip_first, skip_second))
    adapt_new = adam_update(adapt_weight, adapt_first, adapt_second, adapt_sum, rates[1])
    return (
        results.reshape(frames.shape),
        frame_grads,
        skip_grads,
        time_grad[:, None, :],
        *skip_new,
        *adapt_new,
        *(value.transpose(1, 0, 2) for value in attention_new[:4]),
        *attention_new[4:],
        *feed_new,
    )


def solution(mesh):
    groups, parts = mesh.devices.shape
    split_mesh = Mesh(mesh.devices.reshape(groups, parts // 2, 2), ("dp", *TENSOR))
    return jax.shard_map(
        body,
        mesh=split_mesh,
        in_specs=(
            P(None, "dp", TENSOR, None),
            P(None, "dp", TENSOR, None),
            P(None, "dp", None),
            P(None, "dp"),
            P(None, "dp", TENSOR, None),
            P(("dp", *TENSOR), None),
            P(None, ("dp", *TENSOR)),
            P("dp", None, TENSOR),
            P(TENSOR, "dp"),
            P("dp", TENSOR),
            P(TENSOR, "dp"),
            P(("dp", *TENSOR), None),
            P(None, ("dp", *TENSOR)),
            P("dp", None, TENSOR),
            P(TENSOR, "dp"),
            P("dp", TENSOR),
            P(TENSOR, "dp"),
            P(("dp", *TENSOR), None),
            P(None, ("dp", *TENSOR)),
            P("dp", None, TENSOR),
            P(TENSOR, "dp"),
            P("dp", TENSOR),
            P(TENSOR, "dp"),
        ),
        out_specs=(
            P(None, "dp", TENSOR, None),
            P(None, "dp", TENSOR, None),
            P(None, "dp", TENSOR, None),
            P(None, "dp", None),
            P(("dp", *TENSOR), None),
            P(("dp", *TENSOR), None),
            P(("dp", *TENSOR), None),
            P(("dp", *TENSOR), None),
            P(None, ("dp", *TENSOR)),
            P(None, ("dp", *TENSOR)),
            P(None, ("dp", *TENSOR)),
            P(None, ("dp", *TENSOR)),
            P("dp", None, TENSOR),
            P("dp", None, TENSOR),
            P("dp", None, TENSOR),
            P("dp", None, TENSOR),
            P(TENSOR, "dp"),
            P(TENSOR, "dp"),
            P(TENSOR, "dp"),
            P(TENSOR, "dp"),
            P("dp", TENSOR),
            P("dp", TENSOR),
            P("dp", TENSOR),
            P("dp", TENSOR),
            P(TENSOR, "dp"),
            P(TENSOR, "dp"),
            P(TENSOR, "dp"),
            P(TENSOR, "dp"),
        ),
        check_vma=False,
    )
```
